32 devices in a mesh: seq: 4 (over z), fsdp: 8 (over y, x, core).
Axes of the slice: x: 2, y: 2, z: 4, core: 2. Of those that a mesh axis runs over, the one named last changes fastest.
Arguments:
- stream_in: bfloat16 [16, 1024, 1024], P('fsdp', 'seq'), may hold values from -6 to 6
- timestep: bfloat16 [16, 1024], P('fsdp'), may hold values from -3 to 3
- doc_start: int32 [16, 1024], P('fsdp'), may hold values from 0 to 1023, as said below
- query_weight: bfloat16 [1024, 1024], P('fsdp'), may hold values from -0.1875 to 0.1875
- key_weight: bfloat16 [1024, 1024], P('fsdp'), may hold values from -0.1875 to 0.1875
- value_weight: bfloat16 [1024, 1024], P('fsdp'), may hold values from -0.1875 to 0.1875
- output_weight: bfloat16 [1024, 1024], P('fsdp'), may hold values from -0.75 to 0.75
- query_bias: bfloat16 [1024], P('fsdp'), may hold values from -3 to 3
- value_bias: bfloat16 [1024], P('fsdp'), may hold values from -3 to 3
- output_bias: bfloat16 [1024], P('fsdp'), may hold values from -3 to 3
- first_gain: bfloat16 [1024], P('fsdp'), may hold values from 0.5 to 1.5
- first_shift: bfloat16 [1024], P('fsdp'), may hold values from -3 to 3
- inner_weight: bfloat16 [1024, 4096], P('fsdp'), may hold values from -0.1875 to 0.1875
- inner_bias: bfloat16 [4096], P('fsdp'), may hold values from -3 to 3
- outer_weight: bfloat16 [4096, 1024], P('fsdp'), may hold values from -0.09375 to 0.09375
- outer_bias: bfloat16 [1024], P('fsdp'), may hold values from -3 to 3
- second_gain: bfloat16 [1024], P('fsdp'), may hold values from 0.5 to 1.5
- second_shift: bfloat16 [1024], P('fsdp'), may hold values from -3 to 3
- cotangent: bfloat16 [16, 1024, 1024], P('fsdp', 'seq'), may hold values from -6 to 6
Outputs:
- layer_out: bfloat16 [16, 1024, 1024], P('fsdp', 'seq')
- input_grad: float32 [16, 1024, 1024], P('fsdp', 'seq')
- query_weight_grad: float32 [1024, 1024], P('fsdp')
- key_weight_grad: float32 [1024, 1024], P('fsdp')
- value_weight_grad: float32 [1024, 1024], P('fsdp')
- output_weight_grad: float32 [1024, 1024], P('fsdp')
- query_bias_grad: float32 [1024], P('fsdp')
- value_bias_grad: float32 [1024], P('fsdp')
- output_bias_grad: float32 [1024], P('fsdp')
- first_gain_grad: float32 [1024], P('fsdp')
- first_shift_grad: float32 [1024], P('fsdp')
- inner_weight_grad: float32 [1024, 4096], P('fsdp')
- inner_bias_grad: float32 [4096], P('fsdp')
- outer_weight_grad: float32 [4096, 1024], P('fsdp')
- outer_bias_grad: float32 [1024], P('fsdp')
- second_gain_grad: float32 [1024], P('fsdp')
- second_shift_grad: float32 [1024], P('fsdp')
The draws below stay inside these ranges and needn't reach their ends.
Inputs may be any that keep to these rules, and one draw needn't show every extreme that they name: `doc_start`: each entry is the position of the first token of its document in the stream; a document is a run of equal entries of 1 to 512 positions, each stream holds one document of exactly 512 positions, and the last position of each stream is a document of its own.
All inputs are finite; a program needn't handle non-finite values.
Results may differ from the reference program's by a relative error of at most 0.017.
Values may be sent and summed in bfloat16 or wider, within the bound.
No kernel may reach another device: no remote copies, remote signals or barrier semaphores. Data moves between devices by JAX's collectives and lax.ppermute only.
A program may use at most 192 MiB of HBM per device.

```python
import jax
import jax.numpy as jnp
from jax import lax

D = 1024
FF = 4096
HEADS = 16
HEAD_DIM = 64
LEN = 1024
DOC_MAX = 512
STREAMS = 16


def draw_doc_start(key, part):
    first_key, second_key = jax.random.split(key)
    long_begin = jax.random.randint(first_key, (STREAMS, 1), 0, LEN - DOC_MAX)
    position = jnp.arange(LEN, dtype=jnp.int32)[None, :]
    inside = (position > long_begin) & (position < long_begin + DOC_MAX)
    border = (position == long_begin) | (position == long_begin + DOC_MAX) | (position == LEN - 1)
    forced = position % (DOC_MAX // 2) == 0
    random_cut = jax.random.randint(second_key, (STREAMS, LEN), 0, 192) == 0
    cutting = border | jnp.logical_not(inside) & (forced | random_cut)
    marks = jnp.where(cutting, position, 0).astype(jnp.int32)
    return lax.cummax(marks, axis=1).astype(jnp.int32)


def shard_levels(stream_key, shape, cuts, least, high):
    def one(axis_at, blocks):
        heights = jax.random.uniform(jax.random.fold_in(jax.random.fold_in(stream_key, 6), axis_at), (blocks,), jnp.float32, least / len(cuts), high / len(cuts))
        return jnp.repeat(jnp.exp(heights), shape[axis_at] // blocks).reshape((-1,) + (1,) * (len(shape) - axis_at - 1))

    factor_of = one(*cuts[0])
    for cut in cuts[1:]:
        factor_of = factor_of * one(*cut)
    return factor_of


def scatter_about(rng, extent, width, reach, shards=(), kind=jnp.bfloat16):
    values = jax.random.normal(rng, extent, jnp.float32) * width
    if len(shards) > 0:
        values = shard_levels(rng, extent, shards, -0.22, 0.18) * values
    return jnp.clip(values, min=-reach, max=reach).astype(kind)


def setup_inputs(seed: int = 0) -> dict:
    arg_keys = jax.random.split(jax.random.key(seed), 20)
    return {
        "stream_in": scatter_about(arg_keys[0], (STREAMS, LEN, D), 1.0, 6.0, ((0, 8), (1, 4))),
        "timestep": scatter_about(arg_keys[1], (STREAMS, D), 0.5, 3.0, ((0, 8),)),
        "doc_start": draw_doc_start(jax.random.fold_in(arg_keys[19], 71), 0),
        "query_weight": scatter_about(arg_keys[3], (D, D), D ** -0.5, 0.1875, ((0, 8),)),
        "key_weight": scatter_about(arg_keys[4], (D, D), D ** -0.5, 0.1875, ((0, 8),)),
        "value_weight": scatter_about(arg_keys[5], (D, D), D ** -0.5, 0.1875, ((0, 8),)),
        "output_weight": scatter_about(arg_keys[6], (D, D), (D // 16) ** -0.5, 0.75, ((0, 8),)),
        "query_bias": scatter_about(arg_keys[7], (D,), 0.5, 3.0, ((0, 8),)),
        "value_bias": scatter_about(arg_keys[8], (D,), 0.5, 3.0, ((0, 8),)),
        "output_bias": scatter_about(arg_keys[9], (D,), 0.5, 3.0, ((0, 8),)),
        "first_gain": jnp.clip(1.0 + 0.1 * jax.random.normal(arg_keys[10], (D,), jnp.float32), 0.5, 1.5).astype(jnp.bfloat16),
        "first_shift": scatter_about(arg_keys[11], (D,), 0.5, 3.0, ((0, 8),)),
        "inner_weight": scatter_about(arg_keys[12], (D, FF), D ** -0.5, 0.1875, ((0, 8),)),
        "inner_bias": scatter_about(arg_keys[13], (FF,), 0.5, 3.0, ((0, 8),)),
        "outer_weight": scatter_about(arg_keys[14], (FF, D), FF ** -0.5, 0.09375, ((0, 8),)),
        "outer_bias": scatter_about(arg_keys[15], (D,), 0.5, 3.0, ((0, 8),)),
        "second_gain": jnp.clip(1.0 + 0.1 * jax.random.normal(arg_keys[16], (D,), jnp.float32), 0.5, 1.5).astype(jnp.bfloat16),
        "second_shift": scatter_about(arg_keys[17], (D,), 0.5, 3.0, ((0, 8),)),
        "cotangent": scatter_about(arg_keys[18], (STREAMS, LEN, D), 1.0, 6.0, ((0, 8), (1, 4))),
    }


@jax.custom_vjp
def low(v):
    return lax.optimization_barrier(v.astype(jnp.bfloat16)).astype(jnp.float32)

@jax.custom_vjp
def low_back(v):
    return v

def low_keep(v):
    return (low(v), None)

def low_pass(kept, grad):
    return (grad,)

def back_keep(v):
    return (v, None)

def back_low(kept, grad):
    return (low(grad),)
low.defvjp(low_keep, low_pass)
low_back.defvjp(back_keep, back_low)

def matmul(left, right):
    return jnp.dot(left, right, precision=lax.Precision.HIGHEST)

def layer_norm(rows, gain, shift):
    centred = rows - lax.optimization_barrier(jnp.mean(rows, axis=-1, keepdims=True))
    spread = lax.optimization_barrier(jnp.mean(centred * centred, axis=-1, keepdims=True))
    return centred * lax.rsqrt(spread + 1e-05) * gain + shift

def attend(queries, key_rows, values, starts):
    length = queries.shape[0]
    block = min(512, length)
    count = length // block
    query_blocks = queries.reshape(count, block, HEADS, HEAD_DIM)
    start_blocks = starts.reshape(count, block)

    def one_block(pair):
        query_block, start_block = pair
        scores = jnp.einsum('qhd,khd->hqk', query_block, key_rows, precision=lax.Precision.HIGHEST)
        scores = low_back(scores)
        same = start_block[:, None] == starts[None, :]
        scores = jnp.where(same[None], scores, -1e+30)
        peak = lax.optimization_barrier(jnp.max(scores, axis=-1, keepdims=True))
        weights = jnp.exp(scores - peak)
        probs = weights / lax.optimization_barrier(jnp.sum(weights, axis=-1, keepdims=True))
        return jnp.einsum('hqk,khd->qhd', low(probs), values, precision=lax.Precision.HIGHEST)
    mixed = lax.map(jax.checkpoint(one_block), (query_blocks, start_blocks))
    return mixed.reshape(length, HEADS * HEAD_DIM)

def reference(stream_in, timestep, doc_start, query_weight, key_weight, value_weight, output_weight, query_bias, value_bias, output_bias, first_gain, first_shift, inner_weight, inner_bias, outer_weight, outer_bias, second_gain, second_shift, cotangent):
    floats = tuple((item.astype(jnp.float32) for item in (stream_in, timestep, query_weight, key_weight, value_weight, output_weight, query_bias, value_bias, output_bias, first_gain, first_shift, inner_weight, inner_bias, outer_weight, outer_bias, second_gain, second_shift)))

    def forward(stream, embed, wquery, wkey, wvalue, woutput, bquery, bvalue, boutput, gain_one, shift_one, winner, binner, wouter, bouter, gain_two, shift_two):

        def one_stream(triple):
            rows, embed_row, starts = triple
            hidden = rows + embed_row[None, :]
            hidden_low = low(hidden)
            queries = low_back(low((matmul(hidden_low, wquery) + bquery) * 0.125))
            key_rows = low_back(low(matmul(hidden_low, wkey)))
            values = low_back(low(matmul(hidden_low, wvalue) + bvalue))
            length = rows.shape[0]
            shaped = (length, HEADS, HEAD_DIM)
            mixed = low_back(low(attend(queries.reshape(shaped), key_rows.reshape(shaped), values.reshape(shaped), starts)))
            attended = low_back(matmul(mixed, woutput) + boutput)
            first_out = layer_norm(hidden + attended, gain_one, shift_one)
            inner = low_back(matmul(low(first_out), winner) + binner)
            active = low(jax.nn.gelu(inner, approximate=False))
            outer = low_back(matmul(active, wouter) + bouter)
            return layer_norm(first_out + outer, gain_two, shift_two)
        return lax.map(jax.checkpoint(one_stream), (stream, embed, doc_start))
    result, pullback = jax.vjp(forward, *floats)
    grads = pullback(cotangent.astype(jnp.float32))
    return (result.astype(jnp.bfloat16), grads[0], grads[2], grads[3], grads[4], grads[5], grads[6], grads[7], grads[8], grads[9], grads[10], grads[11], grads[12], grads[13], grads[14], grads[15], grads[16])
```

```python
from functools import partial

import jax
import jax.numpy as jnp
from jax import lax
from jax.experimental import pallas as pl
from jax.experimental.pallas import tpu as pltpu
from jax.sharding import PartitionSpec as P

HEAD_DIM = 64
PAIR = 2 * HEAD_DIM
BLOCK = 256
F32 = jnp.float32
BF16 = jnp.bfloat16

PHI_POLY = (
    0.11962928975633808,
    0.12075411058236112,
    0.09991242675653945,
    0.12856547821204567,
    -0.053691543682108024,
    0.20636272322745108,
    -0.15720876784307727,
    0.03567620985200702,
)


def normal_cdf_pdf(z):
    u = jnp.abs(z)
    bell = jnp.exp(-0.5 * u * u)
    t = 1.0 / (1.0 + 0.3 * u)
    poly = jnp.full_like(t, PHI_POLY[-1])
    for coef in PHI_POLY[-2::-1]:
        poly = poly * t + coef
    tail = bell * (t * poly)
    return jnp.where(z < 0, tail, 1.0 - tail), bell * 0.3989422804014327


def layer_norm(rows, gain, shift):
    centred = rows - jnp.mean(rows, axis=-1, keepdims=True)
    factor = lax.rsqrt(jnp.mean(centred * centred, axis=-1, keepdims=True) + 1e-05)
    normed = centred * factor
    return (normed * gain + shift, normed, factor)


def norm_back(upstream, normed, factor, gain):
    scaled = upstream * gain
    return factor * (
        scaled
        - jnp.mean(scaled, axis=-1, keepdims=True)
        - normed * jnp.mean(scaled * normed, axis=-1, keepdims=True)
    )


def matmul(left, right):
    return jnp.dot(left, right, preferred_element_type=F32)


def contract_rows(left, right):
    return lax.dot_general(left, right, (((0,), (0,)), ((), ())), preferred_element_type=F32)


def contract_cols(left, right):
    return lax.dot_general(left, right, (((1,), (1,)), ((), ())), preferred_element_type=F32)


def column_sum(rows):
    return jnp.sum(rows.astype(F32), axis=0)


def half_rows(block, head):
    zero = jnp.zeros((HEAD_DIM, block.shape[1]), block.dtype)
    part = block[head * HEAD_DIM : (head + 1) * HEAD_DIM]
    return jnp.concatenate([part, zero] if head == 0 else [zero, part], axis=0)


def forward_kernel(bounds, qkv_ref, row_ref, col_ref, mixed_ref, logsum_ref, vt_ref):
    length = qkv_ref.shape[0]
    q_t = qkv_ref[:, :PAIR].T
    vt_ref[...] = qkv_ref[:, 2 * PAIR :].T
    for i in range(length // BLOCK):
        at = slice(i * BLOCK, (i + 1) * BLOCK)
        row = row_ref[:, at]
        halves = [half_rows(q_t[:, at], head) for head in range(2)]

        def step(j, carry):
            span = pl.ds(pl.multiple_of(j * BLOCK, BLOCK), BLOCK)
            keys = qkv_ref[span, PAIR : 2 * PAIR]
            same = col_ref[span, :] == row
            new = []
            for head in range(2):
                peak, total, mix = carry[head]
                scores = jnp.where(same, matmul(keys, halves[head]), -1e30)
                top = jnp.maximum(peak, jnp.max(scores, axis=0, keepdims=True))
                weights = jnp.exp(scores - top)
                decay = jnp.exp(peak - top)
                total = total * decay + jnp.sum(weights, axis=0, keepdims=True)
                v_t = vt_ref[head * HEAD_DIM : (head + 1) * HEAD_DIM, span]
                mix = mix * decay + matmul(v_t, weights.astype(BF16))
                new.append((top, total, mix))
            return tuple(new)

        first = (
            jnp.full((1, BLOCK), -1e30, F32),
            jnp.zeros((1, BLOCK), F32),
            jnp.zeros((HEAD_DIM, BLOCK), F32),
        )
        done = lax.fori_loop(bounds[i, 0], bounds[i, 1], step, (first, first))
        mixed_ref[at, :] = jnp.concatenate([d[2] / d[1] for d in done], axis=0).T.astype(BF16)
        for head in range(2):
            logsum_ref[0, head : head + 1, at] = done[head][0] + jnp.log(done[head][1])


def backward_kernel(
    bounds, qkv_ref, row_ref, col_ref, mixed_ref, logsum_ref, grad_ref, out_ref, kt_ref, dk_ref, dv_ref
):
    length = qkv_ref.shape[0]
    q_all = qkv_ref[:, :PAIR]
    g_all = grad_ref[...]
    q_t = q_all.T
    g_t = g_all.T
    kt_ref[...] = qkv_ref[:, PAIR : 2 * PAIR].T
    dk_ref[...] = jnp.zeros_like(dk_ref)
    dv_ref[...] = jnp.zeros_like(dv_ref)
    product_t = (g_all.astype(F32) * mixed_ref[...].astype(F32)).T
    delta = [
        jnp.sum(product_t[head * HEAD_DIM : (head + 1) * HEAD_DIM], axis=0, keepdims=True) for head in range(2)
    ]
    lane = lax.broadcasted_iota(jnp.int32, (BLOCK, PAIR), 1)
    for i in range(length // BLOCK):
        at = slice(i * BLOCK, (i + 1) * BLOCK)
        row = row_ref[:, at]
        q_halves = [half_rows(q_t[:, at], head) for head in range(2)]
        g_halves = [half_rows(g_t[:, at], head) for head in range(2)]
        low, high = lane < HEAD_DIM, lane >= HEAD_DIM
        zero = jnp.zeros((BLOCK, PAIR), BF16)
        q_split = jnp.concatenate([jnp.where(low, q_all[at], zero), jnp.where(high, q_all[at], zero)], axis=0)
        g_split = jnp.concatenate([jnp.where(low, g_all[at], zero), jnp.where(high, g_all[at], zero)], axis=0)
        logsum = [logsum_ref[0, head : head + 1, at] for head in range(2)]

        def step(j, carry):
            span = pl.ds(pl.multiple_of(j * BLOCK, BLOCK), BLOCK)
            keys = qkv_ref[span, PAIR : 2 * PAIR]
            values = qkv_ref[span, 2 * PAIR :]
            same = col_ref[span, :] == row
            probs_low, grad_low, new = [], [], []
            for head in range(2):
                scores = jnp.where(same, matmul(keys, q_halves[head]), -1e30)
                probs = jnp.exp(scores - logsum[head])
                grad_probs = matmul(values, g_halves[head])
                grad_scores = (probs * (grad_probs - delta[head][:, at])).astype(BF16)
                probs_low.append(probs.astype(BF16))
                grad_low.append(grad_scores)
                k_t = kt_ref[head * HEAD_DIM : (head + 1) * HEAD_DIM, span]
                new.append(carry[head] + matmul(k_t, grad_scores))
            dv_ref[span, :] += matmul(jnp.concatenate(probs_low, axis=1), g_split)
            dk_ref[span, :] += matmul(jnp.concatenate(grad_low, axis=1), q_split)
            return tuple(new)

        empty = jnp.zeros((HEAD_DIM, BLOCK), F32)
        done = lax.fori_loop(bounds[i, 0], bounds[i, 1], step, (empty, empty))
        grad_q = jnp.concatenate(done, axis=0).T
        out_ref[at, :PAIR] = (grad_q * 0.125).astype(BF16)
    out_ref[:, PAIR : 2 * PAIR] = dk_ref[...].astype(BF16)
    out_ref[:, 2 * PAIR :] = dv_ref[...].astype(BF16)


def block_bounds(starts):
    blocks = starts.reshape(-1, BLOCK)
    least, most = blocks[:, 0], blocks[:, -1]
    low = jnp.sum(most[None, :] < least[:, None], axis=1)
    high = jnp.sum(least[None, :] <= most[:, None], axis=1)
    return jnp.stack([low, high], axis=1).astype(jnp.int32)


def attention_forward(qkv, starts):
    length, packed = qkv.shape
    pairs = packed // (3 * PAIR)
    return pl.pallas_call(
        forward_kernel,
        grid_spec=pltpu.PrefetchScalarGridSpec(
            num_scalar_prefetch=1,
            grid=(pairs,),
            in_specs=[
                pl.BlockSpec((length, 3 * PAIR), lambda p, b: (0, p)),
                pl.BlockSpec((1, length), lambda p, b: (0, 0)),
                pl.BlockSpec((length, 1), lambda p, b: (0, 0)),
            ],
            out_specs=[
                pl.BlockSpec((length, PAIR), lambda p, b: (0, p)),
                pl.BlockSpec((1, 2, length), lambda p, b: (p, 0, 0)),
            ],
            scratch_shapes=[pltpu.VMEM((PAIR, length), BF16)],
        ),
        out_shape=[
            jax.ShapeDtypeStruct((length, pairs * PAIR), BF16),
            jax.ShapeDtypeStruct((pairs, 2, length), F32),
        ],
        compiler_params=pltpu.CompilerParams(vmem_limit_bytes=40 * 1024 * 1024),
        cost_estimate=pl.CostEstimate(
            flops=pairs * 2 * length * length * HEAD_DIM * 4,
            bytes_accessed=length * packed * 3,
            transcendentals=pairs * 2 * length * length,
        ),
        name="attend",
    )(block_bounds(starts), qkv, starts[None, :], starts[:, None])


def attention_backward(qkv, starts, mixed, logsum, grad):
    length, packed = qkv.shape
    pairs = packed // (3 * PAIR)
    return pl.pallas_call(
        backward_kernel,
        grid_spec=pltpu.PrefetchScalarGridSpec(
            num_scalar_prefetch=1,
            grid=(pairs,),
            in_specs=[
                pl.BlockSpec((length, 3 * PAIR), lambda p, b: (0, p)),
                pl.BlockSpec((1, length), lambda p, b: (0, 0)),
                pl.BlockSpec((length, 1), lambda p, b: (0, 0)),
                pl.BlockSpec((length, PAIR), lambda p, b: (0, p)),
                pl.BlockSpec((1, 2, length), lambda p, b: (p, 0, 0)),
                pl.BlockSpec((length, PAIR), lambda p, b: (0, p)),
            ],
            out_specs=pl.BlockSpec((length, 3 * PAIR), lambda p, b: (0, p)),
            scratch_shapes=[
                pltpu.VMEM((PAIR, length), BF16),
                pltpu.VMEM((length, PAIR), F32),
                pltpu.VMEM((length, PAIR), F32),
            ],
        ),
        out_shape=jax.ShapeDtypeStruct((length, packed), BF16),
        compiler_params=pltpu.CompilerParams(vmem_limit_bytes=40 * 1024 * 1024),
        cost_estimate=pl.CostEstimate(
            flops=pairs * 2 * length * length * HEAD_DIM * 10,
            bytes_accessed=length * packed * 6,
            transcendentals=pairs * 2 * length * length,
        ),
        name="attend_back",
    )(block_bounds(starts), qkv, starts[None, :], starts[:, None], mixed, logsum, grad)


def flip(x, axis, size, bit):
    return lax.ppermute(x, axis, [(i, i ^ bit) for i in range(size)])


class Cube:
    def __init__(self):
        self.me = lax.axis_index("fsdp")
        self.n = 8

    def swap(self, x, bit):
        return flip(x, "fsdp", 8, bit)

    def gather(self, piece, route):
        first, second = (2, 4) if route == 0 else (4, 2)
        near = self.swap(piece, first)
        side = self.swap(piece, second)
        far = self.swap(near, second)
        out = []
        for mask, block in ((0, piece), (first, near), (second, side), (6, far)):
            out.append((self.me ^ mask, block))
            out.append((self.me ^ mask ^ 1, self.swap(block, 1)))
        return out

    def scatter(self, left, right, route):
        block = left.shape[1] // 8
        width = right.shape[1]

        def part(masks):
            picked = [lax.dynamic_slice_in_dim(left, (self.me ^ m) * block, block, 1) for m in masks]
            return contract_rows(jnp.concatenate(picked, axis=1), right).astype(BF16)

        first, second = (2, 4) if route == 0 else (4, 2)
        order = (0, second, first, 6)
        send = part([m ^ 1 for m in order]).reshape(4, block, width)
        keep = part(order).reshape(4, block, width)
        got = self.swap(send, 1)
        there = (keep[2:].astype(F32) + got[2:].astype(F32)).astype(BF16)
        got_two = self.swap(there, first)
        here = keep[:2].astype(F32) + got[:2].astype(F32) + got_two.astype(F32)
        last = self.swap(here[1].astype(BF16), second)
        return here[0] + last.astype(F32)

    def scatter_small(self, rows):
        cube = rows.reshape(2, 2, 2, -1)
        for axis, bit in ((0, 4), (1, 2), (2, 1)):
            cube = jnp.where(self.me & bit != 0, jnp.flip(cube, axis), cube)
        cube = cube[:, :, 0] + self.swap(cube[:, :, 1], 1)
        cube = cube[:, 0] + self.swap(cube[:, 1], 2)
        return cube[0] + self.swap(cube[1], 4)


class Line:
    def __init__(self, n):
        self.n = n

    def gather(self, piece, route):
        whole = lax.all_gather(piece, "fsdp", axis=0, tiled=False)
        return [(i, whole[i]) for i in range(self.n)]

    def scatter(self, left, right, route):
        part = contract_rows(left, right).astype(BF16)
        return lax.psum_scatter(part, "fsdp", scatter_dimension=0, tiled=True).astype(F32)

    def scatter_small(self, rows):
        return lax.psum_scatter(rows, "fsdp", scatter_dimension=0, tiled=False)


def assemble(pieces, rows):
    cols = pieces[0][1].shape[1]
    whole = jnp.zeros((rows * len(pieces), cols), pieces[0][1].dtype)
    for owner, block in pieces:
        whole = lax.dynamic_update_slice(whole, block[:rows], (owner * rows, 0))
    return whole


def pair_pack(parts):
    rows = parts[0].shape[0]
    return jnp.stack([p.reshape(rows, -1, PAIR) for p in parts], axis=2).reshape(rows, -1)


def pair_unpack(packed):
    rows = packed.shape[0]
    cut = packed.reshape(rows, -1, 3, PAIR)
    return [cut[:, :, i].reshape(rows, -1) for i in range(3)]


def body(
    fsdp,
    stream_in,
    timestep,
    doc_start,
    query_weight,
    key_weight,
    value_weight,
    output_weight,
    query_bias,
    value_bias,
    output_bias,
    first_gain,
    first_shift,
    inner_weight,
    inner_bias,
    outer_weight,
    outer_bias,
    second_gain,
    second_shift,
    cotangent,
):
    links = Cube() if fsdp == 8 else Line(fsdp)
    streams, tok, width = stream_in.shape
    own_rows = query_weight.shape[0]
    half = width // 2
    ff = inner_weight.shape[1]
    length = 4 * tok
    z = lax.axis_index("seq")
    h, s = z % 2, z // 2

    def flip_h(x):
        return flip(x, "seq", 4, 1)

    def flip_s(x):
        return flip(x, "seq", 4, 2)

    def in_order(mine, other):
        return jnp.where(s == 0, jnp.concatenate([mine, other]), jnp.concatenate([other, mine]))

    def pick(x, index, axis=0):
        return lax.dynamic_index_in_dim(x, index, axis, keepdims=False)

    own = pick(stream_in, s)
    distant = flip_s(pick(stream_in, 1 - s))
    beside = flip_h(own)
    corner = flip_h(distant)
    moved = flip_s(pick(cotangent, 1 - s))
    upstream = in_order(pick(cotangent, s), moved).astype(F32)

    head_cols = [lax.dynamic_slice_in_dim(w, h * half, half, 1) for w in (query_weight, key_weight, value_weight)]
    small = jnp.concatenate(
        [
            query_bias,
            value_bias,
            output_bias,
            first_gain,
            first_shift,
            outer_bias,
            second_gain,
            second_shift,
            inner_bias,
        ]
    )
    packed = pair_pack(head_cols)
    if fsdp == 8:
        packed = jnp.concatenate([packed, jnp.broadcast_to(small[None, :], (16, small.shape[0]))])
        qkv_pieces = links.gather(packed, 0)
        small_rows = jnp.zeros((fsdp, small.shape[0]), BF16)
        for owner, block in qkv_pieces:
            small_rows = lax.dynamic_update_slice(small_rows, block[own_rows : own_rows + 1], (owner, 0))
    else:
        qkv_pieces = links.gather(packed, 0)
        small_rows = lax.all_gather(small, "fsdp", axis=0, tiled=False)
    full_qkv = assemble(qkv_pieces, own_rows)
    full_output = assemble(links.gather(output_weight, 1), own_rows)
    full_inner = assemble(links.gather(inner_weight, 0), own_rows)
    full_outer = assemble(links.gather(outer_weight, 1), outer_weight.shape[0])
    small_rows = small_rows.astype(F32)
    qbias, vbias, obias, gain_one, shift_one, obias_two, gain_two, shift_two = [
        small_rows[:, i * own_rows : (i + 1) * own_rows].reshape(-1) for i in range(8)
    ]
    ibias = small_rows[:, 8 * own_rows :].reshape(-1)

    ts = pick(timestep, s).astype(F32)
    stream = jnp.zeros((length, width), BF16)
    for mask, block in ((0, own), (1, beside), (2, distant), (3, corner)):
        stream = lax.dynamic_update_slice(stream, block, ((z ^ mask) * tok, 0))
    stream_low = (stream.astype(F32) + ts).astype(BF16)
    hidden = in_order(own, distant).astype(F32) + ts
    starts = pick(doc_start, s)

    qb = lax.dynamic_slice_in_dim(qbias, h * half, half, 0)
    vb = lax.dynamic_slice_in_dim(vbias, h * half, half, 0)
    bias_row = pair_pack([qb[None], jnp.zeros_like(qb)[None], vb[None]])
    scale_row = pair_pack([jnp.full((1, half), 0.125, F32), jnp.ones((1, half), F32), jnp.ones((1, half), F32)])
    qkv = ((matmul(stream_low, full_qkv) + bias_row) * scale_row).astype(BF16)
    mixed_heads, logsum = attention_forward(qkv, starts)

    def rows_of(x, parity):
        cut = x.reshape(2, 2, tok, x.shape[1])
        return pick(cut, parity, 1).reshape(2 * tok, x.shape[1])

    def swap_heads(mine, other):
        return jnp.where(h == 0, jnp.concatenate([mine, other], axis=1), jnp.concatenate([other, mine], axis=1))

    mixed = swap_heads(rows_of(mixed_heads, h), flip_h(rows_of(mixed_heads, 1 - h)))
    attended = matmul(mixed, full_output) + obias
    first_out, first_normed, first_factor = layer_norm(hidden + attended, gain_one, shift_one)
    first_low = first_out.astype(BF16)

    inner = matmul(first_low, full_inner) + ibias
    cdf, pdf = normal_cdf_pdf(inner)
    active = (inner * cdf).astype(BF16)
    slope = (cdf + inner * pdf).astype(BF16)
    second_in = first_out + matmul(active, full_outer) + obias_two
    result, second_normed, second_factor = layer_norm(second_in, gain_two, shift_two)
    result = result.astype(BF16)

    grad_second_gain = jnp.sum(upstream * second_normed, axis=0)
    grad_second_shift = jnp.sum(upstream, axis=0)
    grad_second_in = norm_back(upstream, second_normed, second_factor, gain_two)
    grad_outer = grad_second_in.astype(BF16)
    grad_outer_bias = column_sum(grad_outer)
    outer_share = links.scatter(active, grad_outer, 0)
    grad_active = contract_cols(grad_outer, full_outer)
    grad_inner = (grad_active * slope.astype(F32)).astype(BF16)
    grad_inner_bias = column_sum(grad_inner)
    inner_share = links.scatter(first_low, grad_inner, 1)
    grad_first_out = grad_second_in + contract_cols(grad_inner, full_inner)
    grad_first_gain = jnp.sum(grad_first_out * first_normed, axis=0)
    grad_first_shift = jnp.sum(grad_first_out, axis=0)
    grad_first_in = norm_back(grad_first_out, first_normed, first_factor, gain_one)
    grad_attended = grad_first_in.astype(BF16)
    grad_output_bias = column_sum(grad_attended)
    grad_mixed = contract_cols(grad_attended, full_output).astype(BF16)
    grad_cols = grad_mixed.reshape(2 * tok, 2, half)
    received = flip_h(pick(grad_cols, 1 - h, 1)).reshape(2, 1, tok, half)
    kept = pick(grad_cols, h, 1).reshape(2, 1, tok, half)
    grad_heads = jnp.where(
        h == 0, jnp.concatenate([kept, received], axis=1), jnp.concatenate([received, kept], axis=1)
    ).reshape(length, half)
    output_share = links.scatter(mixed, grad_attended, 0)
    grad_qkv = attention_backward(qkv, starts, mixed_heads, logsum, grad_heads)
    partial_hidden = contract_cols(grad_qkv, full_qkv)
    away = flip_h(rows_of(partial_hidden, 1 - h).astype(BF16)).astype(F32)
    grad_hidden = (grad_first_in + rows_of(partial_hidden, h) + away).reshape(2, tok, width)
    qkv_share = links.scatter(stream_low, grad_qkv, 0)
    grad_q_cols, _, grad_v_cols = pair_unpack(column_sum(grad_qkv)[None])

    grad_own = pick(grad_hidden, s)
    grad_away = flip_s(pick(grad_hidden, 1 - s).astype(BF16)).astype(F32)
    input_grad = jnp.where(s == 0, jnp.stack([grad_own, grad_away]), jnp.stack([grad_away, grad_own]))
    result = result.reshape(2, tok, width)
    result_own = pick(result, s)
    result_away = flip_s(pick(result, 1 - s))
    layer_out = jnp.where(s == 0, jnp.stack([result_own, result_away]), jnp.stack([result_away, result_own]))

    def seq_sum(share):
        rows = share.shape[0]
        cut = share.reshape(2, rows // 2, -1)
        mine = pick(cut, h) + flip_h(pick(cut, 1 - h).astype(BF16)).astype(F32)
        cut = mine.reshape(2, rows // 4, -1)
        mine = (pick(cut, s) + flip_s(pick(cut, 1 - s).astype(BF16)).astype(F32)).astype(BF16)
        by_s = flip_s(mine)
        by_h = flip_h(mine)
        by_both = flip_h(by_s)
        out = jnp.zeros(share.shape, F32)
        for hh, ss, block in ((h, s, mine), (h, 1 - s, by_s), (1 - h, s, by_h), (1 - h, 1 - s, by_both)):
            out = lax.dynamic_update_slice(out, block.astype(F32), ((2 * hh + ss) * (rows // 4), 0))
        return out

    def seq_sum_small(share):
        share = share + flip_h(share)
        return share + flip_s(share)

    outer_grad = seq_sum(outer_share)
    inner_grad = seq_sum(inner_share)
    output_grad = seq_sum(output_share)
    qkv_half = (qkv_share + flip_s(qkv_share.astype(BF16)).astype(F32)).astype(BF16)
    qkv_other = flip_h(qkv_half)
    qkv_grads = [
        swap_heads(mine, other).astype(F32) for mine, other in zip(pair_unpack(qkv_half), pair_unpack(qkv_other))
    ]
    early = jnp.concatenate(
        [
            v.reshape(fsdp, -1)
            for v in (
                grad_output_bias,
                grad_first_gain,
                grad_first_shift,
                grad_outer_bias,
                grad_second_gain,
                grad_second_shift,
                grad_inner_bias,
            )
        ],
        axis=1,
    )
    early = seq_sum_small(links.scatter_small(early))
    zero_half = jnp.zeros((half,), F32)

    def widen(v):
        v = v.reshape(-1)
        return jnp.where(h == 0, jnp.concatenate([v, zero_half]), jnp.concatenate([zero_half, v])).reshape(fsdp, -1)

    late = jnp.concatenate([widen(grad_q_cols), widen(grad_v_cols)], axis=1)
    late = seq_sum_small(links.scatter_small(late))
    cut = [early[i * own_rows : (i + 1) * own_rows] for i in range(6)]
    return (
        layer_out,
        input_grad,
        qkv_grads[0],
        qkv_grads[1],
        qkv_grads[2],
        output_grad,
        late[:own_rows],
        late[own_rows:],
        cut[0],
        cut[1],
        cut[2],
        inner_grad,
        early[6 * own_rows :],
        outer_grad,
        cut[3],
        cut[4],
        cut[5],
    )


def solution(mesh):
    rows = P("fsdp", "seq", None)
    mat = P("fsdp", None)
    vec = P("fsdp")
    in_specs = (
        (rows, mat, mat) + (mat,) * 4 + (vec,) * 5 + (mat, vec, mat, vec, vec, vec) + (rows,)
    )
    out_specs = (rows, rows) + (mat,) * 4 + (vec,) * 5 + (mat, vec, mat, vec, vec, vec)
    return jax.shard_map(
        partial(body, mesh.shape["fsdp"]), mesh=mesh, in_specs=in_specs, out_specs=out_specs, check_vma=False
    )
```

```python
from functools import partial

import jax
import jax.numpy as jnp
from jax import lax
from jax.experimental import pallas as pl
from jax.experimental.pallas import tpu as pltpu
from jax.sharding import PartitionSpec as P

HEAD_DIM = 64
PAIR = 2 * HEAD_DIM
BLOCK = 256
F32 = jnp.float32
BF16 = jnp.bfloat16

PHI_POLY = (
    0.11962928975633808,
    0.12075411058236112,
    0.09991242675653945,
    0.12856547821204567,
    -0.053691543682108024,
    0.20636272322745108,
    -0.15720876784307727,
    0.03567620985200702,
)


def normal_cdf_pdf(z):
    u = jnp.abs(z)
    bell = jnp.exp(-0.5 * u * u)
    t = 1.0 / (1.0 + 0.3 * u)
    poly = jnp.full_like(t, PHI_POLY[-1])
    for coef in PHI_POLY[-2::-1]:
        poly = poly * t + coef
    tail = bell * (t * poly)
    return jnp.where(z < 0, tail, 1.0 - tail), bell * 0.3989422804014327


def layer_norm(rows, gain, shift):
    centred = rows - jnp.mean(rows, axis=-1, keepdims=True)
    factor = lax.rsqrt(jnp.mean(centred * centred, axis=-1, keepdims=True) + 1e-05)
    normed = centred * factor
    return (normed * gain + shift, normed, factor)


def norm_back(upstream, normed, factor, gain):
    scaled = upstream * gain
    return factor * (
        scaled
        - jnp.mean(scaled, axis=-1, keepdims=True)
        - normed * jnp.mean(scaled * normed, axis=-1, keepdims=True)
    )


def matmul(left, right):
    return jnp.dot(left, right, preferred_element_type=F32)


def contract_rows(left, right):
    return lax.dot_general(left, right, (((0,), (0,)), ((), ())), preferred_element_type=F32)


def contract_cols(left, right):
    return lax.dot_general(left, right, (((1,), (1,)), ((), ())), preferred_element_type=F32)


def column_sum(rows):
    return jnp.sum(rows.astype(F32), axis=0)


def half_rows(block, head):
    zero = jnp.zeros((HEAD_DIM, block.shape[1]), block.dtype)
    part = block[head * HEAD_DIM : (head + 1) * HEAD_DIM]
    return jnp.concatenate([part, zero] if head == 0 else [zero, part], axis=0)


def columns(pair, kind):
    return slice((3 * pair + kind) * PAIR, (3 * pair + kind + 1) * PAIR)


def head_rows(n):
    return slice(n * HEAD_DIM, (n + 1) * HEAD_DIM)


def forward_kernel(bounds, qkv_ref, row_ref, col_ref, mixed_ref, logsum_ref, vt_ref):
    length = qkv_ref.shape[0]
    pairs = logsum_ref.shape[0]
    heads = [(p, head) for p in range(pairs) for head in range(2)]
    q_t = [qkv_ref[:, columns(p, 0)].T for p in range(pairs)]
    for p in range(pairs):
        vt_ref[p * PAIR : (p + 1) * PAIR, :] = qkv_ref[:, columns(p, 2)].T
    for i in range(length // BLOCK):
        at = slice(i * BLOCK, (i + 1) * BLOCK)
        row = row_ref[:, at]
        halves = [half_rows(q_t[p][:, at], head) for p, head in heads]

        def step(j, carry):
            span = pl.ds(pl.multiple_of(j * BLOCK, BLOCK), BLOCK)
            same = col_ref[span, :] == row
            products = [matmul(qkv_ref[span, columns(p, 1)], halves[2 * p + head]) for p, head in heads]
            new = []
            for n, (peak, total, mix) in enumerate(carry):
                scores = jnp.where(same, products[n], -1e30)
                top = jnp.maximum(peak, jnp.max(scores, axis=0, keepdims=True))
                weights = jnp.exp(scores - top)
                decay = jnp.exp(peak - top)
                total = total * decay + jnp.sum(weights, axis=0, keepdims=True)
                mix = mix * decay + matmul(vt_ref[head_rows(n), span], weights.astype(BF16))
                new.append((top, total, mix))
            return tuple(new)

        first = (
            jnp.full((1, BLOCK), -1e30, F32),
            jnp.zeros((1, BLOCK), F32),
            jnp.zeros((HEAD_DIM, BLOCK), F32),
        )
        done = lax.fori_loop(bounds[i, 0], bounds[i, 1], step, (first,) * len(heads))
        for p in range(pairs):
            mixes = [mix / total for _, total, mix in done[2 * p : 2 * p + 2]]
            mixed_ref[at, p * PAIR : (p + 1) * PAIR] = jnp.concatenate(mixes, axis=0).T.astype(BF16)
        for n, (p, head) in enumerate(heads):
            logsum_ref[p, head : head + 1, at] = done[n][0] + jnp.log(done[n][1])


def backward_kernel(
    bounds, qkv_ref, row_ref, col_ref, mixed_ref, logsum_ref, grad_ref, out_ref, sums_ref, kt_ref, dk_ref, dv_ref
):
    length = qkv_ref.shape[0]
    pairs = logsum_ref.shape[0]
    heads = [(p, head) for p in range(pairs) for head in range(2)]
    dk_ref[...] = jnp.zeros_like(dk_ref)
    dv_ref[...] = jnp.zeros_like(dv_ref)
    q_t, g_t, delta = [], [], []
    for p in range(pairs):
        lanes = slice(p * PAIR, (p + 1) * PAIR)
        q_t.append(qkv_ref[:, columns(p, 0)].T)
        g_t.append(grad_ref[:, lanes].T)
        kt_ref[lanes, :] = qkv_ref[:, columns(p, 1)].T
        product_t = (grad_ref[:, lanes].astype(F32) * mixed_ref[:, lanes].astype(F32)).T
        for head in range(2):
            delta.append(jnp.sum(product_t[head_rows(head)], axis=0, keepdims=True))
    lane = lax.broadcasted_iota(jnp.int32, (BLOCK, PAIR), 1)
    zero = jnp.zeros((BLOCK, PAIR), BF16)

    def split(x):
        return jnp.concatenate(
            [jnp.where(lane < HEAD_DIM, x, zero), jnp.where(lane >= HEAD_DIM, x, zero)], axis=0
        )

    for i in range(length // BLOCK):
        at = slice(i * BLOCK, (i + 1) * BLOCK)
        row = row_ref[:, at]
        q_halves = [half_rows(q_t[p][:, at], head) for p, head in heads]
        g_halves = [half_rows(g_t[p][:, at], head) for p, head in heads]
        q_split = [split(qkv_ref[at, columns(p, 0)]) for p in range(pairs)]
        g_split = [split(grad_ref[at, p * PAIR : (p + 1) * PAIR]) for p in range(pairs)]
        logsum = [logsum_ref[p, head : head + 1, at] for p, head in heads]

        def step(j, carry):
            span = pl.ds(pl.multiple_of(j * BLOCK, BLOCK), BLOCK)
            same = col_ref[span, :] == row
            scores = [matmul(qkv_ref[span, columns(p, 1)], q_halves[2 * p + head]) for p, head in heads]
            grad_probs = [matmul(qkv_ref[span, columns(p, 2)], g_halves[2 * p + head]) for p, head in heads]
            new = []
            for p in range(pairs):
                probs_low, grad_low = [], []
                for n in (2 * p, 2 * p + 1):
                    probs = jnp.exp(jnp.where(same, scores[n], -1e30) - logsum[n])
                    grad_low.append((probs * (grad_probs[n] - delta[n][:, at])).astype(BF16))
                    probs_low.append(probs.astype(BF16))
                    new.append(carry[n] + matmul(kt_ref[head_rows(n), span], grad_low[-1]))
                lanes = slice(p * PAIR, (p + 1) * PAIR)
                dv_ref[span, lanes] += matmul(jnp.concatenate(probs_low, axis=1), g_split[p])
                dk_ref[span, lanes] += matmul(jnp.concatenate(grad_low, axis=1), q_split[p])
            return tuple(new)

        empty = jnp.zeros((HEAD_DIM, BLOCK), F32)
        done = lax.fori_loop(bounds[i, 0], bounds[i, 1], step, (empty,) * len(heads))
        for p in range(pairs):
            grad_q = jnp.concatenate(done[2 * p : 2 * p + 2], axis=0).T
            out_ref[at, columns(p, 0)] = (grad_q * 0.125).astype(BF16)
    for p in range(pairs):
        lanes = slice(p * PAIR, (p + 1) * PAIR)
        out_ref[:, columns(p, 1)] = dk_ref[:, lanes].astype(BF16)
        out_ref[:, columns(p, 2)] = dv_ref[:, lanes].astype(BF16)
    sums_ref[...] = jnp.sum(out_ref[...].astype(F32), axis=0, keepdims=True)


def block_bounds(starts):
    blocks = starts.reshape(-1, BLOCK)
    least, most = blocks[:, 0], blocks[:, -1]
    low = jnp.sum(most[None, :] < least[:, None], axis=1)
    high = jnp.sum(least[None, :] <= most[:, None], axis=1)
    return jnp.stack([low, high], axis=1).astype(jnp.int32)


def attention_forward(bounds, qkv, starts, index, pairs):
    length = qkv.shape[0]
    operands = (bounds, qkv, starts[None, :], starts[:, None])
    shapes = [shape_of((length, pairs * PAIR), BF16), shape_of((pairs, 2, length), F32)]
    return call(
        forward_kernel,
        "attend",
        (1,),
        [
            pl.BlockSpec((length, pairs * 3 * PAIR), lambda g, b: (0, index)),
            whole((1, length)),
            whole((length, 1)),
        ],
        [whole(x.shape) for x in shapes],
        shapes,
        pairs * 2 * length * length * HEAD_DIM * 4,
        operands,
        scratch=[pltpu.VMEM((pairs * PAIR, length), BF16)],
        prefetch=1,
        vmem=16,
    )


def attention_backward(bounds, qkv, starts, mixed, logsum, grad, index, pairs):
    length = qkv.shape[0]
    operands = (bounds, qkv, starts[None, :], starts[:, None], mixed, logsum, grad)
    shapes = [shape_of((length, pairs * 3 * PAIR), BF16), shape_of((1, pairs * 3 * PAIR), F32)]
    return call(
        backward_kernel,
        "attend_back",
        (1,),
        [
            pl.BlockSpec((length, pairs * 3 * PAIR), lambda g, b: (0, index)),
            whole((1, length)),
            whole((length, 1)),
            whole(mixed.shape),
            whole(logsum.shape),
            pl.BlockSpec((length, pairs * PAIR), lambda g, b: (0, index)),
        ],
        [whole(x.shape) for x in shapes],
        shapes,
        pairs * 2 * length * length * HEAD_DIM * 10,
        operands,
        scratch=[
            pltpu.VMEM((pairs * PAIR, length), BF16),
            pltpu.VMEM((length, pairs * PAIR), F32),
            pltpu.VMEM((length, pairs * PAIR), F32),
        ],
        prefetch=1,
        vmem=24,
    )


MEGA = 1024 * 1024


def whole(shape):
    return pl.BlockSpec(shape, lambda *_: (0,) * len(shape), pipeline_mode=pl.Buffered(1))


def call(kernel, name, grid, in_specs, out_specs, out_shape, flops, operands, scratch=(), prefetch=0, vmem=32):
    moved = sum(x.size * x.dtype.itemsize for x in operands) + sum(
        x.size * x.dtype.itemsize for x in out_shape
    )
    return pl.pallas_call(
        kernel,
        grid_spec=pltpu.PrefetchScalarGridSpec(
            num_scalar_prefetch=prefetch,
            grid=grid,
            in_specs=in_specs,
            out_specs=out_specs,
            scratch_shapes=list(scratch),
        ),
        out_shape=out_shape,
        compiler_params=pltpu.CompilerParams(vmem_limit_bytes=vmem * MEGA),
        cost_estimate=pl.CostEstimate(flops=flops, bytes_accessed=moved, transcendentals=0),
        name=name,
    )(*operands)


def shape_of(shape, dtype):
    return jax.ShapeDtypeStruct(shape, dtype)


def output_kernel(where, *refs):
    (mine_refs, their_refs), (weight_ref, bias_ref, hidden_ref, gain_ref, shift_ref) = (
        (refs[:4], refs[4:6]),
        refs[6:11],
    )
    out_ref, low_ref, normed_ref, factor_ref, mixed_ref = refs[11:]
    h = where[0]
    half = weight_ref.shape[0] // 2
    part = half // 2
    rows = mine_refs[0].shape[0]
    for i in range(2):
        at = slice(i * rows, (i + 1) * rows)
        total = hidden_ref[at, :] + bias_ref[...]
        for cut in range(2):
            mine = pl.ds(pl.multiple_of(h * half + cut * part, 128), part)
            other = pl.ds(pl.multiple_of((1 - h) * half + cut * part, 128), part)
            left, right = mine_refs[2 * cut + i][...], their_refs[cut][at, :]
            mixed_ref[at, mine] = left
            mixed_ref[at, other] = right
            total = total + matmul(left, weight_ref[mine, :]) + matmul(right, weight_ref[other, :])
        out, normed, factor = layer_norm(total, gain_ref[...], shift_ref[...])
        out_ref[at, :] = out
        low_ref[at, :] = out.astype(BF16)
        normed_ref[at, :] = normed
        factor_ref[at, :] = factor


def project_output(h, mine, their, weight, bias, hidden, gain, shift):
    rows, width = hidden.shape
    tok = rows // 2
    part = mine[0].shape[1]
    where = jnp.stack([h, h + 2]).astype(jnp.int32)
    in_specs = [
        pl.BlockSpec((tok, part), lambda g, w: (w[0], 0)),
        pl.BlockSpec((tok, part), lambda g, w: (w[1], 0)),
    ] * 2
    in_specs += [whole((rows, part))] * 2
    in_specs += [whole(weight.shape), whole((1, width)), whole((rows, width)), whole((1, width)), whole((1, width))]
    shapes = [
        shape_of((rows, width), F32),
        shape_of((rows, width), BF16),
        shape_of((rows, width), F32),
        shape_of((rows, 1), F32),
        shape_of((rows, width), BF16),
    ]
    operands = (where, mine[0], mine[0], mine[1], mine[1], their[0], their[1], weight, bias, hidden, gain, shift)
    return call(
        output_kernel,
        "project_output",
        (1,),
        in_specs,
        [whole(x.shape) for x in shapes],
        shapes,
        2 * rows * width * width,
        operands,
        prefetch=1,
    )


def inner_kernel(order, first_ref, *refs):
    pieces, (bias_ref, active_ref, slope_ref, full_ref) = refs[:-4], refs[-4:]
    block = first_ref.shape[1] // 8
    done = 0
    for piece in pieces:
        rows = piece.shape[0]
        at = order[done // block] * block + done % block
        full_ref[pl.ds(pl.multiple_of(at, rows), rows), :] = piece[...]
        done += rows
    rows = first_ref.shape[0]
    step = 256
    for i in range(rows // step):
        at = slice(i * step, (i + 1) * step)
        inner = matmul(first_ref[at, :], full_ref[...]) + bias_ref[...]
        cdf, pdf = normal_cdf_pdf(inner)
        active_ref[0, at, :] = (inner * cdf).astype(BF16)
        slope_ref[0, at, :] = (cdf + inner * pdf).astype(BF16)


def feed_inner(order, first_low, pieces, bias):
    rows, width = first_low.shape
    ff = pieces[0].shape[1]
    tile = ff // 8
    shapes = [
        shape_of((8, rows, tile), BF16),
        shape_of((8, rows, tile), BF16),
        shape_of((width, ff), BF16),
    ]
    return call(
        inner_kernel,
        "feed_inner",
        (8,),
        [whole((rows, width))]
        + [pl.BlockSpec((x.shape[0], tile), lambda t, o: (0, t)) for x in pieces]
        + [pl.BlockSpec((1, tile), lambda t, o: (0, t))],
        [
            pl.BlockSpec((1, rows, tile), lambda t, o: (t, 0, 0)),
            pl.BlockSpec((1, rows, tile), lambda t, o: (t, 0, 0)),
            pl.BlockSpec((width, tile), lambda t, o: (0, t)),
        ],
        shapes,
        2 * rows * width * ff,
        (order, first_low, *pieces, bias),
        prefetch=1,
    )


def outer_kernel(order, active_ref, *refs):
    pieces, refs = refs[:-11], refs[-11:]
    bias_ref, first_ref, up_ref, gain_ref, shift_ref = refs[:5]
    full_ref, out_ref, grad_ref, low_ref, sums_ref, acc_ref = refs[5:]
    t = pl.program_id(0)
    block, tile = full_ref.shape[1:]
    done = 0
    for piece in pieces:
        rows = piece.shape[0]
        full_ref[order[done // block], done % block : done % block + rows] = piece[...]
        done += rows
    total = matmul(active_ref[0], full_ref[0])
    for k in range(1, 8):
        total = total + matmul(active_ref[k], full_ref[k])
    acc_ref[:, pl.ds(pl.multiple_of(t * tile, tile), tile)] = total

    @pl.when(t == pl.num_programs(0) - 1)
    def _():
        rows, width = acc_ref.shape
        step = 128
        gain, shift, bias = gain_ref[...], shift_ref[...], bias_ref[...]
        sums = [jnp.zeros((1, width), F32)] * 3
        for i in range(rows // step):
            at = slice(i * step, (i + 1) * step)
            out, normed, factor = layer_norm(first_ref[at, :] + acc_ref[at, :] + bias, gain, shift)
            out_ref[at, :] = out.astype(BF16)
            up = up_ref[at, :].astype(F32)
            grad = norm_back(up, normed, factor, gain)
            low = grad.astype(BF16)
            grad_ref[at, :] = grad
            low_ref[at, :] = low
            for j, item in enumerate((up * normed, up, low.astype(F32))):
                sums[j] = sums[j] + jnp.sum(item, axis=0, keepdims=True)
        sums_ref[...] = jnp.concatenate(sums + [jnp.zeros((5, width), F32)], axis=0)


def feed_outer(order, active, pieces, bias, first_out, upstream, gain, shift):
    rows, width = first_out.shape
    block = sum(x.shape[0] for x in pieces) // 8
    tile = width // 4
    shapes = [
        shape_of((8, block, width), BF16),
        shape_of((rows, width), BF16),
        shape_of((rows, width), F32),
        shape_of((rows, width), BF16),
        shape_of((8, width), F32),
    ]
    row = whole((1, width))
    return call(
        outer_kernel,
        "feed_outer",
        (4,),
        [whole(active.shape)]
        + [pl.BlockSpec((x.shape[0], tile), lambda t, o: (0, t)) for x in pieces]
        + [row, whole((rows, width)), whole((rows, width)), row, row],
        [pl.BlockSpec((8, block, tile), lambda t, o: (0, 0, t))] + [whole(x.shape) for x in shapes[1:]],
        shapes,
        2 * rows * width * block * 8,
        (order, active, *pieces, bias, first_out, upstream, gain, shift),
        scratch=[pltpu.VMEM((rows, width), F32)],
        prefetch=1,
    )


def gelu_back_kernel(grad_ref, weight_ref, slope_ref, out_ref, sums_ref):
    grad = contract_cols(grad_ref[...], weight_ref[0])
    low = (grad * slope_ref[0].astype(F32)).astype(BF16)
    out_ref[0] = low
    sums_ref[0] = jnp.sum(low.astype(F32), axis=0, keepdims=True)


def gelu_back(grad_outer, full_outer, slope):
    rows, width = grad_outer.shape
    _, block, _ = full_outer.shape
    tile = slope.shape[2]
    shapes = [shape_of(slope.shape, BF16), shape_of((8, 1, tile), F32)]
    return call(
        gelu_back_kernel,
        "gelu_back",
        (8,),
        [
            whole((rows, width)),
            pl.BlockSpec((1, block, width), lambda t: (t, 0, 0)),
            pl.BlockSpec((1, rows, tile), lambda t: (t, 0, 0)),
        ],
        [
            pl.BlockSpec((1, rows, tile), lambda t: (t, 0, 0)),
            pl.BlockSpec((1, 1, tile), lambda t: (t, 0, 0)),
        ],
        shapes,
        2 * rows * width * tile * 8,
        (grad_outer, full_outer, slope),
    )


def first_back_kernel(grad_ref, weight_ref, second_ref, normed_ref, factor_ref, gain_ref, output_ref, *refs):
    out_ref, low_ref, mixed_ref, sums_ref, acc_ref = refs
    t = pl.program_id(0)
    part = contract_cols(grad_ref[0], weight_ref[...])

    @pl.when(t == 0)
    def _():
        acc_ref[...] = second_ref[...] + part

    @pl.when(t > 0)
    def _():
        acc_ref[...] += part

    @pl.when(t == pl.num_programs(0) - 1)
    def _():
        rows, width = acc_ref.shape
        step = 128
        gain = gain_ref[...]
        sums = [jnp.zeros((1, width), F32)] * 3
        for i in range(rows // step):
            at = slice(i * step, (i + 1) * step)
            up, normed = acc_ref[at, :], normed_ref[at, :]
            grad = norm_back(up, normed, factor_ref[at, :], gain)
            low = grad.astype(BF16)
            out_ref[at, :] = grad
            low_ref[at, :] = low
            for j, item in enumerate((up * normed, up, low.astype(F32))):
                sums[j] = sums[j] + jnp.sum(item, axis=0, keepdims=True)
        sums_ref[...] = jnp.concatenate(sums + [jnp.zeros((5, width), F32)], axis=0)
        mixed_ref[...] = contract_cols(low_ref[...], output_ref[...]).astype(BF16)


def first_back(grad_inner, full_inner, grad_second, normed, factor, gain, full_output):
    rows, width = grad_second.shape
    tile = grad_inner.shape[2]
    shapes = [
        shape_of((rows, width), F32),
        shape_of((rows, width), BF16),
        shape_of((rows, width), BF16),
        shape_of((8, width), F32),
    ]
    return call(
        first_back_kernel,
        "first_back",
        (8,),
        [
            pl.BlockSpec((1, rows, tile), lambda t: (t, 0, 0)),
            pl.BlockSpec((width, tile), lambda t: (0, t)),
            whole((rows, width)),
            whole((rows, width)),
            whole((rows, 1)),
            whole((1, width)),
            whole(full_output.shape),
        ],
        [whole(x.shape) for x in shapes],
        shapes,
        2 * rows * width * (tile * 8 + width),
        (grad_inner, full_inner, grad_second, normed, factor, gain, full_output),
        scratch=[pltpu.VMEM((rows, width), F32)],
    )


def block_grad_kernel(order, left_ref, right_ref, out_ref):
    out_ref[0] = contract_rows(left_ref[0], right_ref[...]).astype(BF16)


def block_grad(order, left, right):
    rows, width = right.shape
    block = left.shape[2]
    shapes = [shape_of((4, block, width), BF16)]
    return call(
        block_grad_kernel,
        "block_grad",
        (4,),
        [pl.BlockSpec((1, rows, block), lambda i, o: (o[i], 0, 0)), whole((rows, width))],
        [pl.BlockSpec((1, block, width), lambda i, o: (i, 0, 0))],
        shapes,
        2 * rows * width * block * 4,
        (order, left, right),
        prefetch=1,
    )[0]


def turn_strips(order, left_ref, turned_ref):
    block = turned_ref.shape[0] // 4
    for i in range(4):
        strip = left_ref[:, pl.ds(pl.multiple_of(order[i] * block, block), block)]
        turned_ref[i * block : (i + 1) * block, : strip.shape[0]] = strip.T


def tile_grad_kernel(order, left_ref, right_ref, out_ref, turned_ref):
    block = out_ref.shape[1]

    @pl.when(pl.program_id(0) == 0)
    def _():
        turn_strips(order, left_ref, turned_ref)

    out = matmul(turned_ref[...], right_ref[0]).astype(BF16)
    for i in range(4):
        out_ref[i] = out[i * block : (i + 1) * block]


def tile_grad(order, left, right):
    rows, width = left.shape
    block = width // 8
    tiles, _, tile = right.shape
    shapes = [shape_of((4, block, tiles * tile), BF16)]
    return call(
        tile_grad_kernel,
        "tile_grad",
        (tiles,),
        [whole((rows, width)), pl.BlockSpec((1, rows, tile), lambda t, o: (t, 0, 0))],
        [pl.BlockSpec((4, block, tile), lambda t, o: (0, 0, t))],
        shapes,
        2 * rows * block * 4 * tiles * tile,
        (order, left, right),
        scratch=[pltpu.VMEM((4 * block, rows), BF16)],
        prefetch=1,
        vmem=12,
    )[0]


def strip_grad_kernel(
    parts, order, left_ref, first_ref, second_ref, extra_ref, low_ref, third_ref, out_ref, turned_ref
):
    t = pl.program_id(0)
    last = parts[0] + parts[1]
    block = turned_ref.shape[0] // 4

    @pl.when(t == 0)
    def _():
        turn_strips(order, left_ref, turned_ref)

    @pl.when(t == last)
    def _():
        turn_strips(order, low_ref, turned_ref)

    def put(right, extra):
        out = matmul(turned_ref[:, : right.shape[0]], right).astype(BF16)
        for i in range(4):
            out_ref[i, :block] = out[i * block : (i + 1) * block]
            out_ref[i, block:] = extra_ref[order[i]] if extra else jnp.zeros_like(out_ref[i, block:])

    @pl.when(t < parts[0])
    def _():
        put(first_ref[...], True)

    @pl.when((t >= parts[0]) & (t < last))
    def _():
        put(second_ref[...], True)

    @pl.when(t >= last)
    def _():
        put(third_ref[...], False)


def strip_grad(order, left, first, second, extra, low, third):
    rows, width = left.shape
    block = width // 8
    tile = 512 if first.shape[1] % 512 == 0 else 256
    parts = [x.shape[1] // tile for x in (first, second, third)]
    total = sum(parts)
    tall = block + extra.shape[1]
    shapes = [shape_of((4, tall, total * tile), BF16)]
    return call(
        partial(strip_grad_kernel, parts),
        "strip_grad",
        (total,),
        [
            whole((rows, width)),
            pl.BlockSpec((rows, tile), lambda t, o: (0, jnp.minimum(t, parts[0] - 1))),
            pl.BlockSpec((rows, tile), lambda t, o: (0, jnp.clip(t - parts[0], 0, parts[1] - 1))),
            pl.BlockSpec(
                (8, extra.shape[1], tile), lambda t, o: (0, 0, jnp.minimum(t, parts[0] + parts[1] - 1))
            ),
            whole(low.shape),
            pl.BlockSpec((low.shape[0], tile), lambda t, o: (0, jnp.maximum(t - parts[0] - parts[1], 0))),
        ],
        [pl.BlockSpec((4, tall, tile), lambda t, o: (0, 0, t))],
        shapes,
        2 * rows * block * 4 * total * tile,
        (order, left, first, second, extra, low, third),
        scratch=[pltpu.VMEM((4 * block, rows), BF16)],
        prefetch=1,
        vmem=20,
    )[0]


def hidden_back_kernel(where, *refs):
    lefts, weight_ref, rest = refs[:2], refs[2], refs[3:]
    part = lefts[0].shape[1]
    total = contract_cols(lefts[0][...], weight_ref[:, :part]) + contract_cols(lefts[1][...], weight_ref[:, part:])
    if len(rest) == 2:
        total = total + rest[0][...]
    rest[-1][...] = total.astype(rest[-1].dtype)


def hidden_back(parity, grads, weight, base, tok):
    width = weight.shape[0]
    part = grads[0].shape[1]
    where = jnp.stack([parity, parity + 2]).astype(jnp.int32)
    row = pl.BlockSpec((tok, width), lambda i, w: (i, 0))
    extra = () if base is None else (base,)
    shapes = [shape_of((2 * tok, width), BF16 if base is None else F32)]
    return call(
        hidden_back_kernel,
        "hidden_back",
        (2,),
        [pl.BlockSpec((tok, part), lambda i, w: (w[i], 0))] * 2 + [whole(weight.shape)] + [row] * len(extra),
        [row],
        shapes,
        2 * 2 * tok * width * part * 2,
        (where, *grads, weight, *extra),
        prefetch=1,
    )[0]


def after(x, *deps):
    return lax.optimization_barrier((x, deps))[0]


class Steps:
    def __init__(self):
        self.last = ()

    def __call__(self, fn, *args):
        args, _ = lax.optimization_barrier((args, self.last))
        out = fn(*args)
        self.last = out
        return out


def flip(x, axis, size, bit):
    return lax.ppermute(x, axis, [(i, i ^ bit) for i in range(size)])


def swap(x, bit):
    return flip(x, "fsdp", 8, bit)


def widen(*items):
    return sum(item.astype(F32) for item in items)


class CubeSum:
    def __init__(self, send, width, x_columns):
        self.got = swap(send, 1)
        self.parts = []
        if x_columns > 0:
            self.parts.append((slice(0, x_columns), 1, 2, 2, 4))
        if x_columns < width:
            self.parts.append((slice(x_columns, width), 2, 1, 4, 2))

    def first_hop(self, steps, keep):
        def add(keep, got):
            return [
                jnp.stack([widen(keep[i, :, cols], got[i, :, cols]).astype(BF16) for i in (away, 3)])
                for cols, _, away, _, _ in self.parts
            ]

        self.keep = keep
        there = steps(add, keep, self.got)
        self.back = [swap(x, part[3]) for x, part in zip(there, self.parts)]

    def second_hop(self, steps):
        def add(keep, got, back):
            here, there = [], []
            for (cols, near, _, _, _), b in zip(self.parts, back):
                here.append(widen(keep[0, :, cols], got[0, :, cols], b[0]))
                there.append(widen(keep[near, :, cols], got[near, :, cols], b[1]).astype(BF16))
            return here, there

        self.here, there = steps(add, self.keep, self.got, self.back)
        self.last = [swap(x, part[4]) for x, part in zip(there, self.parts)]

    def result(self, steps):
        def add(here, last):
            sums = [widen(x, y).astype(BF16) for x, y in zip(here, last)]
            return sums[0] if len(sums) == 1 else jnp.concatenate(sums, axis=1)

        return steps(add, self.here, self.last)


class PlainSum:
    def __init__(self, product, extra=()):
        self.product, self.extra = product.astype(BF16), extra

    def first_hop(self, steps, keep):
        pass

    def second_hop(self, steps):
        pass

    def result(self, steps):
        share = lax.psum_scatter(self.product, "fsdp", scatter_dimension=0, tiled=True)
        lines = [lax.psum_scatter(x, "fsdp", scatter_dimension=0, tiled=False) for x in self.extra]
        return (share, *lines) if lines else share


def pair_pack(parts):
    rows = parts[0].shape[0]
    return jnp.stack([p.reshape(rows, -1, PAIR) for p in parts], axis=2).reshape(rows, -1)


def pair_unpack(packed):
    rows = packed.shape[0]
    cut = packed.reshape(rows, -1, 3, PAIR)
    return [cut[:, :, i].reshape(rows, -1) for i in range(3)]


def body(
    fsdp,
    stream_in,
    timestep,
    doc_start,
    query_weight,
    key_weight,
    value_weight,
    output_weight,
    query_bias,
    value_bias,
    output_bias,
    first_gain,
    first_shift,
    inner_weight,
    inner_bias,
    outer_weight,
    outer_bias,
    second_gain,
    second_shift,
    cotangent,
):
    cube = fsdp == 8
    steps = Steps()
    me = lax.axis_index("fsdp")
    streams, tok, width = stream_in.shape
    own_rows = query_weight.shape[0]
    half = width // 2
    ff = inner_weight.shape[1]
    length = 4 * tok
    z = lax.axis_index("seq")
    h, s = z % 2, z // 2

    def flip_h(x):
        return flip(x, "seq", 4, 1)

    def flip_s(x):
        return flip(x, "seq", 4, 2)

    def in_order(mine, other):
        return jnp.where(s == 0, jnp.concatenate([mine, other]), jnp.concatenate([other, mine]))

    def pick(x, index, axis=0):
        return lax.dynamic_index_in_dim(x, index, axis, keepdims=False)

    head_cols = [lax.dynamic_slice_in_dim(w, h * half, half, 1) for w in (query_weight, key_weight, value_weight)]
    small = jnp.concatenate(
        [
            query_bias,
            value_bias,
            output_bias,
            first_gain,
            first_shift,
            outer_bias,
            second_gain,
            second_shift,
            inner_bias,
        ]
    )
    packed = pair_pack(head_cols)
    own = pick(stream_in, s)
    if cube:
        owners = [me ^ m for m in range(8)]
        packed = jnp.concatenate([packed, jnp.broadcast_to(small[None, :], (16, small.shape[0]))])
        gathered = lax.all_gather(packed, "fsdp", axis=0, tiled=False)
        full_qkv = gathered[:, :own_rows].reshape(-1, packed.shape[1])
        small_rows = gathered[:, own_rows]
        output_w = after(output_weight, gathered)
        full_output = lax.all_gather(output_w, "fsdp", axis=0, tiled=True)
        inner_w = after(inner_weight, packed)
        ix, iy = swap(inner_w, 2), swap(inner_w, 4)
        distant = flip_s(pick(stream_in, 1 - s))
        beside = flip_h(own)
        cut = own_rows // 2
        top, bottom, distant, beside, inner_w, outer_w = steps(
            lambda x, y, *rest: (x[:cut], y[cut:], *rest), ix, iy, distant, beside, inner_w, outer_weight
        )
        corner = flip_h(distant)
        jy, jx = swap(top, 4), swap(bottom, 2)
        ic = swap(inner_w, 1)
    else:
        owners = list(range(8))

        def gather(piece):
            full = lax.all_gather(piece, "fsdp", axis=0, tiled=True)
            return list(full.reshape(8, full.shape[0] // 8, full.shape[1]))

        distant, beside = flip_s(pick(stream_in, 1 - s)), flip_h(own)
        corner = flip_h(distant)
        full_qkv = lax.all_gather(packed, "fsdp", axis=0, tiled=True)
        full_output = lax.all_gather(output_weight, "fsdp", axis=0, tiled=True)
        inner_pieces, outer_pieces = gather(inner_weight), gather(outer_weight)
        small_rows = lax.all_gather(small, "fsdp", axis=0, tiled=False)
    order = jnp.stack([jnp.asarray(o, jnp.int32) for o in owners])
    small_rows = small_rows.astype(F32)
    qbias, vbias, obias, gain_one, shift_one, obias_two, gain_two, shift_two = [
        small_rows[:, i * own_rows : (i + 1) * own_rows].reshape(1, -1) for i in range(8)
    ]
    ibias = small_rows[:, 8 * own_rows :].reshape(1, -1)

    ts = pick(timestep, s).astype(F32)

    def place(own, beside, distant, corner):
        stream = jnp.zeros((length, width), BF16)
        for mask, block in ((0, own), (1, beside), (2, distant), (3, corner)):
            stream = lax.dynamic_update_slice(stream, block, ((z ^ mask) * tok, 0))
        stream_low = (stream.astype(F32) + ts).astype(BF16)
        return stream_low, in_order(own, distant).astype(F32) + ts

    if cube:
        own, ic, ix, corner, outer_w = steps(lambda *x: x, own, ic, ix, corner, outer_w)
        ox, oy = swap(outer_w, 2), swap(outer_w, 4)
        ixc = swap(ix, 1)
    stream_low, hidden = steps(place, own, beside, distant, corner)
    starts = pick(doc_start, s)
    bounds = block_bounds(starts)

    qb = lax.dynamic_slice_in_dim(qbias, h * half, half, 1)
    vb = lax.dynamic_slice_in_dim(vbias, h * half, half, 1)
    bias_row = pair_pack([qb, jnp.zeros_like(qb), vb])
    scale_row = pair_pack([jnp.full((1, half), 0.125, F32), jnp.ones((1, half), F32), jnp.ones((1, half), F32)])
    if cube:
        stream_low, ixc, iy = steps(lambda *x: x, stream_low, ixc, iy)
        iyc = swap(iy, 1)
    qkv = steps(
        lambda x, w, b: ((matmul(x, w) + b) * scale_row).astype(BF16), stream_low, full_qkv, bias_row
    )
    pairs = half // PAIR
    part = pairs // 2

    def rows_of(x, parity):
        cut = x.reshape(2, 2, tok, x.shape[1])
        return pick(cut, parity, 1).reshape(2 * tok, x.shape[1])

    def attend(index, qkv):
        return attention_forward(bounds, qkv, starts, index, part)

    if cube:
        jy, jx, iyc, qkv = steps(lambda *x: x, jy, jx, iyc, qkv)
        jyc, jxc = swap(jy, 1), swap(jx, 1)
    mixed_a, logsum_a = steps(partial(attend, 0), qkv)
    out_a, jyc, jxc = steps(
        lambda x, *rest: (rows_of(x, 1 - h), *rest), mixed_a, *((jyc, jxc) if cube else (0.0, 0.0))
    )
    their_a = flip_h(out_a)
    mixed_b, logsum_b = steps(partial(attend, 1), qkv)
    cotangent_out = pick(cotangent, 1 - s)
    if cube:
        inner_pieces = [inner_w, ic, ix, ixc, iy, iyc, jy, jx, jyc, jxc]
        cut = outer_weight.shape[0] // 2
        top, bottom, ox, oy = steps(lambda x, y: (x[:cut], y[cut:], x, y), ox, oy)
        jy, jx = swap(top, 4), swap(bottom, 2)
    out_b, their_a, cotangent_out = steps(lambda x, *rest: (rows_of(x, 1 - h), *rest), mixed_b, their_a, cotangent_out)
    their_b = flip_h(out_b)
    if cube:
        oxc = swap(ox, 1)
    moved = flip_s(cotangent_out)
    first_out, first_low, first_normed, first_factor, mixed = steps(
        partial(project_output, h),
        (mixed_a, mixed_b),
        (their_a, their_b),
        full_output,
        obias,
        hidden,
        gain_one,
        shift_one,
    )

    if cube:
        jy, jx, oxc, oy, outer_w, first_low = steps(lambda *x: x, jy, jx, oxc, oy, outer_w, first_low)
        oc, oyc, jyc, jxc = swap(outer_w, 1), swap(oy, 1), swap(jy, 1), swap(jx, 1)
        outer_pieces = [outer_w, oc, ox, oxc, oy, oyc, jy, jx, jyc, jxc]
    active, slope, full_inner = steps(partial(feed_inner, order), first_low, inner_pieces, ibias)
    upstream = in_order(pick(cotangent, s), moved)
    full_outer, result, grad_second_in, grad_outer, second_sums = steps(
        partial(feed_outer, order), active, outer_pieces, obias_two, first_out, upstream, gain_two, shift_two
    )
    result = result.reshape(2, tok, width)
    result_own, result_out = steps(lambda x: (pick(x, s), pick(x, 1 - s)), result)
    result_away = flip_s(result_out)

    if cube:
        send_order = jnp.stack([me ^ m for m in (1, 5, 3, 7)]).astype(jnp.int32)
        keep_order = jnp.stack([me ^ m for m in (0, 4, 2, 6)]).astype(jnp.int32)

    if cube:
        outer_send = steps(partial(block_grad, send_order), active, grad_outer)
        outer_sum = CubeSum(outer_send, width, half)
        outer_keep = steps(partial(block_grad, keep_order), active, grad_outer)
    else:
        outer_keep = ()
        outer_sum = PlainSum(contract_rows(active.transpose(1, 0, 2).reshape(2 * tok, -1), grad_outer))
    grad_inner, inner_sums = steps(gelu_back, grad_outer, full_outer, slope)
    outer_sum.first_hop(steps, outer_keep)
    if cube:
        inner_send = steps(partial(tile_grad, send_order), first_low, grad_inner)
        inner_sum = CubeSum(inner_send, ff, ff // 2)
    else:
        inner_sum = PlainSum(contract_rows(first_low, grad_inner.transpose(1, 0, 2).reshape(2 * tok, -1)))

    def first_step(*args):
        grad_first_in, grad_attended, grad_mixed, sums = first_back(*args)
        wide = half // 2
        theirs = lax.dynamic_slice_in_dim(grad_mixed, (1 - h) * half, half, 1)
        mine = lax.dynamic_slice_in_dim(grad_mixed, h * half, half, 1)
        return grad_first_in, grad_attended, sums, theirs, mine

    grad_first_in, grad_attended, first_sums, theirs, mine = steps(
        first_step, grad_inner, full_inner, grad_second_in, first_normed, first_factor, gain_one, full_output
    )
    received = flip_h(theirs)
    inner_keep = steps(partial(tile_grad, keep_order), first_low, grad_inner) if cube else ()
    outer_sum.second_hop(steps)

    def to_heads(mine, received):
        mine = mine.reshape(2, 1, tok, half)
        received = received.reshape(2, 1, tok, half)
        return jnp.where(
            h == 0, jnp.concatenate([mine, received], axis=1), jnp.concatenate([received, mine], axis=1)
        ).reshape(length, half)

    grad_heads = steps(to_heads, mine, received)

    def seq_sum(share):
        def halve(x, bit):
            pair = x.reshape(2, x.shape[0] // 2, -1)
            return pick(pair, bit), pick(pair, 1 - bit)

        def join(mine, other, bit):
            return jnp.where(bit == 0, jnp.concatenate([mine, other]), jnp.concatenate([other, mine]))

        mine, out = halve(share, h)
        back = flip_h(out)
        yield
        mine, out = steps(lambda m, b: halve(widen(m, b), s), mine, back)
        back = flip_s(out.astype(BF16))
        yield
        mine = steps(lambda m, b: widen(m, b).astype(BF16), mine, back)
        back = flip_s(mine)
        yield
        mine = steps(lambda m, b: join(m, b, s), mine, back)
        back = flip_h(mine)
        yield
        yield steps(lambda m, b: join(m, b, h).astype(F32), mine, back)

    def attend_back(index, qkv, mixed, logsum, grad):
        return attention_backward(bounds, qkv, starts, mixed, logsum, grad, index, part)

    grad_a, sums_a = steps(partial(attend_back, 0), qkv, mixed_a, logsum_a, grad_heads)
    inner_sum.first_hop(steps, inner_keep)
    outer_share = outer_sum.result(steps)
    outer_share, result_away = steps(lambda *x: x, outer_share, result_away)
    outer_steps = seq_sum(outer_share)
    next(outer_steps)
    grad_b, sums_b = steps(partial(attend_back, 1), qkv, mixed_b, logsum_b, grad_heads)
    away = flip_h(
        steps(lambda a, b, w: hidden_back(1 - h, (a, b), w, None, tok), grad_a, grad_b, full_qkv)
    )
    zero_half = jnp.zeros((half,), F32)

    def spread(v):
        v = v.reshape(-1)
        return jnp.where(h == 0, jnp.concatenate([v, zero_half]), jnp.concatenate([zero_half, v]))

    grad_q_cols, _, grad_v_cols = pair_unpack(jnp.concatenate([sums_a, sums_b], axis=1))
    vectors = jnp.concatenate(
        [
            v.reshape(fsdp, -1)
            for v in (
                spread(grad_q_cols),
                spread(grad_v_cols),
                first_sums[2],
                first_sums[0],
                first_sums[1],
                second_sums[2],
                second_sums[0],
                second_sums[1],
                inner_sums,
            )
        ],
        axis=1,
    ).astype(BF16)
    if cube:
        lines = vectors.reshape(fsdp, 1, -1)
        lines = jnp.concatenate([lines, jnp.zeros((fsdp, 15, lines.shape[2]), BF16)], axis=1)
        qkv_operands = (stream_low, grad_a, grad_b, lines, mixed, grad_attended)
        qkv_send = steps(partial(strip_grad, send_order), *qkv_operands)
        qkv_sum = CubeSum(qkv_send, qkv_send.shape[2], qkv_send.shape[2] // 2)
        inner_sum.second_hop(steps)
        next(outer_steps)
        qkv_keep = steps(partial(strip_grad, keep_order), *qkv_operands)
    else:
        qkv_keep = ()
        both = jnp.concatenate([grad_a, grad_b], axis=1)
        both = jnp.concatenate([contract_rows(stream_low, both), contract_rows(mixed, grad_attended)], axis=1)
        qkv_sum = PlainSum(both, (vectors,))
    kept = steps(lambda a, b, w, g: hidden_back(h, (a, b), w, g, tok), grad_a, grad_b, full_qkv, grad_first_in)

    def split_rows(kept, away):
        grad_hidden = (kept + away.astype(F32)).reshape(2, tok, width)
        return pick(grad_hidden, s), pick(grad_hidden, 1 - s).astype(BF16)

    grad_own, grad_out = steps(split_rows, kept, away)
    grad_away = flip_s(grad_out)
    if not cube:
        next(outer_steps)
    next(outer_steps)
    inner_share = inner_sum.result(steps)
    inner_steps = seq_sum(inner_share)
    next(inner_steps)
    qkv_sum.first_hop(steps, qkv_keep)
    next(outer_steps)
    next(inner_steps)
    qkv_sum.second_hop(steps)
    outer_grad = next(outer_steps)
    next(inner_steps)

    grad_away = grad_away.astype(F32)
    input_grad = jnp.where(s == 0, jnp.stack([grad_own, grad_away]), jnp.stack([grad_away, grad_own]))
    layer_out = jnp.where(s == 0, jnp.stack([result_own, result_away]), jnp.stack([result_away, result_own]))

    def swap_heads(mine, other):
        return jnp.where(h == 0, jnp.concatenate([mine, other], axis=1), jnp.concatenate([other, mine], axis=1))

    qkv_share = qkv_sum.result(steps)
    qkv_share, extra = qkv_share if not cube else (qkv_share, None)
    qkv_back = flip_s(qkv_share)
    next(inner_steps)
    qkv_mine = steps(lambda x, y: widen(x, y).astype(BF16), qkv_share, qkv_back)
    qkv_other = flip_h(qkv_mine)
    inner_grad = next(inner_steps)
    three = 3 * half
    output_grad = widen(qkv_mine[:own_rows, three:], qkv_other[:own_rows, three:])
    if cube:
        sums = widen(qkv_mine[own_rows, :three], qkv_other[own_rows, :three])
    else:
        sums = lax.psum(extra.astype(F32), "seq")
    qkv_grads = [
        swap_heads(mine, other).astype(F32)
        for mine, other in zip(
            pair_unpack(qkv_mine[:own_rows, :three]), pair_unpack(qkv_other[:own_rows, :three])
        )
    ]
    cut = [sums[i * own_rows : (i + 1) * own_rows] for i in range(8)]
    return (
        layer_out,
        input_grad,
        qkv_grads[0],
        qkv_grads[1],
        qkv_grads[2],
        output_grad,
        cut[0],
        cut[1],
        cut[2],
        cut[3],
        cut[4],
        inner_grad,
        sums[8 * own_rows :],
        outer_grad,
        cut[5],
        cut[6],
        cut[7],
    )


def solution(mesh):
    rows = P("fsdp", "seq", None)
    mat = P("fsdp", None)
    vec = P("fsdp")
    in_specs = (rows, mat, mat) + (mat,) * 4 + (vec,) * 5 + (mat, vec, mat, vec, vec, vec) + (rows,)
    out_specs = (rows, rows) + (mat,) * 4 + (vec,) * 5 + (mat, vec, mat, vec, vec, vec)
    return jax.shard_map(
        partial(body, mesh.shape["fsdp"]), mesh=mesh, in_specs=in_specs, out_specs=out_specs, check_vma=False
    )
```

```python
from functools import partial

import jax
import jax.numpy as jnp
from jax import lax
from jax.experimental import pallas as pl
from jax.experimental.pallas import tpu as pltpu
from jax.sharding import PartitionSpec as P

HEAD_DIM = 64
PAIR = 2 * HEAD_DIM
BLOCK = 256
F32 = jnp.float32
BF16 = jnp.bfloat16

PHI_POLY = (
    0.11962928975633808,
    0.12075411058236112,
    0.09991242675653945,
    0.12856547821204567,
    -0.053691543682108024,
    0.20636272322745108,
    -0.15720876784307727,
    0.03567620985200702,
)


def normal_cdf_pdf(z):
    u = jnp.abs(z)
    bell = jnp.exp(-0.5 * u * u)
    t = 1.0 / (1.0 + 0.3 * u)
    poly = jnp.full_like(t, PHI_POLY[-1])
    for coef in PHI_POLY[-2::-1]:
        poly = poly * t + coef
    tail = bell * (t * poly)
    return jnp.where(z < 0, tail, 1.0 - tail), bell * 0.3989422804014327


def layer_norm(rows, gain, shift):
    centred = rows - jnp.mean(rows, axis=-1, keepdims=True)
    factor = lax.rsqrt(jnp.mean(centred * centred, axis=-1, keepdims=True) + 1e-05)
    normed = centred * factor
    return (normed * gain + shift, normed, factor)


def norm_back(upstream, normed, factor, gain):
    scaled = upstream * gain
    return factor * (
        scaled
        - jnp.mean(scaled, axis=-1, keepdims=True)
        - normed * jnp.mean(scaled * normed, axis=-1, keepdims=True)
    )


def matmul(left, right):
    return jnp.dot(left, right, preferred_element_type=F32)


def contract_rows(left, right):
    return lax.dot_general(left, right, (((0,), (0,)), ((), ())), preferred_element_type=F32)


def contract_cols(left, right):
    return lax.dot_general(left, right, (((1,), (1,)), ((), ())), preferred_element_type=F32)


def column_sum(rows):
    return jnp.sum(rows.astype(F32), axis=0)


def half_rows(block, head):
    zero = jnp.zeros((HEAD_DIM, block.shape[1]), block.dtype)
    part = block[head * HEAD_DIM : (head + 1) * HEAD_DIM]
    return jnp.concatenate([part, zero] if head == 0 else [zero, part], axis=0)


def columns(pair, kind):
    return slice((3 * pair + kind) * PAIR, (3 * pair + kind + 1) * PAIR)


def head_rows(n):
    return slice(n * HEAD_DIM, (n + 1) * HEAD_DIM)


def forward_kernel(bounds, qkv_ref, row_ref, col_ref, mixed_ref, logsum_ref, vt_ref):
    length = qkv_ref.shape[0]
    pairs = logsum_ref.shape[0]
    heads = [(p, head) for p in range(pairs) for head in range(2)]
    q_t = [qkv_ref[:, columns(p, 0)].T for p in range(pairs)]
    for p in range(pairs):
        vt_ref[p * PAIR : (p + 1) * PAIR, :] = qkv_ref[:, columns(p, 2)].T
    for i in range(length // BLOCK):
        at = slice(i * BLOCK, (i + 1) * BLOCK)
        row = row_ref[:, at]
        halves = [half_rows(q_t[p][:, at], head) for p, head in heads]

        def step(j, carry):
            span = pl.ds(pl.multiple_of(j * BLOCK, BLOCK), BLOCK)
            same = col_ref[span, :] == row
            products = [matmul(qkv_ref[span, columns(p, 1)], halves[2 * p + head]) for p, head in heads]
            new = []
            for n, (peak, total, mix) in enumerate(carry):
                scores = jnp.where(same, products[n], -1e30)
                top = jnp.maximum(peak, jnp.max(scores, axis=0, keepdims=True))
                weights = jnp.exp(scores - top)
                decay = jnp.exp(peak - top)
                total = total * decay + jnp.sum(weights, axis=0, keepdims=True)
                mix = mix * decay + matmul(vt_ref[head_rows(n), span], weights.astype(BF16))
                new.append((top, total, mix))
            return tuple(new)

        first = (
            jnp.full((1, BLOCK), -1e30, F32),
            jnp.zeros((1, BLOCK), F32),
            jnp.zeros((HEAD_DIM, BLOCK), F32),
        )
        done = lax.fori_loop(bounds[i, 0], bounds[i, 1], step, (first,) * len(heads))
        for p in range(pairs):
            mixes = [mix / total for _, total, mix in done[2 * p : 2 * p + 2]]
            mixed_ref[at, p * PAIR : (p + 1) * PAIR] = jnp.concatenate(mixes, axis=0).T.astype(BF16)
        for n, (p, head) in enumerate(heads):
            logsum_ref[p, head : head + 1, at] = done[n][0] + jnp.log(done[n][1])


def backward_kernel(
    bounds, qkv_ref, row_ref, col_ref, mixed_ref, logsum_ref, grad_ref, out_ref, sums_ref, kt_ref, dk_ref, dv_ref
):
    length = qkv_ref.shape[0]
    pairs = logsum_ref.shape[0]
    heads = [(p, head) for p in range(pairs) for head in range(2)]
    dk_ref[...] = jnp.zeros_like(dk_ref)
    dv_ref[...] = jnp.zeros_like(dv_ref)
    q_t, g_t, delta = [], [], []
    for p in range(pairs):
        lanes = slice(p * PAIR, (p + 1) * PAIR)
        q_t.append(qkv_ref[:, columns(p, 0)].T)
        g_t.append(grad_ref[:, lanes].T)
        kt_ref[lanes, :] = qkv_ref[:, columns(p, 1)].T
        product_t = (grad_ref[:, lanes].astype(F32) * mixed_ref[:, lanes].astype(F32)).T
        for head in range(2):
            delta.append(jnp.sum(product_t[head_rows(head)], axis=0, keepdims=True))
    lane = lax.broadcasted_iota(jnp.int32, (BLOCK, PAIR), 1)
    zero = jnp.zeros((BLOCK, PAIR), BF16)

    def split(x):
        return jnp.concatenate(
            [jnp.where(lane < HEAD_DIM, x, zero), jnp.where(lane >= HEAD_DIM, x, zero)], axis=0
        )

    for i in range(length // BLOCK):
        at = slice(i * BLOCK, (i + 1) * BLOCK)
        row = row_ref[:, at]
        q_halves = [half_rows(q_t[p][:, at], head) for p, head in heads]
        g_halves = [half_rows(g_t[p][:, at], head) for p, head in heads]
        q_split = [split(qkv_ref[at, columns(p, 0)]) for p in range(pairs)]
        g_split = [split(grad_ref[at, p * PAIR : (p + 1) * PAIR]) for p in range(pairs)]
        logsum = [logsum_ref[p, head : head + 1, at] for p, head in heads]

        def step(j, carry):
            span = pl.ds(pl.multiple_of(j * BLOCK, BLOCK), BLOCK)
            same = col_ref[span, :] == row
            scores = [matmul(qkv_ref[span, columns(p, 1)], q_halves[2 * p + head]) for p, head in heads]
            grad_probs = [matmul(qkv_ref[span, columns(p, 2)], g_halves[2 * p + head]) for p, head in heads]
            new = []
            for p in range(pairs):
                probs_low, grad_low = [], []
                for n in (2 * p, 2 * p + 1):
                    probs = jnp.exp(jnp.where(same, scores[n], -1e30) - logsum[n])
                    grad_low.append((probs * (grad_probs[n] - delta[n][:, at])).astype(BF16))
                    probs_low.append(probs.astype(BF16))
                    new.append(carry[n] + matmul(kt_ref[head_rows(n), span], grad_low[-1]))
                lanes = slice(p * PAIR, (p + 1) * PAIR)
                dv_ref[span, lanes] += matmul(jnp.concatenate(probs_low, axis=1), g_split[p])
                dk_ref[span, lanes] += matmul(jnp.concatenate(grad_low, axis=1), q_split[p])
            return tuple(new)

        empty = jnp.zeros((HEAD_DIM, BLOCK), F32)
        done = lax.fori_loop(bounds[i, 0], bounds[i, 1], step, (empty,) * len(heads))
        for p in range(pairs):
            grad_q = jnp.concatenate(done[2 * p : 2 * p + 2], axis=0).T
            out_ref[at, columns(p, 0)] = (grad_q * 0.125).astype(BF16)
    for p in range(pairs):
        lanes = slice(p * PAIR, (p + 1) * PAIR)
        out_ref[:, columns(p, 1)] = dk_ref[:, lanes].astype(BF16)
        out_ref[:, columns(p, 2)] = dv_ref[:, lanes].astype(BF16)
    sums_ref[...] = jnp.sum(out_ref[...].astype(F32), axis=0, keepdims=True)


def block_bounds(starts):
    blocks = starts.reshape(-1, BLOCK)
    least, most = blocks[:, 0], blocks[:, -1]
    low = jnp.sum(most[None, :] < least[:, None], axis=1)
    high = jnp.sum(least[None, :] <= most[:, None], axis=1)
    return jnp.stack([low, high], axis=1).astype(jnp.int32)


def attention_forward(bounds, qkv, starts, index, pairs):
    length = qkv.shape[0]
    operands = (bounds, qkv, starts[None, :], starts[:, None])
    shapes = [shape_of((length, pairs * PAIR), BF16), shape_of((pairs, 2, length), F32)]
    return call(
        forward_kernel,
        "attend",
        (1,),
        [
            pl.BlockSpec((length, pairs * 3 * PAIR), lambda g, b: (0, index)),
            whole((1, length)),
            whole((length, 1)),
        ],
        [whole(x.shape) for x in shapes],
        shapes,
        pairs * 2 * length * length * HEAD_DIM * 4,
        operands,
        scratch=[pltpu.VMEM((pairs * PAIR, length), BF16)],
        prefetch=1,
        vmem=16,
    )


def attention_backward(bounds, qkv, starts, mixed, logsum, grad, index, pairs):
    length = qkv.shape[0]
    operands = (bounds, qkv, starts[None, :], starts[:, None], mixed, logsum, grad)
    shapes = [shape_of((length, pairs * 3 * PAIR), BF16), shape_of((1, pairs * 3 * PAIR), F32)]
    return call(
        backward_kernel,
        "attend_back",
        (1,),
        [
            pl.BlockSpec((length, pairs * 3 * PAIR), lambda g, b: (0, index)),
            whole((1, length)),
            whole((length, 1)),
            whole(mixed.shape),
            whole(logsum.shape),
            pl.BlockSpec((length, pairs * PAIR), lambda g, b: (0, index)),
        ],
        [whole(x.shape) for x in shapes],
        shapes,
        pairs * 2 * length * length * HEAD_DIM * 10,
        operands,
        scratch=[
            pltpu.VMEM((pairs * PAIR, length), BF16),
            pltpu.VMEM((length, pairs * PAIR), F32),
            pltpu.VMEM((length, pairs * PAIR), F32),
        ],
        prefetch=1,
        vmem=24,
    )


MEGA = 1024 * 1024


def whole(shape):
    return pl.BlockSpec(shape, lambda *_: (0,) * len(shape), pipeline_mode=pl.Buffered(1))


def call(kernel, name, grid, in_specs, out_specs, out_shape, flops, operands, scratch=(), prefetch=0, vmem=32):
    moved = sum(x.size * x.dtype.itemsize for x in operands) + sum(
        x.size * x.dtype.itemsize for x in out_shape
    )
    return pl.pallas_call(
        kernel,
        grid_spec=pltpu.PrefetchScalarGridSpec(
            num_scalar_prefetch=prefetch,
            grid=grid,
            in_specs=in_specs,
            out_specs=out_specs,
            scratch_shapes=list(scratch),
        ),
        out_shape=out_shape,
        compiler_params=pltpu.CompilerParams(vmem_limit_bytes=vmem * MEGA),
        cost_estimate=pl.CostEstimate(flops=flops, bytes_accessed=moved, transcendentals=0),
        name=name,
    )(*operands)


def shape_of(shape, dtype):
    return jax.ShapeDtypeStruct(shape, dtype)


def output_kernel(where, *refs):
    (mine_refs, their_refs), (weight_ref, bias_ref, hidden_ref, gain_ref, shift_ref) = (
        (refs[:4], refs[4:6]),
        refs[6:11],
    )
    out_ref, low_ref, normed_ref, factor_ref, mixed_ref = refs[11:]
    h = where[0]
    half = weight_ref.shape[0] // 2
    part = half // 2
    rows = mine_refs[0].shape[0]
    for i in range(2):
        at = slice(i * rows, (i + 1) * rows)
        total = hidden_ref[at, :] + bias_ref[...]
        for cut in range(2):
            mine = pl.ds(pl.multiple_of(h * half + cut * part, 128), part)
            other = pl.ds(pl.multiple_of((1 - h) * half + cut * part, 128), part)
            left, right = mine_refs[2 * cut + i][...], their_refs[cut][at, :]
            mixed_ref[at, mine] = left
            mixed_ref[at, other] = right
            total = total + matmul(left, weight_ref[mine, :]) + matmul(right, weight_ref[other, :])
        out, normed, factor = layer_norm(total, gain_ref[...], shift_ref[...])
        out_ref[at, :] = out
        low_ref[at, :] = out.astype(BF16)
        normed_ref[at, :] = normed
        factor_ref[at, :] = factor


def project_output(h, mine, their, weight, bias, hidden, gain, shift):
    rows, width = hidden.shape
    tok = rows // 2
    part = mine[0].shape[1]
    where = jnp.stack([h, h + 2]).astype(jnp.int32)
    in_specs = [
        pl.BlockSpec((tok, part), lambda g, w: (w[0], 0)),
        pl.BlockSpec((tok, part), lambda g, w: (w[1], 0)),
    ] * 2
    in_specs += [whole((rows, part))] * 2
    in_specs += [whole(weight.shape), whole((1, width)), whole((rows, width)), whole((1, width)), whole((1, width))]
    shapes = [
        shape_of((rows, width), F32),
        shape_of((rows, width), BF16),
        shape_of((rows, width), F32),
        shape_of((rows, 1), F32),
        shape_of((rows, width), BF16),
    ]
    operands = (where, mine[0], mine[0], mine[1], mine[1], their[0], their[1], weight, bias, hidden, gain, shift)
    return call(
        output_kernel,
        "project_output",
        (1,),
        in_specs,
        [whole(x.shape) for x in shapes],
        shapes,
        2 * rows * width * width,
        operands,
        prefetch=1,
    )


def inner_kernel(order, first_ref, *refs):
    pieces, (bias_ref, active_ref, slope_ref, full_ref) = refs[:-4], refs[-4:]
    block = first_ref.shape[1] // 8
    done = 0
    for piece in pieces:
        rows = piece.shape[0]
        at = order[done // block] * block + done % block
        full_ref[pl.ds(pl.multiple_of(at, rows), rows), :] = piece[...]
        done += rows
    rows = first_ref.shape[0]
    step = 256
    for i in range(rows // step):
        at = slice(i * step, (i + 1) * step)
        inner = matmul(first_ref[at, :], full_ref[...]) + bias_ref[...]
        cdf, pdf = normal_cdf_pdf(inner)
        active_ref[0, at, :] = (inner * cdf).astype(BF16)
        slope_ref[0, at, :] = (cdf + inner * pdf).astype(BF16)


def feed_inner(order, first_low, pieces, bias):
    rows, width = first_low.shape
    ff = pieces[0].shape[1]
    tile = ff // 8
    shapes = [
        shape_of((8, rows, tile), BF16),
        shape_of((8, rows, tile), BF16),
        shape_of((width, ff), BF16),
    ]
    return call(
        inner_kernel,
        "feed_inner",
        (8,),
        [whole((rows, width))]
        + [pl.BlockSpec((x.shape[0], tile), lambda t, o: (0, t)) for x in pieces]
        + [pl.BlockSpec((1, tile), lambda t, o: (0, t))],
        [
            pl.BlockSpec((1, rows, tile), lambda t, o: (t, 0, 0)),
            pl.BlockSpec((1, rows, tile), lambda t, o: (t, 0, 0)),
            pl.BlockSpec((width, tile), lambda t, o: (0, t)),
        ],
        shapes,
        2 * rows * width * ff,
        (order, first_low, *pieces, bias),
        prefetch=1,
    )


def outer_kernel(order, active_ref, *refs):
    pieces, refs = refs[:-11], refs[-11:]
    bias_ref, first_ref, up_ref, gain_ref, shift_ref = refs[:5]
    full_ref, out_ref, grad_ref, low_ref, sums_ref, acc_ref = refs[5:]
    t = pl.program_id(0)
    block, tile = full_ref.shape[1:]
    done = 0
    for piece in pieces:
        rows = piece.shape[0]
        full_ref[order[done // block], done % block : done % block + rows] = piece[...]
        done += rows
    total = matmul(active_ref[0], full_ref[0])
    for k in range(1, 8):
        total = total + matmul(active_ref[k], full_ref[k])
    acc_ref[:, pl.ds(pl.multiple_of(t * tile, tile), tile)] = total

    @pl.when(t == pl.num_programs(0) - 1)
    def _():
        rows, width = acc_ref.shape
        step = 128
        gain, shift, bias = gain_ref[...], shift_ref[...], bias_ref[...]
        sums = [jnp.zeros((1, width), F32)] * 3
        for i in range(rows // step):
            at = slice(i * step, (i + 1) * step)
            out, normed, factor = layer_norm(first_ref[at, :] + acc_ref[at, :] + bias, gain, shift)
            out_ref[at, :] = out.astype(BF16)
            up = up_ref[at, :].astype(F32)
            grad = norm_back(up, normed, factor, gain)
            low = grad.astype(BF16)
            grad_ref[at, :] = grad
            low_ref[at, :] = low
            for j, item in enumerate((up * normed, up, low.astype(F32))):
                sums[j] = sums[j] + jnp.sum(item, axis=0, keepdims=True)
        sums_ref[...] = jnp.concatenate(sums + [jnp.zeros((5, width), F32)], axis=0)


def feed_outer(order, active, pieces, bias, first_out, upstream, gain, shift):
    rows, width = first_out.shape
    block = sum(x.shape[0] for x in pieces) // 8
    tile = width // 4
    shapes = [
        shape_of((8, block, width), BF16),
        shape_of((rows, width), BF16),
        shape_of((rows, width), F32),
        shape_of((rows, width), BF16),
        shape_of((8, width), F32),
    ]
    row = whole((1, width))
    return call(
        outer_kernel,
        "feed_outer",
        (4,),
        [whole(active.shape)]
        + [pl.BlockSpec((x.shape[0], tile), lambda t, o: (0, t)) for x in pieces]
        + [row, whole((rows, width)), whole((rows, width)), row, row],
        [pl.BlockSpec((8, block, tile), lambda t, o: (0, 0, t))] + [whole(x.shape) for x in shapes[1:]],
        shapes,
        2 * rows * width * block * 8,
        (order, active, *pieces, bias, first_out, upstream, gain, shift),
        scratch=[pltpu.VMEM((rows, width), F32)],
        prefetch=1,
    )


def gelu_back_kernel(grad_ref, weight_ref, slope_ref, out_ref, sums_ref):
    grad = contract_cols(grad_ref[...], weight_ref[0])
    low = (grad * slope_ref[0].astype(F32)).astype(BF16)
    out_ref[0] = low
    sums_ref[0] = jnp.sum(low.astype(F32), axis=0, keepdims=True)


def gelu_back(grad_outer, full_outer, slope):
    rows, width = grad_outer.shape
    _, block, _ = full_outer.shape
    tile = slope.shape[2]
    shapes = [shape_of(slope.shape, BF16), shape_of((8, 1, tile), F32)]
    return call(
        gelu_back_kernel,
        "gelu_back",
        (8,),
        [
            whole((rows, width)),
            pl.BlockSpec((1, block, width), lambda t: (t, 0, 0)),
            pl.BlockSpec((1, rows, tile), lambda t: (t, 0, 0)),
        ],
        [
            pl.BlockSpec((1, rows, tile), lambda t: (t, 0, 0)),
            pl.BlockSpec((1, 1, tile), lambda t: (t, 0, 0)),
        ],
        shapes,
        2 * rows * width * tile * 8,
        (grad_outer, full_outer, slope),
    )


def first_back_kernel(grad_ref, weight_ref, second_ref, normed_ref, factor_ref, gain_ref, output_ref, *refs):
    out_ref, low_ref, mixed_ref, sums_ref, acc_ref = refs
    t = pl.program_id(0)
    part = contract_cols(grad_ref[0], weight_ref[...])

    @pl.when(t == 0)
    def _():
        acc_ref[...] = second_ref[...] + part

    @pl.when(t > 0)
    def _():
        acc_ref[...] += part

    @pl.when(t == pl.num_programs(0) - 1)
    def _():
        rows, width = acc_ref.shape
        step = 128
        gain = gain_ref[...]
        sums = [jnp.zeros((1, width), F32)] * 3
        for i in range(rows // step):
            at = slice(i * step, (i + 1) * step)
            up, normed = acc_ref[at, :], normed_ref[at, :]
            grad = norm_back(up, normed, factor_ref[at, :], gain)
            low = grad.astype(BF16)
            out_ref[at, :] = grad
            low_ref[at, :] = low
            for j, item in enumerate((up * normed, up, low.astype(F32))):
                sums[j] = sums[j] + jnp.sum(item, axis=0, keepdims=True)
        sums_ref[...] = jnp.concatenate(sums + [jnp.zeros((5, width), F32)], axis=0)
        mixed_ref[...] = contract_cols(low_ref[...], output_ref[...]).astype(BF16)


def first_back(grad_inner, full_inner, grad_second, normed, factor, gain, full_output):
    rows, width = grad_second.shape
    tile = grad_inner.shape[2]
    shapes = [
        shape_of((rows, width), F32),
        shape_of((rows, width), BF16),
        shape_of((rows, width), BF16),
        shape_of((8, width), F32),
    ]
    return call(
        first_back_kernel,
        "first_back",
        (8,),
        [
            pl.BlockSpec((1, rows, tile), lambda t: (t, 0, 0)),
            pl.BlockSpec((width, tile), lambda t: (0, t)),
            whole((rows, width)),
            whole((rows, width)),
            whole((rows, 1)),
            whole((1, width)),
            whole(full_output.shape),
        ],
        [whole(x.shape) for x in shapes],
        shapes,
        2 * rows * width * (tile * 8 + width),
        (grad_inner, full_inner, grad_second, normed, factor, gain, full_output),
        scratch=[pltpu.VMEM((rows, width), F32)],
    )


def block_grad_kernel(order, left_ref, right_ref, out_ref):
    out_ref[0] = contract_rows(left_ref[0], right_ref[...]).astype(BF16)


def block_grad(order, left, right):
    rows, width = right.shape
    block = left.shape[2]
    shapes = [shape_of((4, block, width), BF16)]
    return call(
        block_grad_kernel,
        "block_grad",
        (4,),
        [pl.BlockSpec((1, rows, block), lambda i, o: (o[i], 0, 0)), whole((rows, width))],
        [pl.BlockSpec((1, block, width), lambda i, o: (i, 0, 0))],
        shapes,
        2 * rows * width * block * 4,
        (order, left, right),
        prefetch=1,
    )[0]


def turn_strips(order, left_ref, turned_ref):
    block = turned_ref.shape[0] // 4
    for i in range(4):
        strip = left_ref[:, pl.ds(pl.multiple_of(order[i] * block, block), block)]
        turned_ref[i * block : (i + 1) * block, : strip.shape[0]] = strip.T


def tile_grad_kernel(order, left_ref, right_ref, out_ref, turned_ref):
    block = out_ref.shape[1]

    @pl.when(pl.program_id(0) == 0)
    def _():
        turn_strips(order, left_ref, turned_ref)

    out = matmul(turned_ref[...], right_ref[0]).astype(BF16)
    for i in range(4):
        out_ref[i] = out[i * block : (i + 1) * block]


def tile_grad(order, left, right):
    rows, width = left.shape
    block = width // 8
    tiles, _, tile = right.shape
    shapes = [shape_of((4, block, tiles * tile), BF16)]
    return call(
        tile_grad_kernel,
        "tile_grad",
        (tiles,),
        [whole((rows, width)), pl.BlockSpec((1, rows, tile), lambda t, o: (t, 0, 0))],
        [pl.BlockSpec((4, block, tile), lambda t, o: (0, 0, t))],
        shapes,
        2 * rows * block * 4 * tiles * tile,
        (order, left, right),
        scratch=[pltpu.VMEM((4 * block, rows), BF16)],
        prefetch=1,
        vmem=12,
    )[0]


def strip_grad_kernel(
    parts, order, left_ref, first_ref, second_ref, extra_ref, low_ref, third_ref, out_ref, turned_ref
):
    t = pl.program_id(0)
    last = parts[0] + parts[1]
    block = turned_ref.shape[0] // 4

    @pl.when(t == 0)
    def _():
        turn_strips(order, left_ref, turned_ref)

    @pl.when(t == last)
    def _():
        turn_strips(order, low_ref, turned_ref)

    def put(right, extra):
        out = matmul(turned_ref[:, : right.shape[0]], right).astype(BF16)
        for i in range(4):
            out_ref[i, :block] = out[i * block : (i + 1) * block]
            out_ref[i, block:] = extra_ref[order[i]] if extra else jnp.zeros_like(out_ref[i, block:])

    @pl.when(t < parts[0])
    def _():
        put(first_ref[...], True)

    @pl.when((t >= parts[0]) & (t < last))
    def _():
        put(second_ref[...], True)

    @pl.when(t >= last)
    def _():
        put(third_ref[...], False)


def strip_grad(order, left, first, second, extra, low, third):
    rows, width = left.shape
    block = width // 8
    tile = 512 if first.shape[1] % 512 == 0 else 256
    parts = [x.shape[1] // tile for x in (first, second, third)]
    total = sum(parts)
    tall = block + extra.shape[1]
    shapes = [shape_of((4, tall, total * tile), BF16)]
    return call(
        partial(strip_grad_kernel, parts),
        "strip_grad",
        (total,),
        [
            whole((rows, width)),
            pl.BlockSpec((rows, tile), lambda t, o: (0, jnp.minimum(t, parts[0] - 1))),
            pl.BlockSpec((rows, tile), lambda t, o: (0, jnp.clip(t - parts[0], 0, parts[1] - 1))),
            pl.BlockSpec(
                (8, extra.shape[1], tile), lambda t, o: (0, 0, jnp.minimum(t, parts[0] + parts[1] - 1))
            ),
            whole(low.shape),
            pl.BlockSpec((low.shape[0], tile), lambda t, o: (0, jnp.maximum(t - parts[0] - parts[1], 0))),
        ],
        [pl.BlockSpec((4, tall, tile), lambda t, o: (0, 0, t))],
        shapes,
        2 * rows * block * 4 * total * tile,
        (order, left, first, second, extra, low, third),
        scratch=[pltpu.VMEM((4 * block, rows), BF16)],
        prefetch=1,
        vmem=20,
    )[0]


def hidden_back_kernel(where, *refs):
    lefts, weight_ref, rest = refs[:2], refs[2], refs[3:]
    part = lefts[0].shape[1]
    total = contract_cols(lefts[0][...], weight_ref[:, :part]) + contract_cols(lefts[1][...], weight_ref[:, part:])
    if len(rest) == 2:
        total = total + rest[0][...]
    rest[-1][...] = total.astype(rest[-1].dtype)


def hidden_back(parity, grads, weight, base, tok):
    width = weight.shape[0]
    part = grads[0].shape[1]
    where = jnp.stack([parity, parity + 2]).astype(jnp.int32)
    row = pl.BlockSpec((tok, width), lambda i, w: (i, 0))
    extra = () if base is None else (base,)
    shapes = [shape_of((2 * tok, width), BF16 if base is None else F32)]
    return call(
        hidden_back_kernel,
        "hidden_back",
        (2,),
        [pl.BlockSpec((tok, part), lambda i, w: (w[i], 0))] * 2 + [whole(weight.shape)] + [row] * len(extra),
        [row],
        shapes,
        2 * 2 * tok * width * part * 2,
        (where, *grads, weight, *extra),
        prefetch=1,
    )[0]


def after(x, *deps):
    return lax.optimization_barrier((x, deps))[0]


class Steps:
    def __init__(self):
        self.last = ()

    def __call__(self, fn, *args):
        args, _ = lax.optimization_barrier((args, self.last))
        out = fn(*args)
        self.last = out
        return out


def flip(x, axis, size, bit):
    return lax.ppermute(x, axis, [(i, i ^ bit) for i in range(size)])


def swap(x, bit):
    return flip(x, "fsdp", 8, bit)


def widen(*items):
    return sum(item.astype(F32) for item in items)


class CubeSum:
    def __init__(self, send, width, x_columns):
        self.got = swap(send, 1)
        self.parts = []
        if x_columns > 0:
            self.parts.append((slice(0, x_columns), 1, 2, 2, 4))
        if x_columns < width:
            self.parts.append((slice(x_columns, width), 2, 1, 4, 2))

    def first_hop(self, steps, keep):
        def add(keep, got):
            return [
                jnp.stack([widen(keep[i, :, cols], got[i, :, cols]).astype(BF16) for i in (away, 3)])
                for cols, _, away, _, _ in self.parts
            ]

        self.keep = keep
        there = steps(add, keep, self.got)
        self.back = [swap(x, part[3]) for x, part in zip(there, self.parts)]

    def second_hop(self, steps):
        def add(keep, got, back):
            here, there = [], []
            for (cols, near, _, _, _), b in zip(self.parts, back):
                here.append(widen(keep[0, :, cols], got[0, :, cols], b[0]))
                there.append(widen(keep[near, :, cols], got[near, :, cols], b[1]).astype(BF16))
            return here, there

        self.here, there = steps(add, self.keep, self.got, self.back)
        self.last = [swap(x, part[4]) for x, part in zip(there, self.parts)]

    def result(self, steps):
        def add(here, last):
            sums = [widen(x, y).astype(BF16) for x, y in zip(here, last)]
            return sums[0] if len(sums) == 1 else jnp.concatenate(sums, axis=1)

        return steps(add, self.here, self.last)


class PlainSum:
    def __init__(self, product, extra=()):
        self.product, self.extra = product.astype(BF16), extra

    def first_hop(self, steps, keep):
        pass

    def second_hop(self, steps):
        pass

    def result(self, steps):
        share = lax.psum_scatter(self.product, "fsdp", scatter_dimension=0, tiled=True)
        lines = [lax.psum_scatter(x, "fsdp", scatter_dimension=0, tiled=False) for x in self.extra]
        return (share, *lines) if lines else share


def pair_pack(parts):
    rows = parts[0].shape[0]
    return jnp.stack([p.reshape(rows, -1, PAIR) for p in parts], axis=2).reshape(rows, -1)


def pair_unpack(packed):
    rows = packed.shape[0]
    cut = packed.reshape(rows, -1, 3, PAIR)
    return [cut[:, :, i].reshape(rows, -1) for i in range(3)]


def body(
    fsdp,
    stream_in,
    timestep,
    doc_start,
    query_weight,
    key_weight,
    value_weight,
    output_weight,
    query_bias,
    value_bias,
    output_bias,
    first_gain,
    first_shift,
    inner_weight,
    inner_bias,
    outer_weight,
    outer_bias,
    second_gain,
    second_shift,
    cotangent,
):
    cube = fsdp == 8
    steps = Steps()
    me = lax.axis_index("fsdp")
    streams, tok, width = stream_in.shape
    own_rows = query_weight.shape[0]
    half = width // 2
    ff = inner_weight.shape[1]
    length = 4 * tok
    z = lax.axis_index("seq")
    h, s = z % 2, z // 2

    def flip_h(x):
        return flip(x, "seq", 4, 1)

    def flip_s(x):
        return flip(x, "seq", 4, 2)

    def in_order(mine, other):
        return jnp.where(s == 0, jnp.concatenate([mine, other]), jnp.concatenate([other, mine]))

    def pick(x, index, axis=0):
        return lax.dynamic_index_in_dim(x, index, axis, keepdims=False)

    head_cols = [lax.dynamic_slice_in_dim(w, h * half, half, 1) for w in (query_weight, key_weight, value_weight)]
    small = jnp.concatenate(
        [
            query_bias,
            value_bias,
            output_bias,
            first_gain,
            first_shift,
            outer_bias,
            second_gain,
            second_shift,
            inner_bias,
        ]
    )
    packed = pair_pack(head_cols)
    own = pick(stream_in, s)
    if cube:
        owners = [me ^ m for m in range(8)]
        packed = jnp.concatenate([packed, jnp.broadcast_to(small[None, :], (16, small.shape[0]))])
        gathered = lax.all_gather(packed, "fsdp", axis=0, tiled=False)
        full_qkv = gathered[:, :own_rows].reshape(-1, packed.shape[1])
        small_rows = gathered[:, own_rows]
        output_w = after(output_weight, gathered)
        full_output = lax.all_gather(output_w, "fsdp", axis=0, tiled=True)
        inner_w = after(inner_weight, packed)
        ix, iy = swap(inner_w, 2), swap(inner_w, 4)
        distant = flip_s(pick(stream_in, 1 - s))
        beside = flip_h(own)
        cut = own_rows // 2
        top, bottom, distant, beside, inner_w, outer_w = steps(
            lambda x, y, *rest: (x[:cut], y[cut:], *rest), ix, iy, distant, beside, inner_w, outer_weight
        )
        corner = flip_h(distant)
        jy, jx = swap(top, 4), swap(bottom, 2)
        ic = swap(inner_w, 1)
    else:
        owners = list(range(8))

        def gather(piece):
            full = lax.all_gather(piece, "fsdp", axis=0, tiled=True)
            return list(full.reshape(8, full.shape[0] // 8, full.shape[1]))

        distant, beside = flip_s(pick(stream_in, 1 - s)), flip_h(own)
        corner = flip_h(distant)
        full_qkv = lax.all_gather(packed, "fsdp", axis=0, tiled=True)
        full_output = lax.all_gather(output_weight, "fsdp", axis=0, tiled=True)
        inner_pieces, outer_pieces = gather(inner_weight), gather(outer_weight)
        small_rows = lax.all_gather(small, "fsdp", axis=0, tiled=False)
    order = jnp.stack([jnp.asarray(o, jnp.int32) for o in owners])
    small_rows = small_rows.astype(F32)
    qbias, vbias, obias, gain_one, shift_one, obias_two, gain_two, shift_two = [
        small_rows[:, i * own_rows : (i + 1) * own_rows].reshape(1, -1) for i in range(8)
    ]
    ibias = small_rows[:, 8 * own_rows :].reshape(1, -1)

    ts = pick(timestep, s).astype(F32)

    def place(own, beside, distant, corner):
        stream = jnp.zeros((length, width), BF16)
        for mask, block in ((0, own), (1, beside), (2, distant), (3, corner)):
            stream = lax.dynamic_update_slice(stream, block, ((z ^ mask) * tok, 0))
        stream_low = (stream.astype(F32) + ts).astype(BF16)
        return stream_low, in_order(own, distant).astype(F32) + ts

    if cube:
        own, ic, ix, corner, outer_w = steps(lambda *x: x, own, ic, ix, corner, outer_w)
        ox, oy = swap(outer_w, 2), swap(outer_w, 4)
        ixc = swap(ix, 1)
    stream_low, hidden = steps(place, own, beside, distant, corner)
    starts = pick(doc_start, s)
    bounds = block_bounds(starts)

    qb = lax.dynamic_slice_in_dim(qbias, h * half, half, 1)
    vb = lax.dynamic_slice_in_dim(vbias, h * half, half, 1)
    bias_row = pair_pack([qb, jnp.zeros_like(qb), vb])
    scale_row = pair_pack([jnp.full((1, half), 0.125, F32), jnp.ones((1, half), F32), jnp.ones((1, half), F32)])
    if cube:
        stream_low, ixc, iy = steps(lambda *x: x, stream_low, ixc, iy)
        iyc = swap(iy, 1)
    qkv = steps(
        lambda x, w, b: ((matmul(x, w) + b) * scale_row).astype(BF16), stream_low, full_qkv, bias_row
    )
    pairs = half // PAIR
    part = pairs // 2

    def rows_of(x, parity):
        cut = x.reshape(2, 2, tok, x.shape[1])
        return pick(cut, parity, 1).reshape(2 * tok, x.shape[1])

    def attend(index, qkv):
        return attention_forward(bounds, qkv, starts, index, part)

    if cube:
        jy, jx, iyc, qkv = steps(lambda *x: x, jy, jx, iyc, qkv)
        jyc, jxc = swap(jy, 1), swap(jx, 1)
    mixed_a, logsum_a = steps(partial(attend, 0), qkv)
    out_a, jyc, jxc = steps(
        lambda x, *rest: (rows_of(x, 1 - h), *rest), mixed_a, *((jyc, jxc) if cube else (0.0, 0.0))
    )
    their_a = flip_h(out_a)
    mixed_b, logsum_b = steps(partial(attend, 1), qkv)
    cotangent_out = pick(cotangent, 1 - s)
    if cube:
        inner_pieces = [inner_w, ic, ix, ixc, iy, iyc, jy, jx, jyc, jxc]
        cut = outer_weight.shape[0] // 2
        top, bottom, ox, oy = steps(lambda x, y: (x[:cut], y[cut:], x, y), ox, oy)
        jy, jx = swap(top, 4), swap(bottom, 2)
    out_b, their_a, cotangent_out = steps(lambda x, *rest: (rows_of(x, 1 - h), *rest), mixed_b, their_a, cotangent_out)
    their_b = flip_h(out_b)
    if cube:
        oxc = swap(ox, 1)
    moved = flip_s(cotangent_out)
    first_out, first_low, first_normed, first_factor, mixed = steps(
        partial(project_output, h),
        (mixed_a, mixed_b),
        (their_a, their_b),
        full_output,
        obias,
        hidden,
        gain_one,
        shift_one,
    )

    if cube:
        jy, jx, oxc, oy, outer_w, first_low = steps(lambda *x: x, jy, jx, oxc, oy, outer_w, first_low)
        oc, oyc, jyc, jxc = swap(outer_w, 1), swap(oy, 1), swap(jy, 1), swap(jx, 1)
        outer_pieces = [outer_w, oc, ox, oxc, oy, oyc, jy, jx, jyc, jxc]
    active, slope, full_inner = steps(partial(feed_inner, order), first_low, inner_pieces, ibias)
    upstream = in_order(pick(cotangent, s), moved)
    full_outer, result, grad_second_in, grad_outer, second_sums = steps(
        partial(feed_outer, order), active, outer_pieces, obias_two, first_out, upstream, gain_two, shift_two
    )
    result = result.reshape(2, tok, width)
    result_own, result_out = steps(lambda x: (pick(x, s), pick(x, 1 - s)), result)
    result_away = flip_s(result_out)

    if cube:
        send_order = jnp.stack([me ^ m for m in (1, 5, 3, 7)]).astype(jnp.int32)
        keep_order = jnp.stack([me ^ m for m in (0, 4, 2, 6)]).astype(jnp.int32)

    if cube:
        outer_send = steps(partial(block_grad, send_order), active, grad_outer)
        outer_sum = CubeSum(outer_send, width, half)
        outer_keep = steps(partial(block_grad, keep_order), active, grad_outer)
    else:
        outer_keep = ()
        outer_sum = PlainSum(contract_rows(active.transpose(1, 0, 2).reshape(2 * tok, -1), grad_outer))
    grad_inner, inner_sums = steps(gelu_back, grad_outer, full_outer, slope)
    outer_sum.first_hop(steps, outer_keep)
    if cube:
        inner_send = steps(partial(tile_grad, send_order), first_low, grad_inner)
        inner_sum = CubeSum(inner_send, ff, ff // 2)
    else:
        inner_sum = PlainSum(contract_rows(first_low, grad_inner.transpose(1, 0, 2).reshape(2 * tok, -1)))

    def first_step(*args):
        grad_first_in, grad_attended, grad_mixed, sums = first_back(*args)
        wide = half // 2
        theirs = lax.dynamic_slice_in_dim(grad_mixed, (1 - h) * half, half, 1)
        mine = lax.dynamic_slice_in_dim(grad_mixed, h * half, half, 1)
        return grad_first_in, grad_attended, sums, theirs, mine

    grad_first_in, grad_attended, first_sums, theirs, mine = steps(
        first_step, grad_inner, full_inner, grad_second_in, first_normed, first_factor, gain_one, full_output
    )
    received = flip_h(theirs)
    inner_keep = steps(partial(tile_grad, keep_order), first_low, grad_inner) if cube else ()
    result_away = steps(lambda x: x, result_away)
    outer_sum.second_hop(steps)

    def to_heads(mine, received):
        mine = mine.reshape(2, 1, tok, half)
        received = received.reshape(2, 1, tok, half)
        return jnp.where(
            h == 0, jnp.concatenate([mine, received], axis=1), jnp.concatenate([received, mine], axis=1)
        ).reshape(length, half)

    grad_heads = steps(to_heads, mine, received)

    def seq_sum(share):
        def halve(x, bit):
            pair = x.reshape(2, x.shape[0] // 2, -1)
            return pick(pair, bit), pick(pair, 1 - bit)

        def join(mine, other, bit):
            return jnp.where(bit == 0, jnp.concatenate([mine, other]), jnp.concatenate([other, mine]))

        mine, out = steps(lambda x: halve(x, h), share)
        back = flip_h(out)
        yield
        def quarter(m, b):
            mine, out = halve(widen(m, b), s)
            return mine, out.astype(BF16)

        mine, out = steps(quarter, mine, back)
        back = flip_s(out)
        yield
        mine = steps(lambda m, b: widen(m, b).astype(BF16), mine, back)
        back = flip_s(mine)
        yield
        mine = steps(lambda m, b: join(m, b, s), mine, back)
        back = flip_h(mine)
        yield
        yield steps(lambda m, b: join(m, b, h).astype(F32), mine, back)

    def attend_back(index, qkv, mixed, logsum, grad):
        return attention_backward(bounds, qkv, starts, mixed, logsum, grad, index, part)

    grad_a, sums_a = steps(partial(attend_back, 0), qkv, mixed_a, logsum_a, grad_heads)
    inner_sum.first_hop(steps, inner_keep)
    outer_share = outer_sum.result(steps)
    outer_steps = seq_sum(outer_share)
    next(outer_steps)
    grad_b, sums_b = steps(partial(attend_back, 1), qkv, mixed_b, logsum_b, grad_heads)
    next(outer_steps)
    away = flip_h(
        steps(lambda a, b, w: hidden_back(1 - h, (a, b), w, None, tok), grad_a, grad_b, full_qkv)
    )
    zero_half = jnp.zeros((half,), F32)

    def spread(v):
        v = v.reshape(-1)
        return jnp.where(h == 0, jnp.concatenate([v, zero_half]), jnp.concatenate([zero_half, v]))

    grad_q_cols, _, grad_v_cols = pair_unpack(jnp.concatenate([sums_a, sums_b], axis=1))
    vectors = jnp.concatenate(
        [
            v.reshape(fsdp, -1)
            for v in (
                spread(grad_q_cols),
                spread(grad_v_cols),
                first_sums[2],
                first_sums[0],
                first_sums[1],
                second_sums[2],
                second_sums[0],
                second_sums[1],
                inner_sums,
            )
        ],
        axis=1,
    ).astype(BF16)
    if cube:
        lines = vectors.reshape(fsdp, 1, -1)
        lines = jnp.concatenate([lines, jnp.zeros((fsdp, 15, lines.shape[2]), BF16)], axis=1)
        qkv_operands = (stream_low, grad_a, grad_b, lines, mixed, grad_attended)
        qkv_send = steps(partial(strip_grad, send_order), *qkv_operands)
        qkv_sum = CubeSum(qkv_send, qkv_send.shape[2], qkv_send.shape[2] // 2)
        inner_sum.second_hop(steps)
        next(outer_steps)
        qkv_keep = steps(partial(strip_grad, keep_order), *qkv_operands)
    else:
        qkv_keep = ()
        both = jnp.concatenate([grad_a, grad_b], axis=1)
        both = jnp.concatenate([contract_rows(stream_low, both), contract_rows(mixed, grad_attended)], axis=1)
        qkv_sum = PlainSum(both, (vectors,))
        next(outer_steps)
    kept = steps(lambda a, b, w, g: hidden_back(h, (a, b), w, g, tok), grad_a, grad_b, full_qkv, grad_first_in)

    def split_rows(kept, away):
        grad_hidden = (kept + away.astype(F32)).reshape(2, tok, width)
        return pick(grad_hidden, s), pick(grad_hidden, 1 - s).astype(BF16)

    inner_share = inner_sum.result(steps)
    inner_steps = seq_sum(inner_share)
    next(inner_steps)
    qkv_sum.first_hop(steps, qkv_keep)
    grad_own, grad_out = steps(split_rows, kept, away)
    grad_away = flip_s(grad_out)
    next(inner_steps)
    next(outer_steps)
    qkv_sum.second_hop(steps)
    next(inner_steps)

    layer_out = jnp.where(s == 0, jnp.stack([result_own, result_away]), jnp.stack([result_away, result_own]))

    def swap_heads(mine, other):
        return jnp.where(h == 0, jnp.concatenate([mine, other], axis=1), jnp.concatenate([other, mine], axis=1))

    qkv_share = qkv_sum.result(steps)
    qkv_share, extra = qkv_share if not cube else (qkv_share, None)
    qkv_back = flip_s(qkv_share)
    outer_grad = next(outer_steps)
    next(inner_steps)
    grad_own, grad_away = steps(lambda x, y: (x, y.astype(F32)), grad_own, grad_away)
    input_grad = jnp.where(s == 0, jnp.stack([grad_own, grad_away]), jnp.stack([grad_away, grad_own]))
    qkv_mine = steps(lambda x, y: widen(x, y).astype(BF16), qkv_share, qkv_back)
    qkv_other = flip_h(qkv_mine)
    inner_grad = next(inner_steps)
    three = 3 * half
    output_grad = widen(qkv_mine[:own_rows, three:], qkv_other[:own_rows, three:])
    if cube:
        sums = widen(qkv_mine[own_rows, :three], qkv_other[own_rows, :three])
    else:
        sums = lax.psum(extra.astype(F32), "seq")
    qkv_grads = [
        swap_heads(mine, other).astype(F32)
        for mine, other in zip(
            pair_unpack(qkv_mine[:own_rows, :three]), pair_unpack(qkv_other[:own_rows, :three])
        )
    ]
    cut = [sums[i * own_rows : (i + 1) * own_rows] for i in range(8)]
    return (
        layer_out,
        input_grad,
        qkv_grads[0],
        qkv_grads[1],
        qkv_grads[2],
        output_grad,
        cut[0],
        cut[1],
        cut[2],
        cut[3],
        cut[4],
        inner_grad,
        sums[8 * own_rows :],
        outer_grad,
        cut[5],
        cut[6],
        cut[7],
    )


def solution(mesh):
    rows = P("fsdp", "seq", None)
    mat = P("fsdp", None)
    vec = P("fsdp")
    in_specs = (rows, mat, mat) + (mat,) * 4 + (vec,) * 5 + (mat, vec, mat, vec, vec, vec) + (rows,)
    out_specs = (rows, rows) + (mat,) * 4 + (vec,) * 5 + (mat, vec, mat, vec, vec, vec)
    return jax.shard_map(
        partial(body, mesh.shape["fsdp"]), mesh=mesh, in_specs=in_specs, out_specs=out_specs, check_vma=False
    )
```

```python
from functools import partial

import jax
import jax.numpy as jnp
from jax import lax
from jax.experimental import pallas as pl
from jax.experimental.pallas import tpu as pltpu
from jax.sharding import PartitionSpec as P

HEAD_DIM = 64
PAIR = 2 * HEAD_DIM
BLOCK = 256
F32 = jnp.float32
BF16 = jnp.bfloat16

PHI_POLY = (
    0.11962928975633808,
    0.12075411058236112,
    0.09991242675653945,
    0.12856547821204567,
    -0.053691543682108024,
    0.20636272322745108,
    -0.15720876784307727,
    0.03567620985200702,
)


def normal_cdf_pdf(z):
    u = jnp.abs(z)
    bell = jnp.exp(-0.5 * u * u)
    t = 1.0 / (1.0 + 0.3 * u)
    poly = jnp.full_like(t, PHI_POLY[-1])
    for coef in PHI_POLY[-2::-1]:
        poly = poly * t + coef
    tail = bell * (t * poly)
    return jnp.where(z < 0, tail, 1.0 - tail), bell * 0.3989422804014327


def layer_norm(rows, gain, shift):
    centred = rows - jnp.mean(rows, axis=-1, keepdims=True)
    factor = lax.rsqrt(jnp.mean(centred * centred, axis=-1, keepdims=True) + 1e-05)
    normed = centred * factor
    return (normed * gain + shift, normed, factor)


def norm_back(upstream, normed, factor, gain):
    scaled = upstream * gain
    return factor * (
        scaled
        - jnp.mean(scaled, axis=-1, keepdims=True)
        - normed * jnp.mean(scaled * normed, axis=-1, keepdims=True)
    )


def matmul(left, right):
    return jnp.dot(left, right, preferred_element_type=F32)


def contract_rows(left, right):
    return lax.dot_general(left, right, (((0,), (0,)), ((), ())), preferred_element_type=F32)


def contract_cols(left, right):
    return lax.dot_general(left, right, (((1,), (1,)), ((), ())), preferred_element_type=F32)


def column_sum(rows):
    return jnp.sum(rows.astype(F32), axis=0)


def half_rows(block, head):
    zero = jnp.zeros((HEAD_DIM, block.shape[1]), block.dtype)
    part = block[head * HEAD_DIM : (head + 1) * HEAD_DIM]
    return jnp.concatenate([part, zero] if head == 0 else [zero, part], axis=0)


def columns(pair, kind):
    return slice((3 * pair + kind) * PAIR, (3 * pair + kind + 1) * PAIR)


def head_rows(n):
    return slice(n * HEAD_DIM, (n + 1) * HEAD_DIM)


def forward_kernel(bounds, qkv_ref, row_ref, col_ref, mixed_ref, logsum_ref, vt_ref):
    length = qkv_ref.shape[0]
    pairs = logsum_ref.shape[0]
    heads = [(p, head) for p in range(pairs) for head in range(2)]
    q_t = [qkv_ref[:, columns(p, 0)].T for p in range(pairs)]
    for p in range(pairs):
        vt_ref[p * PAIR : (p + 1) * PAIR, :] = qkv_ref[:, columns(p, 2)].T
    for i in range(length // BLOCK):
        at = slice(i * BLOCK, (i + 1) * BLOCK)
        row = row_ref[:, at]
        halves = [half_rows(q_t[p][:, at], head) for p, head in heads]

        def step(j, carry):
            span = pl.ds(pl.multiple_of(j * BLOCK, BLOCK), BLOCK)
            same = col_ref[span, :] == row
            products = [matmul(qkv_ref[span, columns(p, 1)], halves[2 * p + head]) for p, head in heads]
            new = []
            for n, (peak, total, mix) in enumerate(carry):
                scores = jnp.where(same, products[n], -1e30)
                top = jnp.maximum(peak, jnp.max(scores, axis=0, keepdims=True))
                weights = jnp.exp(scores - top)
                decay = jnp.exp(peak - top)
                total = total * decay + jnp.sum(weights, axis=0, keepdims=True)
                mix = mix * decay + matmul(vt_ref[head_rows(n), span], weights.astype(BF16))
                new.append((top, total, mix))
            return tuple(new)

        first = (
            jnp.full((1, BLOCK), -1e30, F32),
            jnp.zeros((1, BLOCK), F32),
            jnp.zeros((HEAD_DIM, BLOCK), F32),
        )
        done = lax.fori_loop(bounds[i, 0], bounds[i, 1], step, (first,) * len(heads))
        for p in range(pairs):
            mixes = [mix / total for _, total, mix in done[2 * p : 2 * p + 2]]
            mixed_ref[at, p * PAIR : (p + 1) * PAIR] = jnp.concatenate(mixes, axis=0).T.astype(BF16)
        for n, (p, head) in enumerate(heads):
            logsum_ref[p, head : head + 1, at] = done[n][0] + jnp.log(done[n][1])


def backward_kernel(
    bounds, qkv_ref, row_ref, col_ref, mixed_ref, logsum_ref, grad_ref, out_ref, sums_ref, kt_ref, dk_ref, dv_ref
):
    length = qkv_ref.shape[0]
    pairs = logsum_ref.shape[0]
    heads = [(p, head) for p in range(pairs) for head in range(2)]
    dk_ref[...] = jnp.zeros_like(dk_ref)
    dv_ref[...] = jnp.zeros_like(dv_ref)
    q_t, g_t, delta = [], [], []
    for p in range(pairs):
        lanes = slice(p * PAIR, (p + 1) * PAIR)
        q_t.append(qkv_ref[:, columns(p, 0)].T)
        g_t.append(grad_ref[:, lanes].T)
        kt_ref[lanes, :] = qkv_ref[:, columns(p, 1)].T
        product_t = (grad_ref[:, lanes].astype(F32) * mixed_ref[:, lanes].astype(F32)).T
        for head in range(2):
            delta.append(jnp.sum(product_t[head_rows(head)], axis=0, keepdims=True))
    lane = lax.broadcasted_iota(jnp.int32, (BLOCK, PAIR), 1)
    zero = jnp.zeros((BLOCK, PAIR), BF16)

    def split(x):
        return jnp.concatenate(
            [jnp.where(lane < HEAD_DIM, x, zero), jnp.where(lane >= HEAD_DIM, x, zero)], axis=0
        )

    for i in range(length // BLOCK):
        at = slice(i * BLOCK, (i + 1) * BLOCK)
        row = row_ref[:, at]
        q_halves = [half_rows(q_t[p][:, at], head) for p, head in heads]
        g_halves = [half_rows(g_t[p][:, at], head) for p, head in heads]
        q_split = [split(qkv_ref[at, columns(p, 0)]) for p in range(pairs)]
        g_split = [split(grad_ref[at, p * PAIR : (p + 1) * PAIR]) for p in range(pairs)]
        logsum = [logsum_ref[p, head : head + 1, at] for p, head in heads]

        def step(j, carry):
            span = pl.ds(pl.multiple_of(j * BLOCK, BLOCK), BLOCK)
            same = col_ref[span, :] == row
            scores = [matmul(qkv_ref[span, columns(p, 1)], q_halves[2 * p + head]) for p, head in heads]
            grad_probs = [matmul(qkv_ref[span, columns(p, 2)], g_halves[2 * p + head]) for p, head in heads]
            new = []
            for p in range(pairs):
                probs_low, grad_low = [], []
                for n in (2 * p, 2 * p + 1):
                    probs = jnp.exp(jnp.where(same, scores[n], -1e30) - logsum[n])
                    grad_low.append((probs * (grad_probs[n] - delta[n][:, at])).astype(BF16))
                    probs_low.append(probs.astype(BF16))
                    new.append(carry[n] + matmul(kt_ref[head_rows(n), span], grad_low[-1]))
                lanes = slice(p * PAIR, (p + 1) * PAIR)
                dv_ref[span, lanes] += matmul(jnp.concatenate(probs_low, axis=1), g_split[p])
                dk_ref[span, lanes] += matmul(jnp.concatenate(grad_low, axis=1), q_split[p])
            return tuple(new)

        empty = jnp.zeros((HEAD_DIM, BLOCK), F32)
        done = lax.fori_loop(bounds[i, 0], bounds[i, 1], step, (empty,) * len(heads))
        for p in range(pairs):
            grad_q = jnp.concatenate(done[2 * p : 2 * p + 2], axis=0).T
            out_ref[at, columns(p, 0)] = (grad_q * 0.125).astype(BF16)
    for p in range(pairs):
        lanes = slice(p * PAIR, (p + 1) * PAIR)
        out_ref[:, columns(p, 1)] = dk_ref[:, lanes].astype(BF16)
        out_ref[:, columns(p, 2)] = dv_ref[:, lanes].astype(BF16)
    sums_ref[...] = jnp.sum(out_ref[...].astype(F32), axis=0, keepdims=True)


def block_bounds(starts):
    blocks = starts.reshape(-1, BLOCK)
    least, most = blocks[:, 0], blocks[:, -1]
    low = jnp.sum(most[None, :] < least[:, None], axis=1)
    high = jnp.sum(least[None, :] <= most[:, None], axis=1)
    return jnp.stack([low, high], axis=1).astype(jnp.int32)


def attention_forward(bounds, qkv, starts, index, pairs):
    length = qkv.shape[0]
    operands = (bounds, qkv, starts[None, :], starts[:, None])
    shapes = [shape_of((length, pairs * PAIR), BF16), shape_of((pairs, 2, length), F32)]
    return call(
        forward_kernel,
        "attend",
        (1,),
        [
            pl.BlockSpec((length, pairs * 3 * PAIR), lambda g, b: (0, index)),
            whole((1, length)),
            whole((length, 1)),
        ],
        [whole(x.shape) for x in shapes],
        shapes,
        pairs * 2 * length * length * HEAD_DIM * 4,
        operands,
        scratch=[pltpu.VMEM((pairs * PAIR, length), BF16)],
        prefetch=1,
        vmem=16,
    )


def attention_backward(bounds, qkv, starts, mixed, logsum, grad, index, pairs):
    length = qkv.shape[0]
    operands = (bounds, qkv, starts[None, :], starts[:, None], mixed, logsum, grad)
    shapes = [shape_of((length, pairs * 3 * PAIR), BF16), shape_of((1, pairs * 3 * PAIR), F32)]
    return call(
        backward_kernel,
        "attend_back",
        (1,),
        [
            pl.BlockSpec((length, pairs * 3 * PAIR), lambda g, b: (0, index)),
            whole((1, length)),
            whole((length, 1)),
            whole(mixed.shape),
            whole(logsum.shape),
            pl.BlockSpec((length, pairs * PAIR), lambda g, b: (0, index)),
        ],
        [whole(x.shape) for x in shapes],
        shapes,
        pairs * 2 * length * length * HEAD_DIM * 10,
        operands,
        scratch=[
            pltpu.VMEM((pairs * PAIR, length), BF16),
            pltpu.VMEM((length, pairs * PAIR), F32),
            pltpu.VMEM((length, pairs * PAIR), F32),
        ],
        prefetch=1,
        vmem=24,
    )


MEGA = 1024 * 1024


def whole(shape):
    return pl.BlockSpec(shape, lambda *_: (0,) * len(shape), pipeline_mode=pl.Buffered(1))


def call(kernel, name, grid, in_specs, out_specs, out_shape, flops, operands, scratch=(), prefetch=0, vmem=32):
    moved = sum(x.size * x.dtype.itemsize for x in operands) + sum(
        x.size * x.dtype.itemsize for x in out_shape
    )
    return pl.pallas_call(
        kernel,
        grid_spec=pltpu.PrefetchScalarGridSpec(
            num_scalar_prefetch=prefetch,
            grid=grid,
            in_specs=in_specs,
            out_specs=out_specs,
            scratch_shapes=list(scratch),
        ),
        out_shape=out_shape,
        compiler_params=pltpu.CompilerParams(vmem_limit_bytes=vmem * MEGA),
        cost_estimate=pl.CostEstimate(flops=flops, bytes_accessed=moved, transcendentals=0),
        name=name,
    )(*operands)


def shape_of(shape, dtype):
    return jax.ShapeDtypeStruct(shape, dtype)


def place_kernel(where, own_ref, beside_ref, distant_ref, corner_ref, ts_ref, low_ref, hidden_ref):
    tok = own_ref.shape[0]
    ts = ts_ref[...]
    for i, ref in enumerate((own_ref, beside_ref, distant_ref, corner_ref)):
        rows = ref[...].astype(F32) + ts
        low_ref[pl.ds(pl.multiple_of(where[i] * tok, tok), tok), :] = rows.astype(BF16)
        if i % 2 == 0:
            hidden_ref[pl.ds(pl.multiple_of(where[4 + i // 2] * tok, tok), tok), :] = rows


def place_rows(where, blocks, ts):
    tok, width = blocks[0].shape
    shapes = [shape_of((4 * tok, width), BF16), shape_of((2 * tok, width), F32)]
    return call(
        place_kernel,
        "place_rows",
        (1,),
        [whole((tok, width))] * 4 + [whole((1, width))],
        [whole(x.shape) for x in shapes],
        shapes,
        1,
        (where, *blocks, ts),
        prefetch=1,
        vmem=12,
    )


def project_kernel(stream_ref, weight_ref, bias_ref, scale_ref, out_ref, full_ref):
    owners = weight_ref.shape[0]
    rows = full_ref.shape[0] // owners
    for m in range(owners):
        full_ref[m * rows : (m + 1) * rows, :] = weight_ref[m, :rows, :]
    out_ref[...] = ((matmul(stream_ref[...], full_ref[...]) + bias_ref[...]) * scale_ref[...]).astype(BF16)


def project_heads(stream, gathered, bias, scale):
    length, width = stream.shape
    owners, tall, cols = gathered.shape
    tile = cols // 3
    shapes = [shape_of((length, cols), BF16), shape_of((width, cols), BF16)]
    row = pl.BlockSpec((1, tile), lambda t: (0, t))
    return call(
        project_kernel,
        "project_heads",
        (3,),
        [whole((length, width)), pl.BlockSpec((owners, tall, tile), lambda t: (0, 0, t)), row, row],
        [pl.BlockSpec((length, tile), lambda t: (0, t)), pl.BlockSpec((width, tile), lambda t: (0, t))],
        shapes,
        2 * length * width * cols,
        (stream, gathered, bias, scale),
        vmem=16,
    )


def output_kernel(where, *refs):
    (mine_refs, their_refs), (weight_ref, bias_ref, hidden_ref, gain_ref, shift_ref) = (
        (refs[:4], refs[4:6]),
        refs[6:11],
    )
    out_ref, low_ref, normed_ref, factor_ref, mixed_ref = refs[11:]
    h = where[0]
    half = weight_ref.shape[0] // 2
    part = half // 2
    rows = mine_refs[0].shape[0]
    for i in range(2):
        at = slice(i * rows, (i + 1) * rows)
        total = hidden_ref[at, :] + bias_ref[...]
        for cut in range(2):
            mine = pl.ds(pl.multiple_of(h * half + cut * part, 128), part)
            other = pl.ds(pl.multiple_of((1 - h) * half + cut * part, 128), part)
            left, right = mine_refs[2 * cut + i][...], their_refs[cut][at, :]
            mixed_ref[at, mine] = left
            mixed_ref[at, other] = right
            total = total + matmul(left, weight_ref[mine, :]) + matmul(right, weight_ref[other, :])
        out, normed, factor = layer_norm(total, gain_ref[...], shift_ref[...])
        out_ref[at, :] = out
        low_ref[at, :] = out.astype(BF16)
        normed_ref[at, :] = normed
        factor_ref[at, :] = factor


def project_output(h, mine, their, weight, bias, hidden, gain, shift):
    rows, width = hidden.shape
    tok = rows // 2
    part = mine[0].shape[1]
    where = jnp.stack([h, h + 2]).astype(jnp.int32)
    in_specs = [
        pl.BlockSpec((tok, part), lambda g, w: (w[0], 0)),
        pl.BlockSpec((tok, part), lambda g, w: (w[1], 0)),
    ] * 2
    in_specs += [whole((rows, part))] * 2
    in_specs += [whole(weight.shape), whole((1, width)), whole((rows, width)), whole((1, width)), whole((1, width))]
    shapes = [
        shape_of((rows, width), F32),
        shape_of((rows, width), BF16),
        shape_of((rows, width), F32),
        shape_of((rows, 1), F32),
        shape_of((rows, width), BF16),
    ]
    operands = (where, mine[0], mine[0], mine[1], mine[1], their[0], their[1], weight, bias, hidden, gain, shift)
    return call(
        output_kernel,
        "project_output",
        (1,),
        in_specs,
        [whole(x.shape) for x in shapes],
        shapes,
        2 * rows * width * width,
        operands,
        prefetch=1,
    )


def inner_kernel(order, first_ref, *refs):
    pieces, (bias_ref, active_ref, slope_ref, full_ref) = refs[:-4], refs[-4:]
    block = first_ref.shape[1] // 8
    done = 0
    for piece in pieces:
        rows = piece.shape[0]
        at = order[done // block] * block + done % block
        full_ref[pl.ds(pl.multiple_of(at, rows), rows), :] = piece[...]
        done += rows
    rows = first_ref.shape[0]
    step = 256
    for i in range(rows // step):
        at = slice(i * step, (i + 1) * step)
        inner = matmul(first_ref[at, :], full_ref[...]) + bias_ref[...]
        cdf, pdf = normal_cdf_pdf(inner)
        active_ref[0, at, :] = (inner * cdf).astype(BF16)
        slope_ref[0, at, :] = (cdf + inner * pdf).astype(BF16)


def feed_inner(order, first_low, pieces, bias):
    rows, width = first_low.shape
    ff = pieces[0].shape[1]
    tile = ff // 8
    shapes = [
        shape_of((8, rows, tile), BF16),
        shape_of((8, rows, tile), BF16),
        shape_of((width, ff), BF16),
    ]
    return call(
        inner_kernel,
        "feed_inner",
        (8,),
        [whole((rows, width))]
        + [pl.BlockSpec((x.shape[0], tile), lambda t, o: (0, t)) for x in pieces]
        + [pl.BlockSpec((1, tile), lambda t, o: (0, t))],
        [
            pl.BlockSpec((1, rows, tile), lambda t, o: (t, 0, 0)),
            pl.BlockSpec((1, rows, tile), lambda t, o: (t, 0, 0)),
            pl.BlockSpec((width, tile), lambda t, o: (0, t)),
        ],
        shapes,
        2 * rows * width * ff,
        (order, first_low, *pieces, bias),
        prefetch=1,
    )


def outer_kernel(order, active_ref, *refs):
    pieces, refs = refs[:-12], refs[-12:]
    bias_ref, first_ref, own_ref, moved_ref, gain_ref, shift_ref = refs[:6]
    full_ref, out_ref, grad_ref, low_ref, sums_ref, acc_ref = refs[6:]
    t = pl.program_id(0)
    block, tile = full_ref.shape[1:]
    done = 0
    for piece in pieces:
        rows = piece.shape[0]
        full_ref[order[done // block], done % block : done % block + rows] = piece[...]
        done += rows
    total = matmul(active_ref[0], full_ref[0])
    for k in range(1, 8):
        total = total + matmul(active_ref[k], full_ref[k])
    acc_ref[:, pl.ds(pl.multiple_of(t * tile, tile), tile)] = total

    @pl.when(t == pl.num_programs(0) - 1)
    def _():
        rows, width = acc_ref.shape
        step = 128
        gain, shift, bias = gain_ref[...], shift_ref[...], bias_ref[...]
        sums = [jnp.zeros((1, width), F32)] * 3
        for i in range(rows // step):
            at = slice(i * step, (i + 1) * step)
            out, normed, factor = layer_norm(first_ref[at, :] + acc_ref[at, :] + bias, gain, shift)
            out_ref[at, :] = out.astype(BF16)
            tok = own_ref.shape[0]
            which, at_block = i * step // tok, slice(i * step % tok, i * step % tok + step)
            up = jnp.where(order[8] == which, own_ref[at_block, :], moved_ref[at_block, :]).astype(F32)
            grad = norm_back(up, normed, factor, gain)
            low = grad.astype(BF16)
            grad_ref[at, :] = grad
            low_ref[at, :] = low
            for j, item in enumerate((up * normed, up, low.astype(F32))):
                sums[j] = sums[j] + jnp.sum(item, axis=0, keepdims=True)
        sums_ref[...] = jnp.concatenate(sums + [jnp.zeros((5, width), F32)], axis=0)


def feed_outer(order, active, pieces, bias, first_out, own, moved, gain, shift):
    rows, width = first_out.shape
    block = sum(x.shape[0] for x in pieces) // 8
    tile = width // 4
    shapes = [
        shape_of((8, block, width), BF16),
        shape_of((rows, width), BF16),
        shape_of((rows, width), F32),
        shape_of((rows, width), BF16),
        shape_of((8, width), F32),
    ]
    row = whole((1, width))
    return call(
        outer_kernel,
        "feed_outer",
        (4,),
        [whole(active.shape)]
        + [pl.BlockSpec((x.shape[0], tile), lambda t, o: (0, t)) for x in pieces]
        + [row, whole((rows, width)), whole(own.shape), whole(moved.shape), row, row],
        [pl.BlockSpec((8, block, tile), lambda t, o: (0, 0, t))] + [whole(x.shape) for x in shapes[1:]],
        shapes,
        2 * rows * width * block * 8,
        (order, active, *pieces, bias, first_out, own, moved, gain, shift),
        scratch=[pltpu.VMEM((rows, width), F32)],
        prefetch=1,
    )


def gelu_back_kernel(grad_ref, weight_ref, slope_ref, out_ref, sums_ref):
    grad = contract_cols(grad_ref[...], weight_ref[0])
    low = (grad * slope_ref[0].astype(F32)).astype(BF16)
    out_ref[0] = low
    sums_ref[0] = jnp.sum(low.astype(F32), axis=0, keepdims=True)


def gelu_back(grad_outer, full_outer, slope):
    rows, width = grad_outer.shape
    _, block, _ = full_outer.shape
    tile = slope.shape[2]
    shapes = [shape_of(slope.shape, BF16), shape_of((8, 1, tile), F32)]
    return call(
        gelu_back_kernel,
        "gelu_back",
        (8,),
        [
            whole((rows, width)),
            pl.BlockSpec((1, block, width), lambda t: (t, 0, 0)),
            pl.BlockSpec((1, rows, tile), lambda t: (t, 0, 0)),
        ],
        [
            pl.BlockSpec((1, rows, tile), lambda t: (t, 0, 0)),
            pl.BlockSpec((1, 1, tile), lambda t: (t, 0, 0)),
        ],
        shapes,
        2 * rows * width * tile * 8,
        (grad_outer, full_outer, slope),
    )


def first_back_kernel(grad_ref, weight_ref, second_ref, normed_ref, factor_ref, gain_ref, output_ref, *refs):
    out_ref, low_ref, mixed_ref, sums_ref, acc_ref = refs
    t = pl.program_id(0)
    part = contract_cols(grad_ref[0], weight_ref[...])

    @pl.when(t == 0)
    def _():
        acc_ref[...] = second_ref[...] + part

    @pl.when(t > 0)
    def _():
        acc_ref[...] += part

    @pl.when(t == pl.num_programs(0) - 1)
    def _():
        rows, width = acc_ref.shape
        step = 128
        gain = gain_ref[...]
        sums = [jnp.zeros((1, width), F32)] * 3
        for i in range(rows // step):
            at = slice(i * step, (i + 1) * step)
            up, normed = acc_ref[at, :], normed_ref[at, :]
            grad = norm_back(up, normed, factor_ref[at, :], gain)
            low = grad.astype(BF16)
            out_ref[at, :] = grad
            low_ref[at, :] = low
            for j, item in enumerate((up * normed, up, low.astype(F32))):
                sums[j] = sums[j] + jnp.sum(item, axis=0, keepdims=True)
        sums_ref[...] = jnp.concatenate(sums + [jnp.zeros((5, width), F32)], axis=0)
        mixed_ref[...] = contract_cols(low_ref[...], output_ref[...]).astype(BF16)


def first_back(grad_inner, full_inner, grad_second, normed, factor, gain, full_output):
    rows, width = grad_second.shape
    tile = grad_inner.shape[2]
    shapes = [
        shape_of((rows, width), F32),
        shape_of((rows, width), BF16),
        shape_of((rows, width), BF16),
        shape_of((8, width), F32),
    ]
    return call(
        first_back_kernel,
        "first_back",
        (8,),
        [
            pl.BlockSpec((1, rows, tile), lambda t: (t, 0, 0)),
            pl.BlockSpec((width, tile), lambda t: (0, t)),
            whole((rows, width)),
            whole((rows, width)),
            whole((rows, 1)),
            whole((1, width)),
            whole(full_output.shape),
        ],
        [whole(x.shape) for x in shapes],
        shapes,
        2 * rows * width * (tile * 8 + width),
        (grad_inner, full_inner, grad_second, normed, factor, gain, full_output),
        scratch=[pltpu.VMEM((rows, width), F32)],
    )


def block_grad_kernel(order, left_ref, right_ref, out_ref):
    out_ref[0] = contract_rows(left_ref[0], right_ref[...]).astype(BF16)


def block_grad(order, left, right):
    rows, width = right.shape
    block = left.shape[2]
    shapes = [shape_of((4, block, width), BF16)]
    return call(
        block_grad_kernel,
        "block_grad",
        (4,),
        [pl.BlockSpec((1, rows, block), lambda i, o: (o[i], 0, 0)), whole((rows, width))],
        [pl.BlockSpec((1, block, width), lambda i, o: (i, 0, 0))],
        shapes,
        2 * rows * width * block * 4,
        (order, left, right),
        prefetch=1,
    )[0]


def turn_strips(order, left_ref, turned_ref):
    block = turned_ref.shape[0] // 4
    for i in range(4):
        strip = left_ref[:, pl.ds(pl.multiple_of(order[i] * block, block), block)]
        turned_ref[i * block : (i + 1) * block, : strip.shape[0]] = strip.T


def tile_grad_kernel(order, left_ref, right_ref, out_ref, turned_ref):
    block = out_ref.shape[1]

    @pl.when(pl.program_id(0) == 0)
    def _():
        turn_strips(order, left_ref, turned_ref)

    out = matmul(turned_ref[...], right_ref[0]).astype(BF16)
    for i in range(4):
        out_ref[i] = out[i * block : (i + 1) * block]


def tile_grad(order, left, right):
    rows, width = left.shape
    block = width // 8
    tiles, _, tile = right.shape
    shapes = [shape_of((4, block, tiles * tile), BF16)]
    return call(
        tile_grad_kernel,
        "tile_grad",
        (tiles,),
        [whole((rows, width)), pl.BlockSpec((1, rows, tile), lambda t, o: (t, 0, 0))],
        [pl.BlockSpec((4, block, tile), lambda t, o: (0, 0, t))],
        shapes,
        2 * rows * block * 4 * tiles * tile,
        (order, left, right),
        scratch=[pltpu.VMEM((4 * block, rows), BF16)],
        prefetch=1,
        vmem=12,
    )[0]


def strip_grad_kernel(
    parts, order, left_ref, first_ref, second_ref, extra_ref, low_ref, third_ref, out_ref, turned_ref
):
    t = pl.program_id(0)
    last = parts[0] + parts[1]
    block = turned_ref.shape[0] // 4

    @pl.when(t == 0)
    def _():
        turn_strips(order, left_ref, turned_ref)

    @pl.when(t == last)
    def _():
        turn_strips(order, low_ref, turned_ref)

    def put(right, extra):
        out = matmul(turned_ref[:, : right.shape[0]], right).astype(BF16)
        for i in range(4):
            out_ref[i, :block] = out[i * block : (i + 1) * block]
            out_ref[i, block:] = extra_ref[order[i]] if extra else jnp.zeros_like(out_ref[i, block:])

    @pl.when(t < parts[0])
    def _():
        put(first_ref[...], True)

    @pl.when((t >= parts[0]) & (t < last))
    def _():
        put(second_ref[...], True)

    @pl.when(t >= last)
    def _():
        put(third_ref[...], False)


def strip_grad(order, left, first, second, extra, low, third):
    rows, width = left.shape
    block = width // 8
    tile = 512 if first.shape[1] % 512 == 0 else 256
    parts = [x.shape[1] // tile for x in (first, second, third)]
    total = sum(parts)
    tall = block + extra.shape[1]
    shapes = [shape_of((4, tall, total * tile), BF16)]
    return call(
        partial(strip_grad_kernel, parts),
        "strip_grad",
        (total,),
        [
            whole((rows, width)),
            pl.BlockSpec((rows, tile), lambda t, o: (0, jnp.minimum(t, parts[0] - 1))),
            pl.BlockSpec((rows, tile), lambda t, o: (0, jnp.clip(t - parts[0], 0, parts[1] - 1))),
            pl.BlockSpec(
                (8, extra.shape[1], tile), lambda t, o: (0, 0, jnp.minimum(t, parts[0] + parts[1] - 1))
            ),
            whole(low.shape),
            pl.BlockSpec((low.shape[0], tile), lambda t, o: (0, jnp.maximum(t - parts[0] - parts[1], 0))),
        ],
        [pl.BlockSpec((4, tall, tile), lambda t, o: (0, 0, t))],
        shapes,
        2 * rows * block * 4 * total * tile,
        (order, left, first, second, extra, low, third),
        scratch=[pltpu.VMEM((4 * block, rows), BF16)],
        prefetch=1,
        vmem=20,
    )[0]


def hidden_back_kernel(where, *refs):
    lefts, weight_ref, rest = refs[:2], refs[2], refs[3:]
    part = lefts[0].shape[1]
    total = contract_cols(lefts[0][...], weight_ref[:, :part]) + contract_cols(lefts[1][...], weight_ref[:, part:])
    if len(rest) == 2:
        total = total + rest[0][...]
    rest[-1][...] = total.astype(rest[-1].dtype)


def hidden_back(parity, grads, weight, base, tok):
    width = weight.shape[0]
    part = grads[0].shape[1]
    where = jnp.stack([parity, parity + 2]).astype(jnp.int32)
    row = pl.BlockSpec((tok, width), lambda i, w: (i, 0))
    extra = () if base is None else (base,)
    shapes = [shape_of((2 * tok, width), BF16 if base is None else F32)]
    return call(
        hidden_back_kernel,
        "hidden_back",
        (2,),
        [pl.BlockSpec((tok, part), lambda i, w: (w[i], 0))] * 2 + [whole(weight.shape)] + [row] * len(extra),
        [row],
        shapes,
        2 * 2 * tok * width * part * 2,
        (where, *grads, weight, *extra),
        prefetch=1,
    )[0]


def after(x, *deps):
    return lax.optimization_barrier((x, deps))[0]


class Steps:
    def __init__(self):
        self.last = ()

    def __call__(self, fn, *args):
        args, _ = lax.optimization_barrier((args, self.last))
        out = fn(*args)
        self.last = out
        return out


def flip(x, axis, size, bit):
    return lax.ppermute(x, axis, [(i, i ^ bit) for i in range(size)])


def swap(x, bit):
    return flip(x, "fsdp", 8, bit)


def widen(*items):
    return sum(item.astype(F32) for item in items)


class CubeSum:
    def __init__(self, send, width, x_columns):
        self.got = swap(send, 1)
        self.parts = []
        if x_columns > 0:
            self.parts.append((slice(0, x_columns), 1, 2, 2, 4))
        if x_columns < width:
            self.parts.append((slice(x_columns, width), 2, 1, 4, 2))

    def first_hop(self, steps, keep):
        def add(keep, got):
            return [
                jnp.stack([widen(keep[i, :, cols], got[i, :, cols]).astype(BF16) for i in (away, 3)])
                for cols, _, away, _, _ in self.parts
            ]

        self.keep = keep
        there = steps(add, keep, self.got)
        self.back = [swap(x, part[3]) for x, part in zip(there, self.parts)]

    def second_hop(self, steps):
        def add(keep, got, back):
            here, there = [], []
            for (cols, near, _, _, _), b in zip(self.parts, back):
                here.append(widen(keep[0, :, cols], got[0, :, cols], b[0]))
                there.append(widen(keep[near, :, cols], got[near, :, cols], b[1]).astype(BF16))
            return here, there

        self.here, there = steps(add, self.keep, self.got, self.back)
        self.last = [swap(x, part[4]) for x, part in zip(there, self.parts)]

    def result(self, steps):
        def add(here, last):
            sums = [widen(x, y).astype(BF16) for x, y in zip(here, last)]
            return sums[0] if len(sums) == 1 else jnp.concatenate(sums, axis=1)

        return steps(add, self.here, self.last)


class PlainSum:
    def __init__(self, product, extra=()):
        self.product, self.extra = product.astype(BF16), extra

    def first_hop(self, steps, keep):
        pass

    def second_hop(self, steps):
        pass

    def result(self, steps):
        share = lax.psum_scatter(self.product, "fsdp", scatter_dimension=0, tiled=True)
        lines = [lax.psum_scatter(x, "fsdp", scatter_dimension=0, tiled=False) for x in self.extra]
        return (share, *lines) if lines else share


def pair_pack(parts):
    rows = parts[0].shape[0]
    return jnp.stack([p.reshape(rows, -1, PAIR) for p in parts], axis=2).reshape(rows, -1)


def pair_unpack(packed):
    rows = packed.shape[0]
    cut = packed.reshape(rows, -1, 3, PAIR)
    return [cut[:, :, i].reshape(rows, -1) for i in range(3)]


def body(
    fsdp,
    stream_in,
    timestep,
    doc_start,
    query_weight,
    key_weight,
    value_weight,
    output_weight,
    query_bias,
    value_bias,
    output_bias,
    first_gain,
    first_shift,
    inner_weight,
    inner_bias,
    outer_weight,
    outer_bias,
    second_gain,
    second_shift,
    cotangent,
):
    cube = fsdp == 8
    steps = Steps()
    me = lax.axis_index("fsdp")
    streams, tok, width = stream_in.shape
    own_rows = query_weight.shape[0]
    half = width // 2
    ff = inner_weight.shape[1]
    length = 4 * tok
    z = lax.axis_index("seq")
    h, s = z % 2, z // 2

    def flip_h(x):
        return flip(x, "seq", 4, 1)

    def flip_s(x):
        return flip(x, "seq", 4, 2)

    def in_order(mine, other):
        return jnp.where(s == 0, jnp.concatenate([mine, other]), jnp.concatenate([other, mine]))

    def pick(x, index, axis=0):
        return lax.dynamic_index_in_dim(x, index, axis, keepdims=False)

    head_cols = [lax.dynamic_slice_in_dim(w, h * half, half, 1) for w in (query_weight, key_weight, value_weight)]
    small = jnp.concatenate(
        [
            query_bias,
            value_bias,
            output_bias,
            first_gain,
            first_shift,
            outer_bias,
            second_gain,
            second_shift,
            inner_bias,
        ]
    )
    packed = pair_pack(head_cols)
    own = pick(stream_in, s)
    if cube:
        owners = [me ^ m for m in range(8)]
        packed = jnp.concatenate([packed, jnp.broadcast_to(small[None, :], (16, small.shape[0]))])
        gathered = lax.all_gather(packed, "fsdp", axis=0, tiled=False)
        small_rows = gathered[:, own_rows]
        output_w = after(output_weight, gathered)
        full_output = lax.all_gather(output_w, "fsdp", axis=0, tiled=True)
        inner_w = after(inner_weight, packed)
        ix, iy = swap(inner_w, 2), swap(inner_w, 4)
        distant = flip_s(pick(stream_in, 1 - s))
        beside = flip_h(own)
        distant, beside = steps(lambda *x: x, distant, beside)
        corner = flip_h(distant)
        cut = own_rows // 2
        top, bottom, ix, iy, inner_w, outer_w = steps(
            lambda x, y, *rest: (x[:cut], y[cut:], x, y, *rest), ix, iy, inner_w, outer_weight
        )
        jy, jx = swap(top, 4), swap(bottom, 2)
        ic = swap(inner_w, 1)
    else:
        owners = list(range(8))

        def gather(piece):
            full = lax.all_gather(piece, "fsdp", axis=0, tiled=True)
            return list(full.reshape(8, full.shape[0] // 8, full.shape[1]))

        distant, beside = flip_s(pick(stream_in, 1 - s)), flip_h(own)
        corner = flip_h(distant)
        gathered = lax.all_gather(packed, "fsdp", axis=0, tiled=False)
        full_output = lax.all_gather(output_weight, "fsdp", axis=0, tiled=True)
        inner_pieces, outer_pieces = gather(inner_weight), gather(outer_weight)
        small_rows = lax.all_gather(small, "fsdp", axis=0, tiled=False)
    order = jnp.stack([jnp.asarray(o, jnp.int32) for o in owners])
    small_rows = small_rows.astype(F32)
    qbias, vbias, obias, gain_one, shift_one, obias_two, gain_two, shift_two = [
        small_rows[:, i * own_rows : (i + 1) * own_rows].reshape(1, -1) for i in range(8)
    ]
    ibias = small_rows[:, 8 * own_rows :].reshape(1, -1)

    ts = pick(timestep, s).astype(F32)

    cotangent_own, cotangent_out = pick(cotangent, s), pick(cotangent, 1 - s)
    if cube:
        corner, ic, outer_w, cotangent_out = steps(lambda *x: x, corner, ic, outer_w, cotangent_out)
        ox, oy = swap(outer_w, 2), swap(outer_w, 4)
    moved = flip_s(cotangent_out)
    where = jnp.stack([z, z ^ 1, z ^ 2, z ^ 3, s, 1 - s]).astype(jnp.int32)
    stream_low, hidden = steps(
        lambda *x: place_rows(where, x[:4], x[4]), own, beside, distant, corner, ts.reshape(1, width)
    )
    starts = pick(doc_start, s)
    bounds = block_bounds(starts)

    qb = lax.dynamic_slice_in_dim(qbias, h * half, half, 1)
    vb = lax.dynamic_slice_in_dim(vbias, h * half, half, 1)
    bias_row = pair_pack([qb, jnp.zeros_like(qb), vb])
    scale_row = pair_pack([jnp.full((1, half), 0.125, F32), jnp.ones((1, half), F32), jnp.ones((1, half), F32)])
    qkv, full_qkv = steps(project_heads, stream_low, gathered, bias_row, scale_row)
    pairs = half // PAIR
    part = pairs // 2

    def rows_of(x, parity):
        cut = x.reshape(2, 2, tok, x.shape[1])
        return pick(cut, parity, 1).reshape(2 * tok, x.shape[1])

    def attend(index, qkv):
        return attention_forward(bounds, qkv, starts, index, part)

    if cube:
        jy, jx, ix, iy, qkv = steps(lambda *x: x, jy, jx, ix, iy, qkv)
        ixc, iyc = swap(ix, 1), swap(iy, 1)
    else:
        ixc = iyc = jy = jx = 0.0
    mixed_a, logsum_a = steps(partial(attend, 0), qkv)
    out_a, ixc, iyc, jy, jx, moved = steps(lambda x, *rest: (rows_of(x, 1 - h), *rest), mixed_a, ixc, iyc, jy, jx, moved)
    their_a = flip_h(out_a)
    if cube:
        jyc, jxc = swap(jy, 1), swap(jx, 1)
    else:
        jyc = jxc = 0.0
    mixed_b, logsum_b = steps(partial(attend, 1), qkv)
    out_b, their_a, jyc, jxc = steps(lambda x, *rest: (rows_of(x, 1 - h), *rest), mixed_b, their_a, jyc, jxc)
    their_b = flip_h(out_b)
    if cube:
        inner_pieces = [inner_w, ic, ix, ixc, iy, iyc, jy, jx, jyc, jxc]
        cut = outer_weight.shape[0] // 2
        top, bottom, ox, oy = steps(lambda x, y: (x[:cut], y[cut:], x, y), ox, oy)
        jy, jx, oxc = swap(top, 4), swap(bottom, 2), swap(ox, 1)
    first_out, first_low, first_normed, first_factor, mixed = steps(
        partial(project_output, h),
        (mixed_a, mixed_b),
        (their_a, their_b),
        full_output,
        obias,
        hidden,
        gain_one,
        shift_one,
    )

    if cube:
        jy, jx, oxc, oy, outer_w, first_low = steps(lambda *x: x, jy, jx, oxc, oy, outer_w, first_low)
        oc, oyc, jyc, jxc = swap(outer_w, 1), swap(oy, 1), swap(jy, 1), swap(jx, 1)
        outer_pieces = [outer_w, oc, ox, oxc, oy, oyc, jy, jx, jyc, jxc]
    active, slope, full_inner = steps(partial(feed_inner, order), first_low, inner_pieces, ibias)
    facts = jnp.concatenate([order, s.astype(jnp.int32).reshape(1)])
    full_outer, result, grad_second_in, grad_outer, second_sums = steps(
        partial(feed_outer, facts),
        active,
        outer_pieces,
        obias_two,
        first_out,
        cotangent_own,
        moved,
        gain_two,
        shift_two,
    )
    result = result.reshape(2, tok, width)
    result_own, result_out = steps(lambda x: (pick(x, s), pick(x, 1 - s)), result)
    result_away = flip_s(result_out)

    if cube:
        send_order = jnp.stack([me ^ m for m in (1, 5, 3, 7)]).astype(jnp.int32)
        keep_order = jnp.stack([me ^ m for m in (0, 4, 2, 6)]).astype(jnp.int32)

    if cube:
        outer_send = steps(partial(block_grad, send_order), active, grad_outer)
        outer_sum = CubeSum(outer_send, width, half)
        outer_keep = steps(partial(block_grad, keep_order), active, grad_outer)
    else:
        outer_keep = ()
        outer_sum = PlainSum(contract_rows(active.transpose(1, 0, 2).reshape(2 * tok, -1), grad_outer))
    grad_inner, inner_sums = steps(gelu_back, grad_outer, full_outer, slope)
    outer_sum.first_hop(steps, outer_keep)
    if cube:
        inner_send = steps(partial(tile_grad, send_order), first_low, grad_inner)
        inner_sum = CubeSum(inner_send, ff, ff // 2)
    else:
        inner_sum = PlainSum(contract_rows(first_low, grad_inner.transpose(1, 0, 2).reshape(2 * tok, -1)))

    def first_step(*args):
        grad_first_in, grad_attended, grad_mixed, sums = first_back(*args)
        wide = half // 2
        theirs = lax.dynamic_slice_in_dim(grad_mixed, (1 - h) * half, half, 1)
        mine = lax.dynamic_slice_in_dim(grad_mixed, h * half, half, 1)
        return grad_first_in, grad_attended, sums, theirs, mine

    grad_first_in, grad_attended, first_sums, theirs, mine = steps(
        first_step, grad_inner, full_inner, grad_second_in, first_normed, first_factor, gain_one, full_output
    )
    received = flip_h(theirs)
    inner_keep = steps(partial(tile_grad, keep_order), first_low, grad_inner) if cube else ()
    result_away = steps(lambda x: x, result_away)
    outer_sum.second_hop(steps)

    def to_heads(mine, received):
        mine = mine.reshape(2, 1, tok, half)
        received = received.reshape(2, 1, tok, half)
        return jnp.where(
            h == 0, jnp.concatenate([mine, received], axis=1), jnp.concatenate([received, mine], axis=1)
        ).reshape(length, half)

    grad_heads = steps(to_heads, mine, received)

    def seq_sum(share):
        def halve(x, bit):
            pair = x.reshape(2, x.shape[0] // 2, -1)
            return pick(pair, bit), pick(pair, 1 - bit)

        def join(mine, other, bit):
            return jnp.where(bit == 0, jnp.concatenate([mine, other]), jnp.concatenate([other, mine]))

        mine, out = steps(lambda x: halve(x, h), share)
        back = flip_h(out)
        yield
        def quarter(m, b):
            mine, out = halve(widen(m, b), s)
            return mine, out.astype(BF16)

        mine, out = steps(quarter, mine, back)
        back = flip_s(out)
        yield
        mine = steps(lambda m, b: widen(m, b).astype(BF16), mine, back)
        back = flip_s(mine)
        yield
        mine = steps(lambda m, b: join(m, b, s), mine, back)
        back = flip_h(mine)
        yield
        yield steps(lambda m, b: join(m, b, h).astype(F32), mine, back)

    def attend_back(index, qkv, mixed, logsum, grad):
        return attention_backward(bounds, qkv, starts, mixed, logsum, grad, index, part)

    grad_a, sums_a = steps(partial(attend_back, 0), qkv, mixed_a, logsum_a, grad_heads)
    inner_sum.first_hop(steps, inner_keep)
    outer_share = outer_sum.result(steps)
    outer_steps = seq_sum(outer_share)
    next(outer_steps)
    grad_b, sums_b = steps(partial(attend_back, 1), qkv, mixed_b, logsum_b, grad_heads)
    next(outer_steps)
    away = flip_h(
        steps(lambda a, b, w: hidden_back(1 - h, (a, b), w, None, tok), grad_a, grad_b, full_qkv)
    )
    zero_half = jnp.zeros((half,), F32)

    def spread(v):
        v = v.reshape(-1)
        return jnp.where(h == 0, jnp.concatenate([v, zero_half]), jnp.concatenate([zero_half, v]))

    grad_q_cols, _, grad_v_cols = pair_unpack(jnp.concatenate([sums_a, sums_b], axis=1))
    vectors = jnp.concatenate(
        [
            v.reshape(fsdp, -1)
            for v in (
                spread(grad_q_cols),
                spread(grad_v_cols),
                first_sums[2],
                first_sums[0],
                first_sums[1],
                second_sums[2],
                second_sums[0],
                second_sums[1],
                inner_sums,
            )
        ],
        axis=1,
    ).astype(BF16)
    if cube:
        lines = vectors.reshape(fsdp, 1, -1)
        lines = jnp.concatenate([lines, jnp.zeros((fsdp, 15, lines.shape[2]), BF16)], axis=1)
        qkv_operands = (stream_low, grad_a, grad_b, lines, mixed, grad_attended)
        qkv_send = steps(partial(strip_grad, send_order), *qkv_operands)
        qkv_sum = CubeSum(qkv_send, qkv_send.shape[2], qkv_send.shape[2] // 2)
        inner_sum.second_hop(steps)
        next(outer_steps)
        qkv_keep = steps(partial(strip_grad, keep_order), *qkv_operands)
    else:
        qkv_keep = ()
        both = jnp.concatenate([grad_a, grad_b], axis=1)
        both = jnp.concatenate([contract_rows(stream_low, both), contract_rows(mixed, grad_attended)], axis=1)
        qkv_sum = PlainSum(both, (vectors,))
        next(outer_steps)
    kept = steps(lambda a, b, w, g: hidden_back(h, (a, b), w, g, tok), grad_a, grad_b, full_qkv, grad_first_in)

    def split_rows(kept, away):
        grad_hidden = (kept + away.astype(F32)).reshape(2, tok, width)
        return pick(grad_hidden, s), pick(grad_hidden, 1 - s).astype(BF16)

    inner_share = inner_sum.result(steps)
    inner_steps = seq_sum(inner_share)
    next(inner_steps)
    qkv_sum.first_hop(steps, qkv_keep)
    grad_own, grad_out = steps(split_rows, kept, away)
    grad_away = flip_s(grad_out)
    next(inner_steps)
    next(outer_steps)
    qkv_sum.second_hop(steps)
    next(inner_steps)

    layer_out = jnp.where(s == 0, jnp.stack([result_own, result_away]), jnp.stack([result_away, result_own]))

    def swap_heads(mine, other):
        return jnp.where(h == 0, jnp.concatenate([mine, other], axis=1), jnp.concatenate([other, mine], axis=1))

    qkv_share = qkv_sum.result(steps)
    qkv_share, extra = qkv_share if not cube else (qkv_share, None)
    qkv_back = flip_s(qkv_share)
    outer_grad = next(outer_steps)
    next(inner_steps)
    grad_own, grad_away = steps(lambda x, y: (x, y.astype(F32)), grad_own, grad_away)
    input_grad = jnp.where(s == 0, jnp.stack([grad_own, grad_away]), jnp.stack([grad_away, grad_own]))
    qkv_mine = steps(lambda x, y: widen(x, y).astype(BF16), qkv_share, qkv_back)
    qkv_other = flip_h(qkv_mine)
    inner_grad = next(inner_steps)
    three = 3 * half
    output_grad = widen(qkv_mine[:own_rows, three:], qkv_other[:own_rows, three:])
    if cube:
        sums = widen(qkv_mine[own_rows, :three], qkv_other[own_rows, :three])
    else:
        sums = lax.psum(extra.astype(F32), "seq")
    qkv_grads = [
        swap_heads(mine, other).astype(F32)
        for mine, other in zip(
            pair_unpack(qkv_mine[:own_rows, :three]), pair_unpack(qkv_other[:own_rows, :three])
        )
    ]
    cut = [sums[i * own_rows : (i + 1) * own_rows] for i in range(8)]
    return (
        layer_out,
        input_grad,
        qkv_grads[0],
        qkv_grads[1],
        qkv_grads[2],
        output_grad,
        cut[0],
        cut[1],
        cut[2],
        cut[3],
        cut[4],
        inner_grad,
        sums[8 * own_rows :],
        outer_grad,
        cut[5],
        cut[6],
        cut[7],
    )


def solution(mesh):
    rows = P("fsdp", "seq", None)
    mat = P("fsdp", None)
    vec = P("fsdp")
    in_specs = (rows, mat, mat) + (mat,) * 4 + (vec,) * 5 + (mat, vec, mat, vec, vec, vec) + (rows,)
    out_specs = (rows, rows) + (mat,) * 4 + (vec,) * 5 + (mat, vec, mat, vec, vec, vec)
    return jax.shard_map(
        partial(body, mesh.shape["fsdp"]), mesh=mesh, in_specs=in_specs, out_specs=out_specs, check_vma=False
    )
```

```python
from functools import partial

import jax
import jax.numpy as jnp
from jax import lax
from jax.experimental import pallas as pl
from jax.experimental.pallas import tpu as pltpu
from jax.sharding import PartitionSpec as P

HEAD_DIM = 64
PAIR = 2 * HEAD_DIM
BLOCK = 256
F32 = jnp.float32
BF16 = jnp.bfloat16

PHI_POLY = (
    0.11962928975633808,
    0.12075411058236112,
    0.09991242675653945,
    0.12856547821204567,
    -0.053691543682108024,
    0.20636272322745108,
    -0.15720876784307727,
    0.03567620985200702,
)


def normal_cdf_pdf(z):
    u = jnp.abs(z)
    bell = jnp.exp(-0.5 * u * u)
    t = 1.0 / (1.0 + 0.3 * u)
    poly = jnp.full_like(t, PHI_POLY[-1])
    for coef in PHI_POLY[-2::-1]:
        poly = poly * t + coef
    tail = bell * (t * poly)
    return jnp.where(z < 0, tail, 1.0 - tail), bell * 0.3989422804014327


def layer_norm(rows, gain, shift):
    centred = rows - jnp.mean(rows, axis=-1, keepdims=True)
    factor = lax.rsqrt(jnp.mean(centred * centred, axis=-1, keepdims=True) + 1e-05)
    normed = centred * factor
    return (normed * gain + shift, normed, factor)


def norm_back(upstream, normed, factor, gain):
    scaled = upstream * gain
    return factor * (
        scaled
        - jnp.mean(scaled, axis=-1, keepdims=True)
        - normed * jnp.mean(scaled * normed, axis=-1, keepdims=True)
    )


def matmul(left, right):
    return jnp.dot(left, right, preferred_element_type=F32)


def contract_rows(left, right):
    return lax.dot_general(left, right, (((0,), (0,)), ((), ())), preferred_element_type=F32)


def contract_cols(left, right):
    return lax.dot_general(left, right, (((1,), (1,)), ((), ())), preferred_element_type=F32)


def column_sum(rows):
    return jnp.sum(rows.astype(F32), axis=0)


def half_rows(block, head):
    zero = jnp.zeros((HEAD_DIM, block.shape[1]), block.dtype)
    part = block[head * HEAD_DIM : (head + 1) * HEAD_DIM]
    return jnp.concatenate([part, zero] if head == 0 else [zero, part], axis=0)


def columns(pair, kind):
    return slice((3 * pair + kind) * PAIR, (3 * pair + kind + 1) * PAIR)


def head_rows(n):
    return slice(n * HEAD_DIM, (n + 1) * HEAD_DIM)


def forward_kernel(bounds, qkv_ref, row_ref, col_ref, mixed_ref, logsum_ref, vt_ref):
    length = qkv_ref.shape[0]
    pairs = logsum_ref.shape[0]
    heads = [(p, head) for p in range(pairs) for head in range(2)]
    q_t = [qkv_ref[:, columns(p, 0)].T for p in range(pairs)]
    for p in range(pairs):
        vt_ref[p * PAIR : (p + 1) * PAIR, :] = qkv_ref[:, columns(p, 2)].T
    for i in range(length // BLOCK):
        at = slice(i * BLOCK, (i + 1) * BLOCK)
        row = row_ref[:, at]
        halves = [half_rows(q_t[p][:, at], head) for p, head in heads]

        def step(j, carry):
            span = pl.ds(pl.multiple_of(j * BLOCK, BLOCK), BLOCK)
            same = col_ref[span, :] == row
            products = [matmul(qkv_ref[span, columns(p, 1)], halves[2 * p + head]) for p, head in heads]
            new = []
            for n, (peak, total, mix) in enumerate(carry):
                scores = jnp.where(same, products[n], -1e30)
                top = jnp.maximum(peak, jnp.max(scores, axis=0, keepdims=True))
                weights = jnp.exp(scores - top)
                decay = jnp.exp(peak - top)
                total = total * decay + jnp.sum(weights, axis=0, keepdims=True)
                mix = mix * decay + matmul(vt_ref[head_rows(n), span], weights.astype(BF16))
                new.append((top, total, mix))
            return tuple(new)

        first = (
            jnp.full((1, BLOCK), -1e30, F32),
            jnp.zeros((1, BLOCK), F32),
            jnp.zeros((HEAD_DIM, BLOCK), F32),
        )
        done = lax.fori_loop(bounds[i, 0], bounds[i, 1], step, (first,) * len(heads))
        for p in range(pairs):
            mixes = [mix / total for _, total, mix in done[2 * p : 2 * p + 2]]
            mixed_ref[at, p * PAIR : (p + 1) * PAIR] = jnp.concatenate(mixes, axis=0).T.astype(BF16)
        for n, (p, head) in enumerate(heads):
            logsum_ref[p, head : head + 1, at] = done[n][0] + jnp.log(done[n][1])


def backward_kernel(
    bounds, qkv_ref, row_ref, col_ref, mixed_ref, logsum_ref, grad_ref, out_ref, sums_ref, kt_ref, dk_ref, dv_ref
):
    length = qkv_ref.shape[0]
    pairs = logsum_ref.shape[0]
    heads = [(p, head) for p in range(pairs) for head in range(2)]
    dk_ref[...] = jnp.zeros_like(dk_ref)
    dv_ref[...] = jnp.zeros_like(dv_ref)
    q_t, g_t, delta = [], [], []
    for p in range(pairs):
        lanes = slice(p * PAIR, (p + 1) * PAIR)
        q_t.append(qkv_ref[:, columns(p, 0)].T)
        g_t.append(grad_ref[:, lanes].T)
        kt_ref[lanes, :] = qkv_ref[:, columns(p, 1)].T
        product_t = (grad_ref[:, lanes].astype(F32) * mixed_ref[:, lanes].astype(F32)).T
        for head in range(2):
            delta.append(jnp.sum(product_t[head_rows(head)], axis=0, keepdims=True))
    lane = lax.broadcasted_iota(jnp.int32, (BLOCK, PAIR), 1)
    zero = jnp.zeros((BLOCK, PAIR), BF16)

    def split(x):
        return jnp.concatenate(
            [jnp.where(lane < HEAD_DIM, x, zero), jnp.where(lane >= HEAD_DIM, x, zero)], axis=0
        )

    for i in range(length // BLOCK):
        at = slice(i * BLOCK, (i + 1) * BLOCK)
        row = row_ref[:, at]
        q_halves = [half_rows(q_t[p][:, at], head) for p, head in heads]
        g_halves = [half_rows(g_t[p][:, at], head) for p, head in heads]
        q_split = [split(qkv_ref[at, columns(p, 0)]) for p in range(pairs)]
        g_split = [split(grad_ref[at, p * PAIR : (p + 1) * PAIR]) for p in range(pairs)]
        logsum = [logsum_ref[p, head : head + 1, at] for p, head in heads]

        def step(j, carry):
            span = pl.ds(pl.multiple_of(j * BLOCK, BLOCK), BLOCK)
            same = col_ref[span, :] == row
            scores = [matmul(qkv_ref[span, columns(p, 1)], q_halves[2 * p + head]) for p, head in heads]
            grad_probs = [matmul(qkv_ref[span, columns(p, 2)], g_halves[2 * p + head]) for p, head in heads]
            new = []
            for p in range(pairs):
                probs_low, grad_low = [], []
                for n in (2 * p, 2 * p + 1):
                    probs = jnp.exp(jnp.where(same, scores[n], -1e30) - logsum[n])
                    grad_low.append((probs * (grad_probs[n] - delta[n][:, at])).astype(BF16))
                    probs_low.append(probs.astype(BF16))
                    new.append(carry[n] + matmul(kt_ref[head_rows(n), span], grad_low[-1]))
                lanes = slice(p * PAIR, (p + 1) * PAIR)
                dv_ref[span, lanes] += matmul(jnp.concatenate(probs_low, axis=1), g_split[p])
                dk_ref[span, lanes] += matmul(jnp.concatenate(grad_low, axis=1), q_split[p])
            return tuple(new)

        empty = jnp.zeros((HEAD_DIM, BLOCK), F32)
        done = lax.fori_loop(bounds[i, 0], bounds[i, 1], step, (empty,) * len(heads))
        for p in range(pairs):
            grad_q = jnp.concatenate(done[2 * p : 2 * p + 2], axis=0).T
            out_ref[at, columns(p, 0)] = (grad_q * 0.125).astype(BF16)
    for p in range(pairs):
        lanes = slice(p * PAIR, (p + 1) * PAIR)
        out_ref[:, columns(p, 1)] = dk_ref[:, lanes].astype(BF16)
        out_ref[:, columns(p, 2)] = dv_ref[:, lanes].astype(BF16)
    sums_ref[...] = jnp.sum(out_ref[...].astype(F32), axis=0, keepdims=True)


def block_bounds(starts):
    blocks = starts.reshape(-1, BLOCK)
    least, most = blocks[:, 0], blocks[:, -1]
    low = jnp.sum(most[None, :] < least[:, None], axis=1)
    high = jnp.sum(least[None, :] <= most[:, None], axis=1)
    return jnp.stack([low, high], axis=1).astype(jnp.int32)


def attention_forward(bounds, qkv, starts, index, pairs):
    length = qkv.shape[0]
    operands = (bounds, qkv, starts[None, :], starts[:, None])
    shapes = [shape_of((length, pairs * PAIR), BF16), shape_of((pairs, 2, length), F32)]
    return call(
        forward_kernel,
        "attend",
        (1,),
        [
            pl.BlockSpec((length, pairs * 3 * PAIR), lambda g, b: (0, index)),
            whole((1, length)),
            whole((length, 1)),
        ],
        [whole(x.shape) for x in shapes],
        shapes,
        pairs * 2 * length * length * HEAD_DIM * 4,
        operands,
        scratch=[pltpu.VMEM((pairs * PAIR, length), BF16)],
        prefetch=1,
        vmem=16,
    )


def attention_backward(bounds, qkv, starts, mixed, logsum, grad, index, pairs):
    length = qkv.shape[0]
    operands = (bounds, qkv, starts[None, :], starts[:, None], mixed, logsum, grad)
    shapes = [shape_of((length, pairs * 3 * PAIR), BF16), shape_of((1, pairs * 3 * PAIR), F32)]
    return call(
        backward_kernel,
        "attend_back",
        (1,),
        [
            pl.BlockSpec((length, pairs * 3 * PAIR), lambda g, b: (0, index)),
            whole((1, length)),
            whole((length, 1)),
            whole(mixed.shape),
            whole(logsum.shape),
            pl.BlockSpec((length, pairs * PAIR), lambda g, b: (0, index)),
        ],
        [whole(x.shape) for x in shapes],
        shapes,
        pairs * 2 * length * length * HEAD_DIM * 10,
        operands,
        scratch=[
            pltpu.VMEM((pairs * PAIR, length), BF16),
            pltpu.VMEM((length, pairs * PAIR), F32),
            pltpu.VMEM((length, pairs * PAIR), F32),
        ],
        prefetch=1,
        vmem=24,
    )


MEGA = 1024 * 1024


def whole(shape):
    return pl.BlockSpec(shape, lambda *_: (0,) * len(shape), pipeline_mode=pl.Buffered(1))


def call(kernel, name, grid, in_specs, out_specs, out_shape, flops, operands, scratch=(), prefetch=0, vmem=32):
    moved = sum(x.size * x.dtype.itemsize for x in operands) + sum(
        x.size * x.dtype.itemsize for x in out_shape
    )
    return pl.pallas_call(
        kernel,
        grid_spec=pltpu.PrefetchScalarGridSpec(
            num_scalar_prefetch=prefetch,
            grid=grid,
            in_specs=in_specs,
            out_specs=out_specs,
            scratch_shapes=list(scratch),
        ),
        out_shape=out_shape,
        compiler_params=pltpu.CompilerParams(vmem_limit_bytes=vmem * MEGA),
        cost_estimate=pl.CostEstimate(flops=flops, bytes_accessed=moved, transcendentals=0),
        name=name,
    )(*operands)


def shape_of(shape, dtype):
    return jax.ShapeDtypeStruct(shape, dtype)


def place_kernel(where, own_ref, beside_ref, distant_ref, corner_ref, ts_ref, low_ref, hidden_ref):
    tok = own_ref.shape[0]
    ts = ts_ref[...]
    for i, ref in enumerate((own_ref, beside_ref, distant_ref, corner_ref)):
        rows = ref[...].astype(F32) + ts
        low_ref[pl.ds(pl.multiple_of(where[i] * tok, tok), tok), :] = rows.astype(BF16)
        if i % 2 == 0:
            hidden_ref[pl.ds(pl.multiple_of(where[4 + i // 2] * tok, tok), tok), :] = rows


def place_rows(where, blocks, ts):
    tok, width = blocks[0].shape
    shapes = [shape_of((4 * tok, width), BF16), shape_of((2 * tok, width), F32)]
    return call(
        place_kernel,
        "place_rows",
        (1,),
        [whole((tok, width))] * 4 + [whole((1, width))],
        [whole(x.shape) for x in shapes],
        shapes,
        1,
        (where, *blocks, ts),
        prefetch=1,
        vmem=12,
    )


def project_kernel(stream_ref, weight_ref, bias_ref, scale_ref, out_ref, full_ref):
    owners = weight_ref.shape[0]
    rows = full_ref.shape[0] // owners
    for m in range(owners):
        full_ref[m * rows : (m + 1) * rows, :] = weight_ref[m, :rows, :]
    out_ref[...] = ((matmul(stream_ref[...], full_ref[...]) + bias_ref[...]) * scale_ref[...]).astype(BF16)


def project_heads(stream, gathered, bias, scale):
    length, width = stream.shape
    owners, tall, cols = gathered.shape
    tile = cols // 3
    shapes = [shape_of((length, cols), BF16), shape_of((width, cols), BF16)]
    row = pl.BlockSpec((1, tile), lambda t: (0, t))
    return call(
        project_kernel,
        "project_heads",
        (3,),
        [whole((length, width)), pl.BlockSpec((owners, tall, tile), lambda t: (0, 0, t)), row, row],
        [pl.BlockSpec((length, tile), lambda t: (0, t)), pl.BlockSpec((width, tile), lambda t: (0, t))],
        shapes,
        2 * length * width * cols,
        (stream, gathered, bias, scale),
        vmem=16,
    )


def output_kernel(where, *refs):
    (mine_refs, their_refs), (weight_ref, bias_ref, hidden_ref, gain_ref, shift_ref) = (
        (refs[:4], refs[4:6]),
        refs[6:11],
    )
    out_ref, low_ref, normed_ref, factor_ref, mixed_ref = refs[11:]
    h = where[0]
    half = weight_ref.shape[0] // 2
    part = half // 2
    rows = mine_refs[0].shape[0]
    for i in range(2):
        at = slice(i * rows, (i + 1) * rows)
        total = hidden_ref[at, :] + bias_ref[...]
        for cut in range(2):
            mine = pl.ds(pl.multiple_of(h * half + cut * part, 128), part)
            other = pl.ds(pl.multiple_of((1 - h) * half + cut * part, 128), part)
            left, right = mine_refs[2 * cut + i][...], their_refs[cut][at, :]
            mixed_ref[at, mine] = left
            mixed_ref[at, other] = right
            total = total + matmul(left, weight_ref[mine, :]) + matmul(right, weight_ref[other, :])
        out, normed, factor = layer_norm(total, gain_ref[...], shift_ref[...])
        out_ref[at, :] = out
        low_ref[at, :] = out.astype(BF16)
        normed_ref[at, :] = normed
        factor_ref[at, :] = factor


def project_output(h, mine, their, weight, bias, hidden, gain, shift):
    rows, width = hidden.shape
    tok = rows // 2
    part = mine[0].shape[1]
    where = jnp.stack([h, h + 2]).astype(jnp.int32)
    in_specs = [
        pl.BlockSpec((tok, part), lambda g, w: (w[0], 0)),
        pl.BlockSpec((tok, part), lambda g, w: (w[1], 0)),
    ] * 2
    in_specs += [whole((rows, part))] * 2
    in_specs += [whole(weight.shape), whole((1, width)), whole((rows, width)), whole((1, width)), whole((1, width))]
    shapes = [
        shape_of((rows, width), F32),
        shape_of((rows, width), BF16),
        shape_of((rows, width), F32),
        shape_of((rows, 1), F32),
        shape_of((rows, width), BF16),
    ]
    operands = (where, mine[0], mine[0], mine[1], mine[1], their[0], their[1], weight, bias, hidden, gain, shift)
    return call(
        output_kernel,
        "project_output",
        (1,),
        in_specs,
        [whole(x.shape) for x in shapes],
        shapes,
        2 * rows * width * width,
        operands,
        prefetch=1,
    )


def inner_kernel(order, first_ref, *refs):
    pieces, (bias_ref, active_ref, slope_ref, full_ref) = refs[:-4], refs[-4:]
    block = first_ref.shape[1] // 8
    done = 0
    for piece in pieces:
        rows = piece.shape[0]
        at = order[done // block] * block + done % block
        full_ref[pl.ds(pl.multiple_of(at, rows), rows), :] = piece[...]
        done += rows
    rows = first_ref.shape[0]
    step = 256
    for i in range(rows // step):
        at = slice(i * step, (i + 1) * step)
        inner = matmul(first_ref[at, :], full_ref[...]) + bias_ref[...]
        cdf, pdf = normal_cdf_pdf(inner)
        active_ref[0, at, :] = (inner * cdf).astype(BF16)
        slope_ref[0, at, :] = (cdf + inner * pdf).astype(BF16)


def feed_inner(order, first_low, pieces, bias):
    rows, width = first_low.shape
    ff = pieces[0].shape[1]
    tile = ff // 8
    shapes = [
        shape_of((8, rows, tile), BF16),
        shape_of((8, rows, tile), BF16),
        shape_of((width, ff), BF16),
    ]
    return call(
        inner_kernel,
        "feed_inner",
        (8,),
        [whole((rows, width))]
        + [pl.BlockSpec((x.shape[0], tile), lambda t, o: (0, t)) for x in pieces]
        + [pl.BlockSpec((1, tile), lambda t, o: (0, t))],
        [
            pl.BlockSpec((1, rows, tile), lambda t, o: (t, 0, 0)),
            pl.BlockSpec((1, rows, tile), lambda t, o: (t, 0, 0)),
            pl.BlockSpec((width, tile), lambda t, o: (0, t)),
        ],
        shapes,
        2 * rows * width * ff,
        (order, first_low, *pieces, bias),
        prefetch=1,
    )


def outer_kernel(order, active_ref, *refs):
    pieces, refs = refs[:-12], refs[-12:]
    bias_ref, first_ref, own_ref, moved_ref, gain_ref, shift_ref = refs[:6]
    full_ref, out_ref, grad_ref, low_ref, sums_ref, acc_ref = refs[6:]
    t = pl.program_id(0)
    block, tile = full_ref.shape[1:]
    done = 0
    for piece in pieces:
        rows = piece.shape[0]
        full_ref[order[done // block], done % block : done % block + rows] = piece[...]
        done += rows
    total = matmul(active_ref[0], full_ref[0])
    for k in range(1, 8):
        total = total + matmul(active_ref[k], full_ref[k])
    acc_ref[:, pl.ds(pl.multiple_of(t * tile, tile), tile)] = total

    @pl.when(t == pl.num_programs(0) - 1)
    def _():
        rows, width = acc_ref.shape
        step = 128
        gain, shift, bias = gain_ref[...], shift_ref[...], bias_ref[...]
        sums = [jnp.zeros((1, width), F32)] * 3
        for i in range(rows // step):
            at = slice(i * step, (i + 1) * step)
            out, normed, factor = layer_norm(first_ref[at, :] + acc_ref[at, :] + bias, gain, shift)
            out_ref[at, :] = out.astype(BF16)
            tok = own_ref.shape[0]
            which, at_block = i * step // tok, slice(i * step % tok, i * step % tok + step)
            up = jnp.where(order[8] == which, own_ref[at_block, :], moved_ref[at_block, :]).astype(F32)
            grad = norm_back(up, normed, factor, gain)
            low = grad.astype(BF16)
            grad_ref[at, :] = grad
            low_ref[at, :] = low
            for j, item in enumerate((up * normed, up, low.astype(F32))):
                sums[j] = sums[j] + jnp.sum(item, axis=0, keepdims=True)
        sums_ref[...] = jnp.concatenate(sums + [jnp.zeros((5, width), F32)], axis=0)


def feed_outer(order, active, pieces, bias, first_out, own, moved, gain, shift):
    rows, width = first_out.shape
    block = sum(x.shape[0] for x in pieces) // 8
    tile = width // 4
    shapes = [
        shape_of((8, block, width), BF16),
        shape_of((rows, width), BF16),
        shape_of((rows, width), F32),
        shape_of((rows, width), BF16),
        shape_of((8, width), F32),
    ]
    row = whole((1, width))
    return call(
        outer_kernel,
        "feed_outer",
        (4,),
        [whole(active.shape)]
        + [pl.BlockSpec((x.shape[0], tile), lambda t, o: (0, t)) for x in pieces]
        + [row, whole((rows, width)), whole(own.shape), whole(moved.shape), row, row],
        [pl.BlockSpec((8, block, tile), lambda t, o: (0, 0, t))] + [whole(x.shape) for x in shapes[1:]],
        shapes,
        2 * rows * width * block * 8,
        (order, active, *pieces, bias, first_out, own, moved, gain, shift),
        scratch=[pltpu.VMEM((rows, width), F32)],
        prefetch=1,
    )


def gelu_back_kernel(grad_ref, weight_ref, slope_ref, out_ref, sums_ref):
    grad = contract_cols(grad_ref[...], weight_ref[0])
    low = (grad * slope_ref[0].astype(F32)).astype(BF16)
    out_ref[0] = low
    sums_ref[0] = jnp.sum(low.astype(F32), axis=0, keepdims=True)


def gelu_back(grad_outer, full_outer, slope):
    rows, width = grad_outer.shape
    _, block, _ = full_outer.shape
    tile = slope.shape[2]
    shapes = [shape_of(slope.shape, BF16), shape_of((8, 1, tile), F32)]
    return call(
        gelu_back_kernel,
        "gelu_back",
        (8,),
        [
            whole((rows, width)),
            pl.BlockSpec((1, block, width), lambda t: (t, 0, 0)),
            pl.BlockSpec((1, rows, tile), lambda t: (t, 0, 0)),
        ],
        [
            pl.BlockSpec((1, rows, tile), lambda t: (t, 0, 0)),
            pl.BlockSpec((1, 1, tile), lambda t: (t, 0, 0)),
        ],
        shapes,
        2 * rows * width * tile * 8,
        (grad_outer, full_outer, slope),
    )


def first_back_kernel(grad_ref, weight_ref, second_ref, normed_ref, factor_ref, gain_ref, output_ref, *refs):
    out_ref, low_ref, mixed_ref, sums_ref, acc_ref = refs
    t = pl.program_id(0)
    part = contract_cols(grad_ref[0], weight_ref[...])

    @pl.when(t == 0)
    def _():
        acc_ref[...] = second_ref[...] + part

    @pl.when(t > 0)
    def _():
        acc_ref[...] += part

    @pl.when(t == pl.num_programs(0) - 1)
    def _():
        rows, width = acc_ref.shape
        step = 128
        gain = gain_ref[...]
        sums = [jnp.zeros((1, width), F32)] * 3
        for i in range(rows // step):
            at = slice(i * step, (i + 1) * step)
            up, normed = acc_ref[at, :], normed_ref[at, :]
            grad = norm_back(up, normed, factor_ref[at, :], gain)
            low = grad.astype(BF16)
            out_ref[at, :] = grad
            low_ref[at, :] = low
            for j, item in enumerate((up * normed, up, low.astype(F32))):
                sums[j] = sums[j] + jnp.sum(item, axis=0, keepdims=True)
        sums_ref[...] = jnp.concatenate(sums + [jnp.zeros((5, width), F32)], axis=0)
        mixed_ref[...] = contract_cols(low_ref[...], output_ref[...]).astype(BF16)


def first_back(grad_inner, full_inner, grad_second, normed, factor, gain, full_output):
    rows, width = grad_second.shape
    tile = grad_inner.shape[2]
    shapes = [
        shape_of((rows, width), F32),
        shape_of((rows, width), BF16),
        shape_of((rows, width), BF16),
        shape_of((8, width), F32),
    ]
    return call(
        first_back_kernel,
        "first_back",
        (8,),
        [
            pl.BlockSpec((1, rows, tile), lambda t: (t, 0, 0)),
            pl.BlockSpec((width, tile), lambda t: (0, t)),
            whole((rows, width)),
            whole((rows, width)),
            whole((rows, 1)),
            whole((1, width)),
            whole(full_output.shape),
        ],
        [whole(x.shape) for x in shapes],
        shapes,
        2 * rows * width * (tile * 8 + width),
        (grad_inner, full_inner, grad_second, normed, factor, gain, full_output),
        scratch=[pltpu.VMEM((rows, width), F32)],
    )


def block_grad_kernel(order, left_ref, right_ref, out_ref):
    out_ref[0] = contract_rows(left_ref[0], right_ref[...]).astype(BF16)


def block_grad(order, left, right):
    rows, width = right.shape
    block = left.shape[2]
    shapes = [shape_of((4, block, width), BF16)]
    return call(
        block_grad_kernel,
        "block_grad",
        (4,),
        [pl.BlockSpec((1, rows, block), lambda i, o: (o[i], 0, 0)), whole((rows, width))],
        [pl.BlockSpec((1, block, width), lambda i, o: (i, 0, 0))],
        shapes,
        2 * rows * width * block * 4,
        (order, left, right),
        prefetch=1,
    )[0]


def turn_strips(order, left_ref, turned_ref):
    block = turned_ref.shape[0] // 4
    for i in range(4):
        strip = left_ref[:, pl.ds(pl.multiple_of(order[i] * block, block), block)]
        turned_ref[i * block : (i + 1) * block, : strip.shape[0]] = strip.T


def tile_grad_kernel(order, left_ref, right_ref, out_ref, turned_ref):
    block = out_ref.shape[1]

    @pl.when(pl.program_id(0) == 0)
    def _():
        turn_strips(order, left_ref, turned_ref)

    out = matmul(turned_ref[...], right_ref[0]).astype(BF16)
    for i in range(4):
        out_ref[i] = out[i * block : (i + 1) * block]


def tile_grad(order, left, right):
    rows, width = left.shape
    block = width // 8
    tiles, _, tile = right.shape
    shapes = [shape_of((4, block, tiles * tile), BF16)]
    return call(
        tile_grad_kernel,
        "tile_grad",
        (tiles,),
        [whole((rows, width)), pl.BlockSpec((1, rows, tile), lambda t, o: (t, 0, 0))],
        [pl.BlockSpec((4, block, tile), lambda t, o: (0, 0, t))],
        shapes,
        2 * rows * block * 4 * tiles * tile,
        (order, left, right),
        scratch=[pltpu.VMEM((4 * block, rows), BF16)],
        prefetch=1,
        vmem=12,
    )[0]


def strip_grad_kernel(
    parts, order, left_ref, first_ref, second_ref, extra_ref, low_ref, third_ref, out_ref, turned_ref
):
    t = pl.program_id(0)
    last = parts[0] + parts[1]
    block = turned_ref.shape[0] // 4

    @pl.when(t == 0)
    def _():
        turn_strips(order, left_ref, turned_ref)

    @pl.when(t == last)
    def _():
        turn_strips(order, low_ref, turned_ref)

    def put(right, extra):
        out = matmul(turned_ref[:, : right.shape[0]], right).astype(BF16)
        for i in range(4):
            out_ref[i, :block] = out[i * block : (i + 1) * block]
            out_ref[i, block:] = extra_ref[order[i]] if extra else jnp.zeros_like(out_ref[i, block:])

    @pl.when(t < parts[0])
    def _():
        put(first_ref[...], True)

    @pl.when((t >= parts[0]) & (t < last))
    def _():
        put(second_ref[...], True)

    @pl.when(t >= last)
    def _():
        put(third_ref[...], False)


def strip_grad(order, left, first, second, extra, low, third):
    rows, width = left.shape
    block = width // 8
    tile = 512 if first.shape[1] % 512 == 0 else 256
    parts = [x.shape[1] // tile for x in (first, second, third)]
    total = sum(parts)
    tall = block + extra.shape[1]
    shapes = [shape_of((4, tall, total * tile), BF16)]
    return call(
        partial(strip_grad_kernel, parts),
        "strip_grad",
        (total,),
        [
            whole((rows, width)),
            pl.BlockSpec((rows, tile), lambda t, o: (0, jnp.minimum(t, parts[0] - 1))),
            pl.BlockSpec((rows, tile), lambda t, o: (0, jnp.clip(t - parts[0], 0, parts[1] - 1))),
            pl.BlockSpec(
                (8, extra.shape[1], tile), lambda t, o: (0, 0, jnp.minimum(t, parts[0] + parts[1] - 1))
            ),
            whole(low.shape),
            pl.BlockSpec((low.shape[0], tile), lambda t, o: (0, jnp.maximum(t - parts[0] - parts[1], 0))),
        ],
        [pl.BlockSpec((4, tall, tile), lambda t, o: (0, 0, t))],
        shapes,
        2 * rows * block * 4 * total * tile,
        (order, left, first, second, extra, low, third),
        scratch=[pltpu.VMEM((4 * block, rows), BF16)],
        prefetch=1,
        vmem=20,
    )[0]


def hidden_back_kernel(where, *refs):
    lefts, weight_ref, rest = refs[:2], refs[2], refs[3:]
    part = lefts[0].shape[1]
    total = contract_cols(lefts[0][...], weight_ref[:, :part]) + contract_cols(lefts[1][...], weight_ref[:, part:])
    if len(rest) == 2:
        total = total + rest[0][...]
    rest[-1][...] = total.astype(rest[-1].dtype)


def hidden_back(parity, grads, weight, base, tok):
    width = weight.shape[0]
    part = grads[0].shape[1]
    where = jnp.stack([parity, parity + 2]).astype(jnp.int32)
    row = pl.BlockSpec((tok, width), lambda i, w: (i, 0))
    extra = () if base is None else (base,)
    shapes = [shape_of((2 * tok, width), BF16 if base is None else F32)]
    return call(
        hidden_back_kernel,
        "hidden_back",
        (2,),
        [pl.BlockSpec((tok, part), lambda i, w: (w[i], 0))] * 2 + [whole(weight.shape)] + [row] * len(extra),
        [row],
        shapes,
        2 * 2 * tok * width * part * 2,
        (where, *grads, weight, *extra),
        prefetch=1,
    )[0]


def after(x, *deps):
    return lax.optimization_barrier((x, deps))[0]


class Steps:
    def __init__(self):
        self.last = ()

    def __call__(self, fn, *args):
        args, _ = lax.optimization_barrier((args, self.last))
        out = fn(*args)
        self.last = out
        return out


def flip(x, axis, size, bit):
    return lax.ppermute(x, axis, [(i, i ^ bit) for i in range(size)])


def swap(x, bit):
    return flip(x, "fsdp", 8, bit)


def widen(*items):
    return sum(item.astype(F32) for item in items)


class CubeSum:
    def __init__(self, send, width, x_columns):
        self.got = swap(send, 1)
        self.parts = []
        if x_columns > 0:
            self.parts.append((slice(0, x_columns), 1, 2, 2, 4))
        if x_columns < width:
            self.parts.append((slice(x_columns, width), 2, 1, 4, 2))

    def first_hop(self, steps, keep):
        def add(keep, got):
            return [
                jnp.stack([widen(keep[i, :, cols], got[i, :, cols]).astype(BF16) for i in (away, 3)])
                for cols, _, away, _, _ in self.parts
            ]

        self.keep = keep
        there = steps(add, keep, self.got)
        self.back = [swap(x, part[3]) for x, part in zip(there, self.parts)]

    def second_hop(self, steps):
        def add(keep, got, back):
            here, there = [], []
            for (cols, near, _, _, _), b in zip(self.parts, back):
                here.append(widen(keep[0, :, cols], got[0, :, cols], b[0]))
                there.append(widen(keep[near, :, cols], got[near, :, cols], b[1]).astype(BF16))
            return here, there

        self.here, there = steps(add, self.keep, self.got, self.back)
        self.last = [swap(x, part[4]) for x, part in zip(there, self.parts)]

    def result(self, steps):
        def add(here, last):
            sums = [widen(x, y).astype(BF16) for x, y in zip(here, last)]
            return sums[0] if len(sums) == 1 else jnp.concatenate(sums, axis=1)

        return steps(add, self.here, self.last)


class PlainSum:
    def __init__(self, product, extra=()):
        self.product, self.extra = product.astype(BF16), extra

    def first_hop(self, steps, keep):
        pass

    def second_hop(self, steps):
        pass

    def result(self, steps):
        share = lax.psum_scatter(self.product, "fsdp", scatter_dimension=0, tiled=True)
        lines = [lax.psum_scatter(x, "fsdp", scatter_dimension=0, tiled=False) for x in self.extra]
        return (share, *lines) if lines else share


def pair_pack(parts):
    rows = parts[0].shape[0]
    return jnp.stack([p.reshape(rows, -1, PAIR) for p in parts], axis=2).reshape(rows, -1)


def pair_unpack(packed):
    rows = packed.shape[0]
    cut = packed.reshape(rows, -1, 3, PAIR)
    return [cut[:, :, i].reshape(rows, -1) for i in range(3)]


def body(
    fsdp,
    stream_in,
    timestep,
    doc_start,
    query_weight,
    key_weight,
    value_weight,
    output_weight,
    query_bias,
    value_bias,
    output_bias,
    first_gain,
    first_shift,
    inner_weight,
    inner_bias,
    outer_weight,
    outer_bias,
    second_gain,
    second_shift,
    cotangent,
):
    cube = fsdp == 8
    steps = Steps()
    me = lax.axis_index("fsdp")
    streams, tok, width = stream_in.shape
    own_rows = query_weight.shape[0]
    half = width // 2
    ff = inner_weight.shape[1]
    length = 4 * tok
    z = lax.axis_index("seq")
    h, s = z % 2, z // 2

    def flip_h(x):
        return flip(x, "seq", 4, 1)

    def flip_s(x):
        return flip(x, "seq", 4, 2)

    def in_order(mine, other):
        return jnp.where(s == 0, jnp.concatenate([mine, other]), jnp.concatenate([other, mine]))

    def pick(x, index, axis=0):
        return lax.dynamic_index_in_dim(x, index, axis, keepdims=False)

    head_cols = [lax.dynamic_slice_in_dim(w, h * half, half, 1) for w in (query_weight, key_weight, value_weight)]
    small = jnp.concatenate(
        [
            query_bias,
            value_bias,
            output_bias,
            first_gain,
            first_shift,
            outer_bias,
            second_gain,
            second_shift,
            inner_bias,
        ]
    )
    packed = pair_pack(head_cols)
    own = pick(stream_in, s)
    if cube:
        owners = [me ^ m for m in range(8)]
        packed = jnp.concatenate([packed, jnp.broadcast_to(small[None, :], (16, small.shape[0]))])
        gathered = lax.all_gather(packed, "fsdp", axis=0, tiled=False)
        small_rows = gathered[:, own_rows]
        output_w = after(output_weight, gathered)
        full_output = lax.all_gather(output_w, "fsdp", axis=0, tiled=True)
        inner_w = after(inner_weight, packed)
        ix, iy = swap(inner_w, 2), swap(inner_w, 4)
        distant = flip_s(pick(stream_in, 1 - s))
        beside = flip_h(own)
        distant, beside = steps(lambda *x: x, distant, beside)
        corner = flip_h(distant)
        cut = own_rows // 2
        top, bottom, ix, iy, inner_w, outer_w = steps(
            lambda x, y, *rest: (x[:cut], y[cut:], x, y, *rest), ix, iy, inner_w, outer_weight
        )
        jy, jx = swap(top, 4), swap(bottom, 2)
        ic = swap(inner_w, 1)
    else:
        owners = list(range(8))

        def gather(piece):
            full = lax.all_gather(piece, "fsdp", axis=0, tiled=True)
            return list(full.reshape(8, full.shape[0] // 8, full.shape[1]))

        distant, beside = flip_s(pick(stream_in, 1 - s)), flip_h(own)
        corner = flip_h(distant)
        gathered = lax.all_gather(packed, "fsdp", axis=0, tiled=False)
        full_output = lax.all_gather(output_weight, "fsdp", axis=0, tiled=True)
        inner_pieces, outer_pieces = gather(inner_weight), gather(outer_weight)
        small_rows = lax.all_gather(small, "fsdp", axis=0, tiled=False)
    order = jnp.stack([jnp.asarray(o, jnp.int32) for o in owners])
    small_rows = small_rows.astype(F32)
    qbias, vbias, obias, gain_one, shift_one, obias_two, gain_two, shift_two = [
        small_rows[:, i * own_rows : (i + 1) * own_rows].reshape(1, -1) for i in range(8)
    ]
    ibias = small_rows[:, 8 * own_rows :].reshape(1, -1)

    ts = pick(timestep, s).astype(F32)

    cotangent_own, cotangent_out = pick(cotangent, s), pick(cotangent, 1 - s)
    if cube:
        corner, ic, outer_w, cotangent_out = steps(lambda *x: x, corner, ic, outer_w, cotangent_out)
        ox, oy = swap(outer_w, 2), swap(outer_w, 4)
    moved = flip_s(cotangent_out)
    where = jnp.stack([z, z ^ 1, z ^ 2, z ^ 3, s, 1 - s]).astype(jnp.int32)
    stream_low, hidden = steps(
        lambda *x: place_rows(where, x[:4], x[4]), own, beside, distant, corner, ts.reshape(1, width)
    )
    starts = pick(doc_start, s)
    bounds = block_bounds(starts)

    qb = lax.dynamic_slice_in_dim(qbias, h * half, half, 1)
    vb = lax.dynamic_slice_in_dim(vbias, h * half, half, 1)
    bias_row = pair_pack([qb, jnp.zeros_like(qb), vb])
    scale_row = pair_pack([jnp.full((1, half), 0.125, F32), jnp.ones((1, half), F32), jnp.ones((1, half), F32)])
    qkv, full_qkv = steps(project_heads, stream_low, gathered, bias_row, scale_row)
    pairs = half // PAIR
    part = pairs // 2

    def rows_of(x, parity):
        cut = x.reshape(2, 2, tok, x.shape[1])
        return pick(cut, parity, 1).reshape(2 * tok, x.shape[1])

    def attend(index, qkv):
        return attention_forward(bounds, qkv, starts, index, part)

    if cube:
        jy, jx, ix, iy, qkv = steps(lambda *x: x, jy, jx, ix, iy, qkv)
        ixc, iyc = swap(ix, 1), swap(iy, 1)
    else:
        ixc = iyc = jy = jx = 0.0
    mixed_a, logsum_a = steps(partial(attend, 0), qkv)
    out_a, ixc, iyc = steps(lambda x, *rest: (rows_of(x, 1 - h), *rest), mixed_a, ixc, iyc)
    their_a = flip_h(out_a)
    mixed_b, logsum_b = steps(partial(attend, 1), qkv)
    out_b, their_a, moved, jy, jx = steps(
        lambda x, *rest: (rows_of(x, 1 - h), *rest), mixed_b, their_a, moved, jy, jx
    )
    their_b = flip_h(out_b)
    if cube:
        jyc, jxc = swap(jy, 1), swap(jx, 1)
        inner_pieces = [inner_w, ic, ix, ixc, iy, iyc, jy, jx, jyc, jxc]
        cut = outer_weight.shape[0] // 2
        top, bottom, ox, oy = steps(lambda x, y: (x[:cut], y[cut:], x, y), ox, oy)
        jy, jx = swap(top, 4), swap(bottom, 2)
    first_out, first_low, first_normed, first_factor, mixed = steps(
        partial(project_output, h),
        (mixed_a, mixed_b),
        (their_a, their_b),
        full_output,
        obias,
        hidden,
        gain_one,
        shift_one,
    )

    if cube:
        jy, jx, ox, oy, outer_w, first_low = steps(lambda *x: x, jy, jx, ox, oy, outer_w, first_low)
        oxc, oc, oyc, jyc, jxc = swap(ox, 1), swap(outer_w, 1), swap(oy, 1), swap(jy, 1), swap(jx, 1)
        outer_pieces = [outer_w, oc, ox, oxc, oy, oyc, jy, jx, jyc, jxc]
    active, slope, full_inner = steps(partial(feed_inner, order), first_low, inner_pieces, ibias)
    facts = jnp.concatenate([order, s.astype(jnp.int32).reshape(1)])
    full_outer, result, grad_second_in, grad_outer, second_sums = steps(
        partial(feed_outer, facts),
        active,
        outer_pieces,
        obias_two,
        first_out,
        cotangent_own,
        moved,
        gain_two,
        shift_two,
    )
    result = result.reshape(2, tok, width)
    result_own, result_out = steps(lambda x: (pick(x, s), pick(x, 1 - s)), result)
    result_away = flip_s(result_out)

    if cube:
        send_order = jnp.stack([me ^ m for m in (1, 5, 3, 7)]).astype(jnp.int32)
        keep_order = jnp.stack([me ^ m for m in (0, 4, 2, 6)]).astype(jnp.int32)

    if cube:
        outer_send = steps(partial(block_grad, send_order), active, grad_outer)
        outer_sum = CubeSum(outer_send, width, half)
        outer_keep = steps(partial(block_grad, keep_order), active, grad_outer)
    else:
        outer_keep = ()
        outer_sum = PlainSum(contract_rows(active.transpose(1, 0, 2).reshape(2 * tok, -1), grad_outer))
    grad_inner, inner_sums = steps(gelu_back, grad_outer, full_outer, slope)
    outer_sum.first_hop(steps, outer_keep)
    if cube:
        inner_send = steps(partial(tile_grad, send_order), first_low, grad_inner)
        inner_sum = CubeSum(inner_send, ff, ff // 2)
    else:
        inner_sum = PlainSum(contract_rows(first_low, grad_inner.transpose(1, 0, 2).reshape(2 * tok, -1)))

    def first_step(*args):
        grad_first_in, grad_attended, grad_mixed, sums = first_back(*args)
        wide = half // 2
        theirs = lax.dynamic_slice_in_dim(grad_mixed, (1 - h) * half, half, 1)
        mine = lax.dynamic_slice_in_dim(grad_mixed, h * half, half, 1)
        return grad_first_in, grad_attended, sums, theirs, mine

    grad_first_in, grad_attended, first_sums, theirs, mine = steps(
        first_step, grad_inner, full_inner, grad_second_in, first_normed, first_factor, gain_one, full_output
    )
    received = flip_h(theirs)
    inner_keep = steps(partial(tile_grad, keep_order), first_low, grad_inner) if cube else ()
    result_away = steps(lambda x: x, result_away)
    outer_sum.second_hop(steps)

    def to_heads(mine, received):
        mine = mine.reshape(2, 1, tok, half)
        received = received.reshape(2, 1, tok, half)
        return jnp.where(
            h == 0, jnp.concatenate([mine, received], axis=1), jnp.concatenate([received, mine], axis=1)
        ).reshape(length, half)

    grad_heads = steps(to_heads, mine, received)

    def seq_sum(share):
        def halve(x, bit):
            pair = x.reshape(2, x.shape[0] // 2, -1)
            return pick(pair, bit), pick(pair, 1 - bit)

        def join(mine, other, bit):
            return jnp.where(bit == 0, jnp.concatenate([mine, other]), jnp.concatenate([other, mine]))

        mine, out = steps(lambda x: halve(x, h), share)
        back = flip_h(out)
        yield
        def quarter(m, b):
            mine, out = halve(widen(m, b), s)
            return mine, out.astype(BF16)

        mine, out = steps(quarter, mine, back)
        back = flip_s(out)
        yield
        mine = steps(lambda m, b: widen(m, b).astype(BF16), mine, back)
        back = flip_s(mine)
        yield
        mine = steps(lambda m, b: join(m, b, s), mine, back)
        back = flip_h(mine)
        yield
        yield steps(lambda m, b: join(m, b, h).astype(F32), mine, back)

    def attend_back(index, qkv, mixed, logsum, grad):
        return attention_backward(bounds, qkv, starts, mixed, logsum, grad, index, part)

    grad_a, sums_a = steps(partial(attend_back, 0), qkv, mixed_a, logsum_a, grad_heads)
    inner_sum.first_hop(steps, inner_keep)
    outer_share = outer_sum.result(steps)
    outer_steps = seq_sum(outer_share)
    next(outer_steps)
    grad_b, sums_b = steps(partial(attend_back, 1), qkv, mixed_b, logsum_b, grad_heads)
    next(outer_steps)
    away = flip_h(
        steps(lambda a, b, w: hidden_back(1 - h, (a, b), w, None, tok), grad_a, grad_b, full_qkv)
    )
    zero_half = jnp.zeros((half,), F32)

    def spread(v):
        v = v.reshape(-1)
        return jnp.where(h == 0, jnp.concatenate([v, zero_half]), jnp.concatenate([zero_half, v]))

    grad_q_cols, _, grad_v_cols = pair_unpack(jnp.concatenate([sums_a, sums_b], axis=1))
    vectors = jnp.concatenate(
        [
            v.reshape(fsdp, -1)
            for v in (
                spread(grad_q_cols),
                spread(grad_v_cols),
                first_sums[2],
                first_sums[0],
                first_sums[1],
                second_sums[2],
                second_sums[0],
                second_sums[1],
                inner_sums,
            )
        ],
        axis=1,
    ).astype(BF16)
    if cube:
        lines = vectors.reshape(fsdp, 1, -1)
        lines = jnp.concatenate([lines, jnp.zeros((fsdp, 15, lines.shape[2]), BF16)], axis=1)
        qkv_operands = (stream_low, grad_a, grad_b, lines, mixed, grad_attended)
        qkv_send = steps(partial(strip_grad, send_order), *qkv_operands)
        qkv_sum = CubeSum(qkv_send, qkv_send.shape[2], qkv_send.shape[2] // 2)
        inner_sum.second_hop(steps)
        next(outer_steps)
        qkv_keep = steps(partial(strip_grad, keep_order), *qkv_operands)
    else:
        qkv_keep = ()
        both = jnp.concatenate([grad_a, grad_b], axis=1)
        both = jnp.concatenate([contract_rows(stream_low, both), contract_rows(mixed, grad_attended)], axis=1)
        qkv_sum = PlainSum(both, (vectors,))
        next(outer_steps)
    kept = steps(lambda a, b, w, g: hidden_back(h, (a, b), w, g, tok), grad_a, grad_b, full_qkv, grad_first_in)

    def split_rows(kept, away):
        grad_hidden = (kept + away.astype(F32)).reshape(2, tok, width)
        return pick(grad_hidden, s), pick(grad_hidden, 1 - s).astype(BF16)

    inner_share = inner_sum.result(steps)
    inner_steps = seq_sum(inner_share)
    next(inner_steps)
    qkv_sum.first_hop(steps, qkv_keep)
    grad_own, grad_out = steps(split_rows, kept, away)
    grad_away = flip_s(grad_out)
    next(inner_steps)
    next(outer_steps)
    qkv_sum.second_hop(steps)
    next(inner_steps)

    layer_out = jnp.where(s == 0, jnp.stack([result_own, result_away]), jnp.stack([result_away, result_own]))

    def swap_heads(mine, other):
        return jnp.where(h == 0, jnp.concatenate([mine, other], axis=1), jnp.concatenate([other, mine], axis=1))

    qkv_share = qkv_sum.result(steps)
    qkv_share, extra = qkv_share if not cube else (qkv_share, None)
    qkv_back = flip_s(qkv_share)
    outer_grad = next(outer_steps)
    next(inner_steps)
    grad_own, grad_away = steps(lambda x, y: (x, y.astype(F32)), grad_own, grad_away)
    input_grad = jnp.where(s == 0, jnp.stack([grad_own, grad_away]), jnp.stack([grad_away, grad_own]))
    qkv_mine = steps(lambda x, y: widen(x, y).astype(BF16), qkv_share, qkv_back)
    qkv_other = flip_h(qkv_mine)
    inner_grad = next(inner_steps)
    three = 3 * half
    output_grad = widen(qkv_mine[:own_rows, three:], qkv_other[:own_rows, three:])
    if cube:
        sums = widen(qkv_mine[own_rows, :three], qkv_other[own_rows, :three])
    else:
        sums = lax.psum(extra.astype(F32), "seq")
    qkv_grads = [
        swap_heads(mine, other).astype(F32)
        for mine, other in zip(
            pair_unpack(qkv_mine[:own_rows, :three]), pair_unpack(qkv_other[:own_rows, :three])
        )
    ]
    cut = [sums[i * own_rows : (i + 1) * own_rows] for i in range(8)]
    return (
        layer_out,
        input_grad,
        qkv_grads[0],
        qkv_grads[1],
        qkv_grads[2],
        output_grad,
        cut[0],
        cut[1],
        cut[2],
        cut[3],
        cut[4],
        inner_grad,
        sums[8 * own_rows :],
        outer_grad,
        cut[5],
        cut[6],
        cut[7],
    )


def solution(mesh):
    rows = P("fsdp", "seq", None)
    mat = P("fsdp", None)
    vec = P("fsdp")
    in_specs = (rows, mat, mat) + (mat,) * 4 + (vec,) * 5 + (mat, vec, mat, vec, vec, vec) + (rows,)
    out_specs = (rows, rows) + (mat,) * 4 + (vec,) * 5 + (mat, vec, mat, vec, vec, vec)
    return jax.shard_map(
        partial(body, mesh.shape["fsdp"]), mesh=mesh, in_specs=in_specs, out_specs=out_specs, check_vma=False
    )
```
